512 devices in a mesh: region: 8 (over y), cell: 64 (over z, x, core).
Axes of the slice: x: 4, y: 8, z: 8, core: 2. Of those that a mesh axis runs over, the one named last changes fastest.
Arguments:
- position: float32 [3, 4096, 128], P(None, ('region', 'cell')), may hold values from 0 to 1
- velocity: float32 [3, 4096, 128], P(None, ('region', 'cell')), may hold values from -6 to 6
- smoothing: float32 [4096, 128], P(('region', 'cell')), may hold values from 0.3 to 0.5
- particle_mass: float32 [4096, 128], P(('region', 'cell')), may hold values from 0.004 to 0.012
- energy: float32 [4096, 128], P(('region', 'cell')), may hold values from 0.5 to 2
- density_old: float32 [4096, 128], P(('region', 'cell')), may hold values from 0.3 to 1.2
- cell_count: int32 [4096], P(('region', 'cell')), may hold values from 8 to 128, as said below
- active: int32 [4096, 128], P(('region', 'cell')), may hold values from 0 to 1, as said below
- time_bin: int32 [4096, 128], P(('region', 'cell')), may hold values from 0 to 5
- pair_source: int32 [4096, 27], P(('region', 'cell')), may hold values from 0 to 137, as said below
- pair_shift: int32 [4096, 27], P(('region', 'cell')), may hold values from 0 to 26, as said below
- export: int32 [32768, 2], P(('region', 'cell')), may hold values from 0 to 7
Outputs:
- density: float32 [4096, 128], P(('region', 'cell'))
- acceleration: float32 [3, 4096, 128], P(None, ('region', 'cell'))
- kicked_velocity: float32 [3, 4096, 128], P(None, ('region', 'cell'))
The draws below stay inside these ranges and needn't reach their ends.
Inputs may be any that keep to these rules, and one draw needn't show every extreme that they name: `cell_count`: every device has a cell of exactly 128 particles. `active`: 0 in the slots past a cell's count. `pair_source`: pair 0 of a device's cell k names source k; a device's pairs name every one of its 138 sources. `pair_shift`: pair 0 has code 13; a cell's 27 codes are distinct.
All inputs are finite; a program needn't handle non-finite values.
Results may differ from the reference program's by a relative error of at most 0.0003.
Values sent between devices are 32-bit elements; how exact they have to be, the bound alone decides.
A program may use at most 64 MiB of HBM per device.

```python
import math
import jax
import jax.numpy as jnp
from jax import lax

C_DEV = 8
CAP = 128
NB = 27
PROXY = 2
DEVS = 512
CELLS = 4096
TABLE = 138
EXPORTS = 32768
N_REGION = 8
N_CELL = 64


def count_table(key):
    device_total = CELLS // C_DEV
    key_low, key_raw, key_full = jax.random.split(key, 3)
    low_count = jax.random.randint(key_low, (device_total, 1), CAP // 16, CAP // 2 + 1)
    raw_draws = jax.random.randint(key_raw, (device_total, C_DEV), 0, 1 << 20)
    counts = low_count + raw_draws % (CAP + 1 - low_count)
    full_slot = jax.random.randint(key_full, (device_total, 1), 0, C_DEV)
    counts = jnp.where(jnp.arange(C_DEV)[None, :] == full_slot, CAP, counts)
    return counts.reshape(CELLS).astype(jnp.int32)


def draw_cell_count(key, part):
    return count_table(key)


def draw_active(key, part):
    counts = count_table(key)
    key = jax.random.fold_in(key, 2)
    device_total = CELLS // C_DEV
    key_share, key_roll = jax.random.split(key, 2)
    percent = jax.random.randint(key_share, (device_total, 1, 1), 3, 31)
    rolled = jax.random.randint(key_roll, (device_total, C_DEV, CAP), 0, 100)
    chosen = (rolled < percent).reshape(CELLS, CAP)
    live_slot = jnp.arange(CAP)[None, :] < counts[:, None]
    return (chosen & live_slot).astype(jnp.int32)


def draw_pair_source(key, part):
    key = jax.random.fold_in(key, 3)
    device_total = CELLS // C_DEV
    others = C_DEV * (NB - 1)
    key_perm, key_fill, key_mix = jax.random.split(key, 3)

    def covering(one_key):
        return jax.random.permutation(one_key, TABLE)
    covered = jax.vmap(covering)(jax.random.split(key_perm, device_total))
    filler = jax.random.randint(key_fill, (device_total, others - TABLE), 0, TABLE)
    listed = jnp.concatenate([covered, filler], axis=1)

    def mixing(one_key, one_row):
        return one_row[jax.random.permutation(one_key, others)]
    placed = jax.vmap(mixing)(jax.random.split(key_mix, device_total), listed)
    own_cells = jnp.broadcast_to(jnp.arange(C_DEV)[None, :, None], (device_total, C_DEV, 1))
    joined = jnp.concatenate([own_cells, placed.reshape(device_total, C_DEV, NB - 1)], axis=2)
    return joined.reshape(CELLS, NB).astype(jnp.int32)


def draw_pair_shift(key, part):
    key = jax.random.fold_in(key, 4)

    def ordering(one_key):
        return jax.random.permutation(one_key, 26)
    shift_codes = jax.vmap(ordering)(jax.random.split(key, CELLS))
    shift_codes = shift_codes + (shift_codes >= 13).astype(shift_codes.dtype)
    centre = jnp.full((CELLS, 1), 13, shift_codes.dtype)
    return jnp.concatenate([centre, shift_codes], axis=1).astype(jnp.int32)


def place_ends(values, own_key, smallest, largest):
    longest = values.shape.index(max(values.shape))
    spots = []
    for shift in (0, 1):
        where = [jax.random.randint(jax.random.fold_in(own_key, axis), (), 0, length) for axis, length in enumerate(values.shape)]
        where[longest] = (where[longest] + shift) % values.shape[longest]
        spots.append(tuple(where))
    return values.at[spots[0]].set(smallest).at[spots[1]].set(largest)


def block_scale(rng, shape, cuts, low, largest):
    level, own = 1.0, jax.random.fold_in(rng, 6)
    for axis_at, shards_of in cuts:
        draws = jnp.exp(jax.random.uniform(jax.random.fold_in(own, axis_at), (shards_of,), jnp.float32, low / len(cuts), largest / len(cuts)))
        level = level * jnp.repeat(draws, shape[axis_at] // shards_of).reshape([-1 if axis == axis_at else 1 for axis in range(len(shape))])
    return level


def normal_values(rng, shape, spread, reach, pieces=(), kind=jnp.bfloat16):
    result = spread * jax.random.normal(rng, shape, jnp.float32)
    if pieces:
        result = result * block_scale(rng, shape, pieces, -0.22, 0.18)
    return jnp.clip(result, -reach, reach).astype(kind)


def setup_inputs(seed: int = 0) -> dict:
    streams_of = jax.random.split(jax.random.key(seed), 13)
    position = jnp.clip(1.0 * jax.random.uniform(streams_of[0], (3, CELLS, CAP), jnp.float32) ** block_scale(streams_of[0], (3, CELLS, CAP), ((1, 512),), -0.2, 0.2), 0.0, 1.0)
    velocity = normal_values(streams_of[1], (3, CELLS, CAP), 1.0, 6.0, ((1, 512),), jnp.float32)
    smoothing = jnp.clip(0.3 + 0.19999999 * jax.random.uniform(streams_of[2], (CELLS, CAP), jnp.float32) ** block_scale(streams_of[2], (CELLS, CAP), ((0, 512),), -0.2, 0.2), 0.3, 0.5)
    particle_mass = jnp.clip(jnp.exp(math.log(0.012) - 1.09861225 * jax.random.uniform(streams_of[3], (CELLS, CAP), jnp.float32) ** block_scale(streams_of[3], (CELLS, CAP), ((0, 512),), -0.2, 0.2)), 0.004, 0.012)
    energy = jnp.clip(jnp.exp(math.log(2.0) - 1.3862944 * jax.random.uniform(streams_of[4], (CELLS, CAP), jnp.float32) ** block_scale(streams_of[4], (CELLS, CAP), ((0, 512),), -0.2, 0.2)), 0.5, 2.0)
    density_old = jnp.clip(jnp.exp(math.log(1.2) - 1.3862944 * jax.random.uniform(streams_of[5], (CELLS, CAP), jnp.float32) ** block_scale(streams_of[5], (CELLS, CAP), ((0, 512),), -0.2, 0.2)), 0.3, 1.2)
    cell_count = draw_cell_count(jax.random.fold_in(streams_of[12], 71), 0)
    active = draw_active(jax.random.fold_in(streams_of[12], 71), 0)
    time_bin = place_ends(jax.random.randint(streams_of[8], (CELLS, CAP), 0, 6), jax.random.fold_in(streams_of[8], 1), 0, 5).astype(jnp.int32)
    pair_source = draw_pair_source(jax.random.fold_in(streams_of[12], 71), 0)
    pair_shift = draw_pair_shift(jax.random.fold_in(streams_of[12], 71), 0)
    export = place_ends(jax.random.randint(streams_of[11], (EXPORTS, PROXY), 0, C_DEV), jax.random.fold_in(streams_of[11], 1), 0, C_DEV - 1).astype(jnp.int32)
    return {"position": position, "velocity": velocity, "smoothing": smoothing, "particle_mass": particle_mass, "energy": energy, "density_old": density_old, "cell_count": cell_count, "active": active, "time_bin": time_bin, "pair_source": pair_source, "pair_shift": pair_shift, "export": export}


ADIABATIC = 5.0 / 3.0
VISC_ALPHA = 1.0
VISC_BETA = 2.0
STEP_MAX = 0.2

def kernel_value(radius, smooth):
    scaled = radius / smooth
    factor = 1.0 / (math.pi * smooth * smooth * smooth)
    inner_part = 1.0 - 1.5 * scaled * scaled + 0.75 * scaled * scaled * scaled
    outer_part = 0.25 * jnp.maximum(2.0 - scaled, 0.0) ** 3
    return factor * jnp.where(scaled < 1.0, inner_part, outer_part)

def kernel_slope(radius, smooth):
    scaled = radius / smooth
    factor = 1.0 / (math.pi * smooth * smooth * smooth * smooth * smooth)
    inner_part = -3.0 + 2.25 * scaled
    bounded = jnp.maximum(scaled, 1.0)
    outer_part = -0.75 * jnp.maximum(2.0 - bounded, 0.0) ** 2 / bounded
    return factor * jnp.where(scaled < 1.0, inner_part, outer_part)

def shift_offsets(shift_codes):
    first = shift_codes // 9 - 1
    second = shift_codes // 3 % 3 - 1
    third = shift_codes % 3 - 1
    return jnp.stack([first, second, third], axis=-1).astype(jnp.float32)

def density_terms(target_pos, target_smooth, source_pos, source_mass):
    square = sum(((target_pos[component] - source_pos[component]) ** 2 for component in range(3)))
    radius = jnp.sqrt(square)
    return source_mass * kernel_value(radius, target_smooth)

def force_terms(target_pos, target_vel, target_smooth, target_press, target_sound, target_dens, source_pos, source_vel, source_smooth, source_mass, source_press, source_sound, source_dens):
    separation = [target_pos[component] - source_pos[component] for component in range(3)]
    square = sum((piece * piece for piece in separation))
    radius = jnp.sqrt(square)
    mean_slope = 0.5 * (kernel_slope(radius, target_smooth) + kernel_slope(radius, source_smooth))
    approach = sum(((target_vel[component] - source_vel[component]) * separation[component] for component in range(3)))
    mean_smooth = 0.5 * (target_smooth + source_smooth)
    mu_term = mean_smooth * jnp.minimum(approach, 0.0) / (square + 0.01 * mean_smooth * mean_smooth)
    viscous = (-VISC_ALPHA * 0.5 * (target_sound + source_sound) * mu_term + VISC_BETA * mu_term * mu_term) / (0.5 * (target_dens + source_dens))
    weight = source_mass * (target_press + source_press + viscous) * mean_slope
    return [-weight * piece for piece in separation]

def source_tables(export):
    device_ids = jnp.arange(DEVS)
    region_ids = device_ids // N_CELL
    column_ids = device_ids % N_CELL
    own_cells = device_ids[:, None] * C_DEV + jnp.arange(C_DEV)[None, :]
    peer_ids = region_ids[:, None] * N_CELL + jnp.arange(N_CELL)[None, :]
    chosen = export[peer_ids * N_CELL + column_ids[:, None]]
    proxies = (peer_ids[:, :, None] * C_DEV + chosen).reshape(DEVS, N_CELL * PROXY)
    before = ((region_ids - 1) % N_REGION * N_CELL + column_ids) * C_DEV + C_DEV - 1
    after = ((region_ids + 1) % N_REGION * N_CELL + column_ids) * C_DEV
    return jnp.concatenate([own_cells, proxies, before[:, None], after[:, None]], axis=1).astype(jnp.int32)

def reference(position, velocity, smoothing, particle_mass, energy, density_old, cell_count, active, time_bin, pair_source, pair_shift, export):
    slot_index = jnp.arange(CAP)
    live_slot = slot_index[None, :] < cell_count[:, None]
    mass_live = jnp.where(live_slot, particle_mass, 0.0)
    is_active = active > 0
    tables = source_tables(export)
    owner_device = (jnp.arange(CELLS) // C_DEV).astype(jnp.int32)
    global_source = jnp.take_along_axis(tables[owner_device], pair_source, axis=1)
    offsets = shift_offsets(pair_shift)
    cell_ids = jnp.arange(CELLS).astype(jnp.int32)

    def cell_density(cell_item):
        target, sources, shifts = cell_item
        target_pos = [position[component, target][:, None, None] for component in range(3)]
        source_pos = [position[component][sources][None, :, :] + shifts[:, component][None, :, None] for component in range(3)]
        pair_terms = density_terms(target_pos, smoothing[target][:, None, None], source_pos, mass_live[sources][None])
        return lax.optimization_barrier(jnp.sum(pair_terms, axis=(1, 2)))
    summed = lax.map(cell_density, (cell_ids, global_source, offsets))
    density = jnp.where(is_active, summed, density_old)
    press_term = (ADIABATIC - 1.0) * energy / density
    sound_speed = jnp.sqrt(ADIABATIC * (ADIABATIC - 1.0) * energy)

    def cell_force(cell_item):
        target, sources, shifts = cell_item
        target_pos = [position[component, target][:, None, None] for component in range(3)]
        target_vel = [velocity[component, target][:, None, None] for component in range(3)]
        source_pos = [position[component][sources][None, :, :] + shifts[:, component][None, :, None] for component in range(3)]
        source_vel = [velocity[component][sources][None] for component in range(3)]
        pair_terms = force_terms(target_pos, target_vel, smoothing[target][:, None, None], press_term[target][:, None, None], sound_speed[target][:, None, None], density[target][:, None, None], source_pos, source_vel, smoothing[sources][None], mass_live[sources][None], press_term[sources][None], sound_speed[sources][None], density[sources][None])
        return jnp.stack([lax.optimization_barrier(jnp.sum(piece, axis=(1, 2))) for piece in pair_terms], axis=0)
    accel_cells = lax.map(cell_force, (cell_ids, global_source, offsets))
    accel_cells = jnp.transpose(accel_cells, (1, 0, 2))
    acceleration = jnp.where(is_active[None], accel_cells, 0.0)
    step_size = STEP_MAX * jnp.exp2(-time_bin.astype(jnp.float32))
    kicked_velocity = velocity + acceleration * step_size[None]
    return (density, acceleration, kicked_velocity)
```

```python
import functools
import math

import jax
import jax.numpy as jnp
from jax import lax
from jax.experimental import pallas as pl
from jax.experimental.pallas import tpu as pltpu
from jax.sharding import PartitionSpec as P

MESH = pl.DeviceIdType.MESH
C_DEV = 8
CAP = 128
NB = 27
GROUP = 8
ADIABATIC = 5.0 / 3.0
STEP_MAX = 0.2
TINY = 1e-30
F32 = jnp.float32


def greet(regions, peers):
    r, c = lax.axis_index("region"), lax.axis_index("cell")
    barrier = pltpu.get_barrier_semaphore()

    def signal(i, carry):
        pl.semaphore_signal(
            barrier, inc=1, device_id=(r, lax.rem(c + i, peers)), device_id_type=MESH
        )
        return carry

    lax.fori_loop(1, peers, signal, 0)
    for step in (1, regions - 1):
        pl.semaphore_signal(
            barrier, inc=1, device_id=(lax.rem(r + step, regions), c), device_id_type=MESH
        )
    pl.semaphore_wait(barrier, peers + 1)


def fill_outbox(peers, export, cells, outbox):
    def fill(d, carry):
        for q in range(2):
            outbox[d, q] = cells[export[d, q]]
        return carry

    lax.fori_loop(0, peers, fill, 0, unroll=4)


def region_copies(regions, cells, table, sems):
    r, c = lax.axis_index("region"), lax.axis_index("cell")
    size = table.shape[0]
    up = pltpu.make_async_remote_copy(
        src_ref=cells.at[pl.ds(C_DEV - 1, 1)],
        dst_ref=table.at[pl.ds(size - 2, 1)],
        send_sem=sems.at[2],
        recv_sem=sems.at[3],
        device_id=(lax.rem(r + 1, regions), c),
        device_id_type=MESH,
    )
    down = pltpu.make_async_remote_copy(
        src_ref=cells.at[pl.ds(0, 1)],
        dst_ref=table.at[pl.ds(size - 1, 1)],
        send_sem=sems.at[4],
        recv_sem=sems.at[5],
        device_id=(lax.rem(r + regions - 1, regions), c),
        device_id_type=MESH,
    )
    return up, down


def start_exchange(regions, peers, cells, outbox, table, sems):
    r, c = lax.axis_index("region"), lax.axis_index("cell")
    for copy in region_copies(regions, cells, table, sems):
        copy.start()

    def send(i, carry):
        d = lax.rem(c + i, peers)
        pltpu.make_async_remote_copy(
            src_ref=outbox.at[d],
            dst_ref=table.at[pl.ds(C_DEV + 2 * c, 2)],
            send_sem=sems.at[0],
            recv_sem=sems.at[1],
            device_id=(r, d),
            device_id_type=MESH,
        ).start()
        return carry

    lax.fori_loop(1, peers, send, 0)
    for k in range(C_DEV):
        table[k] = cells[k]
    for q in range(2):
        table[C_DEV + 2 * c + q] = outbox[c, q]


def finish_exchange(regions, peers, cells, outbox, table, sems):
    for copy in region_copies(regions, cells, table, sems):
        copy.wait()
    sent = outbox.at[pl.ds(0, peers - 1)]
    pltpu.make_async_copy(sent, sent, sems.at[0]).wait()
    landed = table.at[pl.ds(0, 2 * (peers - 1))]
    pltpu.make_async_copy(landed, landed, sems.at[1]).wait()


def static_kernel(
    regions, peers,
    export, count, position, velocity, smoothing, mass, energy, active,
    table, comp, rank, groups,
    cells, outbox, sems,
):
    slot = lax.broadcasted_iota(jnp.int32, (1, CAP), 1)
    for k in range(C_DEV):
        for i in range(3):
            cells[k, i : i + 1] = position[i, k : k + 1]
            cells[k, 5 + i : 6 + i] = velocity[i, k : k + 1]
        cells[k, 3:4] = jnp.where(slot < count[k], mass[k : k + 1], 0.0)
        cells[k, 4:5] = smoothing[k : k + 1]
    fill_outbox(peers, export, cells, outbox)
    greet(regions, peers)
    start_exchange(regions, peers, cells, outbox, table, sems)

    live = active[...] > 0
    row = lax.broadcasted_iota(jnp.int32, (CAP, CAP), 0)
    col = lax.broadcasted_iota(jnp.int32, (CAP, CAP), 1)
    upper = jnp.where(row <= col, 1.0, 0.0)
    ordinal = jnp.dot(jnp.where(live, 1.0, 0.0), upper, preferred_element_type=F32)
    place = jnp.where(live, ordinal - 1.0, -1.0)
    rank[...] = place
    sub = lax.broadcasted_iota(jnp.int32, (8, CAP), 0)
    for k in range(C_DEV):
        groups[k] = (jnp.sum(active[k : k + 1]) + (GROUP - 1)) // GROUP
        fields = jnp.where(sub == 3, energy[k : k + 1], cells[k])
        picked = jnp.where(place[k : k + 1] == row.astype(F32), 1.0, 0.0)
        comp[k] = lax.dot_general(
            picked, fields, (((1,), (1,)), ((), ())),
            precision=lax.Precision.HIGHEST, preferred_element_type=F32,
        )
    finish_exchange(regions, peers, cells, outbox, table, sems)


def moving_kernel(
    regions, peers, export, energy, density, table, cells, outbox, sems
):
    for k in range(C_DEV):
        cells[k, 0:1] = energy[k : k + 1]
        cells[k, 1:2] = density[k : k + 1]
    fill_outbox(peers, export, cells, outbox)
    greet(regions, peers)
    start_exchange(regions, peers, cells, outbox, table, sems)
    finish_exchange(regions, peers, cells, outbox, table, sems)


def fill_shifts(shifts):
    sub = lax.broadcasted_iota(jnp.int32, (8, CAP), 0)
    for s in range(NB):
        offset = (s // 9 - 1, s // 3 % 3 - 1, s % 3 - 1)
        shifts[s] = jnp.where(
            sub == 0, float(offset[0]),
            jnp.where(sub == 1, float(offset[1]), jnp.where(sub == 2, float(offset[2]), 0.0)),
        )


def wide(column):
    return jnp.broadcast_to(column, (GROUP, CAP))


def density_kernel(
    source, shift, groups, table, comp, rank, active, density_old,
    density, comp_density, shifts, near,
):
    fill_shifts(shifts)
    sub = lax.broadcasted_iota(jnp.int32, (GROUP, CAP), 0)
    cube = 4.0 ** (-1.0 / 3.0)

    def cell(k, carry):
        for n in range(NB):
            near[n] = table[source[k, n]] + shifts[shift[k, n]]
        place = rank[pl.ds(k, 1), :]

        def group(g, total):
            at = pl.multiple_of(g * GROUP, GROUP)
            tile = comp[k, pl.ds(at, GROUP), :]
            x, y, z, h = (wide(tile[:, f : f + 1]) for f in (0, 1, 2, 4))
            inverse = 1.0 / h
            scaled = cube * inverse
            partial = jnp.zeros((GROUP, CAP), F32)
            for n in range(NB):
                dx, dy, dz = x - near[n, 0:1], y - near[n, 1:2], z - near[n, 2:3]
                square = jnp.maximum(dx * dx + dy * dy + dz * dz, TINY)
                radius = square * lax.rsqrt(square)
                outer = jnp.maximum(2.0 * cube - radius * scaled, 0.0)
                inner = jnp.maximum(1.0 - radius * inverse, 0.0)
                value = outer * outer * outer - inner * inner * inner
                partial += near[n, 3:4] * value
            norm = inverse * inverse * inverse * (1.0 / math.pi)
            found = jnp.sum(partial, axis=1, keepdims=True) * norm
            comp_density[k, pl.ds(at, GROUP), :] = found
            here = place == (sub + at).astype(F32)
            return total + jnp.where(here, found, 0.0)

        total = lax.fori_loop(0, groups[k], group, jnp.zeros((GROUP, CAP), F32))
        summed = jnp.sum(total, axis=0, keepdims=True)
        mine = pl.ds(k, 1)
        density[mine, :] = jnp.where(active[mine, :] > 0, summed, density_old[mine, :])
        return carry

    lax.fori_loop(0, C_DEV, cell, 0)


def force_kernel(
    source, shift, groups, table, moving, comp, comp_density, rank, velocity, time_bin,
    acceleration, kicked, shifts, derived, near, more,
):
    fill_shifts(shifts)
    sub = lax.broadcasted_iota(jnp.int32, (GROUP, CAP), 0)

    def derive(s, carry):
        h, m = table[s, 4:5], table[s, 3:4]
        e, rho = moving[s, 0:1], moving[s, 1:2]
        inverse = 1.0 / h
        second = inverse * inverse
        derived[s, 0:1] = second
        derived[s, 1:2] = second * inverse
        derived[s, 2:3] = 0.05 * h
        derived[s, 3:4] = m * (1.5 / math.pi)
        derived[s, 4:5] = (ADIABATIC - 1.0) * e / rho
        derived[s, 5:6] = 0.025 * jnp.sqrt(ADIABATIC * (ADIABATIC - 1.0) * e)
        derived[s, 6:7] = rho * (1.0 / 400.0)
        return carry

    lax.fori_loop(0, table.shape[0], derive, 0, unroll=6)

    def cell(k, carry):
        for n in range(NB):
            s = source[k, n]
            near[n] = table[s] + shifts[shift[k, n]]
            more[n] = derived[s]
        place = rank[pl.ds(k, 1), :]

        def group(g, totals):
            at = pl.multiple_of(g * GROUP, GROUP)
            tile = comp[k, pl.ds(at, GROUP), :]
            x, y, z, e, h, vx, vy, vz = (wide(tile[:, f : f + 1]) for f in range(8))
            rho = comp_density[k, pl.ds(at, GROUP), :]
            inverse = 1.0 / h
            second = inverse * inverse
            third = second * inverse
            small = 0.05 * h
            press = (ADIABATIC - 1.0) * e / rho
            sound = 0.025 * jnp.sqrt(ADIABATIC * (ADIABATIC - 1.0) * e)
            thin = rho * (1.0 / 400.0)
            ax = ay = az = jnp.zeros((GROUP, CAP), F32)
            for n in range(NB):
                dx, dy, dz = x - near[n, 0:1], y - near[n, 1:2], z - near[n, 2:3]
                square = jnp.maximum(dx * dx + dy * dy + dz * dz, TINY)
                over = lax.rsqrt(square)
                radius = square * over
                reach = radius * third
                outer = jnp.maximum(second - 0.5 * reach, 0.0)
                inner = jnp.maximum(second - reach, 0.0)
                slope = outer * outer - inner * inner
                second_j = more[n, 0:1]
                reach = radius * more[n, 1:2]
                outer = jnp.maximum(second_j - 0.5 * reach, 0.0)
                inner = jnp.maximum(second_j - reach, 0.0)
                slope += outer * outer - inner * inner
                approach = (
                    (vx - near[n, 5:6]) * dx
                    + (vy - near[n, 6:7]) * dy
                    + (vz - near[n, 7:8]) * dz
                )
                mean = small + more[n, 2:3]
                mu = mean * jnp.minimum(approach, 0.0) * (1.0 / (square + mean * mean))
                viscous = mu * (mu - (sound + more[n, 5:6])) * (1.0 / (thin + more[n, 6:7]))
                weight = more[n, 3:4] * (press + more[n, 4:5] + viscous) * (slope * over)
                ax += weight * dx
                ay += weight * dy
                az += weight * dz
            here = place == (sub + at).astype(F32)
            return tuple(
                total + jnp.where(here, jnp.sum(part, axis=1, keepdims=True), 0.0)
                for total, part in zip(totals, (ax, ay, az))
            )

        none = jnp.zeros((GROUP, CAP), F32)
        totals = lax.fori_loop(0, groups[k], group, (none, none, none))
        mine = pl.ds(k, 1)
        step = STEP_MAX * jnp.exp2(-time_bin[mine, :].astype(F32))
        for i in range(3):
            found = jnp.sum(totals[i], axis=0, keepdims=True)
            acceleration[i, mine, :] = found
            kicked[i, mine, :] = velocity[i, mine, :] + found * step
        return carry

    lax.fori_loop(0, C_DEV, cell, 0)


def shards(
    regions, peers,
    position, velocity, smoothing, particle_mass, energy, density_old, cell_count, active,
    time_bin, pair_source, pair_shift, export,
):
    size = C_DEV + 2 * peers + 2
    vmem = pl.BlockSpec(memory_space=pltpu.VMEM)
    smem = pl.BlockSpec(memory_space=pltpu.SMEM)

    def shape(*dims, dtype=F32):
        return jax.ShapeDtypeStruct(dims, dtype)

    def exchange_scratch(rows):
        return [
            pltpu.VMEM((C_DEV, rows, CAP), F32),
            pltpu.VMEM((peers, 2, rows, CAP), F32),
            pltpu.SemaphoreType.DMA((6,)),
        ]

    limit = 48 << 20
    table, comp, rank, groups = pl.pallas_call(
        functools.partial(static_kernel, regions, peers),
        out_shape=[
            shape(size, 8, CAP), shape(C_DEV, CAP, 8), shape(C_DEV, CAP),
            shape(C_DEV, dtype=jnp.int32),
        ],
        in_specs=[smem, smem] + [vmem] * 6,
        out_specs=[vmem, vmem, vmem, smem],
        scratch_shapes=exchange_scratch(8),
        compiler_params=pltpu.CompilerParams(
            collective_id=0, has_side_effects=True, vmem_limit_bytes=limit
        ),
    )(export, cell_count, position, velocity, smoothing, particle_mass, energy, active)
    density, comp_density = pl.pallas_call(
        density_kernel,
        out_shape=[shape(C_DEV, CAP), shape(C_DEV, CAP, CAP)],
        in_specs=[smem] * 3 + [vmem] * 5,
        out_specs=[vmem, vmem],
        scratch_shapes=[pltpu.VMEM((NB, 8, CAP), F32), pltpu.VMEM((NB, 8, CAP), F32)],
        compiler_params=pltpu.CompilerParams(vmem_limit_bytes=limit),
    )(pair_source, pair_shift, groups, table, comp, rank, active, density_old)
    moving = pl.pallas_call(
        functools.partial(moving_kernel, regions, peers),
        out_shape=shape(size, 2, CAP),
        in_specs=[smem, vmem, vmem],
        out_specs=vmem,
        scratch_shapes=exchange_scratch(2),
        compiler_params=pltpu.CompilerParams(
            collective_id=1, has_side_effects=True, vmem_limit_bytes=limit
        ),
    )(export, energy, density)
    acceleration, kicked = pl.pallas_call(
        force_kernel,
        out_shape=[shape(3, C_DEV, CAP), shape(3, C_DEV, CAP)],
        in_specs=[smem] * 3 + [vmem] * 7,
        out_specs=[vmem, vmem],
        scratch_shapes=[
            pltpu.VMEM((NB, 8, CAP), F32),
            pltpu.VMEM((size, 8, CAP), F32),
            pltpu.VMEM((NB, 8, CAP), F32),
            pltpu.VMEM((NB, 8, CAP), F32),
        ],
        compiler_params=pltpu.CompilerParams(vmem_limit_bytes=limit),
    )(
        pair_source, pair_shift, groups, table, moving, comp, comp_density, rank, velocity,
        time_bin,
    )
    return density, acceleration, kicked


def solution(mesh):
    both = ("region", "cell")
    flat, wide_rows = P(both, None), P(None, both, None)
    return jax.shard_map(
        functools.partial(shards, mesh.shape["region"], mesh.shape["cell"]),
        mesh=mesh,
        in_specs=(
            wide_rows, wide_rows, flat, flat, flat, flat, P(both), flat, flat, flat, flat, flat,
        ),
        out_specs=(flat, wide_rows, wide_rows),
        check_vma=False,
    )
```

```python
import functools
import math

import jax
import jax.numpy as jnp
from jax import lax
from jax.experimental import pallas as pl
from jax.experimental.pallas import tpu as pltpu
from jax.sharding import PartitionSpec as P

MESH = pl.DeviceIdType.MESH
C_DEV = 8
CAP = 128
NB = 27
GROUP = 8
PLANE = 8
ORDER = (1, 7, 2, 6, 3, 5, 4)
BATCH = 4
ADIABATIC = 5.0 / 3.0
STEP_MAX = 0.2
TINY = 1e-30
F32 = jnp.float32
SHIFT_AT, GROUP_AT = 32, 64


def place():
    r, c = lax.axis_index("region"), lax.axis_index("cell")
    return r, lax.div(c, PLANE), lax.rem(c, PLANE)


def along(z, u, planes, ahead):
    return lax.rem(z + ahead, planes) * PLANE + u


def across(z, u, ahead):
    return z * PLANE + lax.rem(u + ahead, PLANE)


def greet(regions, planes):
    r, z, u = place()
    barrier = pltpu.get_barrier_semaphore()
    for ahead in range(1, planes):
        pl.semaphore_signal(
            barrier, inc=1, device_id=(r, along(z, u, planes, ahead)), device_id_type=MESH
        )
    for ahead in range(1, PLANE):
        pl.semaphore_signal(
            barrier, inc=1, device_id=(r, across(z, u, ahead)), device_id_type=MESH
        )
    for ahead in (1, regions - 1):
        pl.semaphore_signal(
            barrier, inc=1, device_id=(lax.rem(r + ahead, regions), z * PLANE + u),
            device_id_type=MESH,
        )
    return lambda: pl.semaphore_wait(barrier, planes + PLANE)


def region_copies(regions, cells, table, sems):
    r, z, u = place()
    size = table.shape[0]
    up = pltpu.make_async_remote_copy(
        src_ref=cells.at[pl.ds(C_DEV - 1, 1)],
        dst_ref=table.at[pl.ds(size - 2, 1)],
        send_sem=sems.at[0],
        recv_sem=sems.at[1],
        device_id=(lax.rem(r + 1, regions), z * PLANE + u),
        device_id_type=MESH,
    )
    down = pltpu.make_async_remote_copy(
        src_ref=cells.at[pl.ds(0, 1)],
        dst_ref=table.at[pl.ds(size - 1, 1)],
        send_sem=sems.at[2],
        recv_sem=sems.at[3],
        device_id=(lax.rem(r + regions - 1, regions), z * PLANE + u),
        device_id_type=MESH,
    )
    return up, down


def send_along(planes, ahead, source, target, send_sem, recv_sem):
    r, z, u = place()
    return pltpu.make_async_remote_copy(
        src_ref=source, dst_ref=target, send_sem=send_sem, recv_sem=recv_sem,
        device_id=(r, along(z, u, planes, ahead)), device_id_type=MESH,
    )


def send_across(first, cells, outbox, table, send_sem, recv_sem):
    r, z, u = place()
    rows = 2 * BATCH

    def send(ahead, carry):
        to = lax.rem(u + ahead, PLANE)
        pltpu.make_async_remote_copy(
            src_ref=outbox.at[to, pl.ds(2 * first, rows)],
            dst_ref=table.at[pl.ds(C_DEV + 2 * cells * u + 2 * first, rows)],
            send_sem=send_sem, recv_sem=recv_sem,
            device_id=(r, z * PLANE + to), device_id_type=MESH,
        ).start()
        return carry

    lax.fori_loop(1, PLANE, send, 0)


def choose(slot, export, cells, outbox):
    r, z, u = place()

    def fill(to, carry):
        for q in range(2):
            outbox[to, 2 * slot + q] = cells[export[slot, q, z * PLANE + to]]
        return carry

    lax.fori_loop(0, PLANE, fill, 0, unroll=True)


def keep_own(planes, cells, outbox, table):
    r, z, u = place()
    for k in range(C_DEV):
        table[k] = cells[k]
    for i in range(2 * planes):
        table[C_DEV + 2 * planes * u + i] = outbox[u, i]


def drain(planes, outbox, table, send_sem, recv_sem):
    sent = outbox.at[pl.ds(0, PLANE - 1)]
    pltpu.make_async_copy(sent, sent, send_sem).wait()
    landed = table.at[pl.ds(0, 2 * planes * (PLANE - 1))]
    pltpu.make_async_copy(landed, landed, recv_sem).wait()


def static_kernel(
    regions, planes,
    position, velocity, smoothing, mass, energy, active, count, export, source, shift, old,
    table, comp, rank, plan, exports, energy_v, old_v,
    position_v, velocity_v, smoothing_v, mass_v, active_v, count_s, source_v, shift_v,
    cells, exports_s, outbox, *rest,
):
    land, (fetch_sems, region_sems, export_sems, along_send, along_recv, across_sems, own_sem) = (
        rest[: planes - 1], rest[planes - 1 :]
    )
    wait_for_all = greet(regions, planes)
    fetches = [
        pltpu.make_async_copy(a, b, fetch_sems.at[i])
        for i, (a, b) in enumerate((
            (position, position_v), (smoothing, smoothing_v), (mass, mass_v), (count, count_s),
            (velocity, velocity_v), (export, exports.at[0]), (energy, energy_v),
            (active, active_v), (source, source_v), (shift, shift_v), (old, old_v),
        ))
    ]
    for fetch in fetches:
        fetch.start()
    for fetch in fetches:
        fetch.wait()
    slot = lax.broadcasted_iota(jnp.int32, (1, CAP), 1)
    for k in range(C_DEV):
        for i in range(3):
            cells[k, i : i + 1] = position_v[i, k : k + 1]
            cells[k, 5 + i : 6 + i] = velocity_v[i, k : k + 1]
        cells[k, 3:4] = jnp.where(slot < count_s[k], mass_v[k : k + 1], 0.0)
        cells[k, 4:5] = smoothing_v[k : k + 1]
    wait_for_all()
    regionals = region_copies(regions, cells, table, region_sems)
    lists = [
        send_along(
            planes, ahead, exports.at[0], exports.at[i + 1], export_sems.at[0], export_sems.at[1]
        )
        for i, ahead in enumerate(ORDER)
    ]
    blocks = [
        send_along(planes, ahead, cells, land[i], along_send.at[i], along_recv.at[i])
        for i, ahead in enumerate(ORDER)
    ]
    for copy in lists + blocks[:2] + list(regionals) + blocks[2:]:
        copy.start()

    live = active_v[...] > 0
    row = lax.broadcasted_iota(jnp.int32, (CAP, CAP), 0)
    col = lax.broadcasted_iota(jnp.int32, (CAP, CAP), 1)
    upper = jnp.where(row <= col, 1.0, 0.0)
    ordinal = jnp.dot(jnp.where(live, 1.0, 0.0), upper, preferred_element_type=F32)
    where_to = jnp.where(live, ordinal - 1.0, -1000.0)
    rank[...] = where_to
    groups = (jnp.sum(active_v[...], axis=1, keepdims=True) + (GROUP - 1)) // GROUP
    r, z, u = place()
    named = source_v[...]
    other = named - C_DEV
    behind = jnp.bitwise_and(z + planes - jnp.right_shift(other, 4), planes - 1)
    slot_of = jnp.zeros_like(behind)
    for i, ahead in enumerate(ORDER):
        slot_of = jnp.where(behind == ahead, i + 1, slot_of)
    peer = jnp.bitwise_and(jnp.right_shift(other, 1), PLANE - 1)
    moved = C_DEV + 2 * planes * peer + 2 * slot_of + jnp.bitwise_and(other, 1)
    inside = jnp.logical_and(named >= C_DEV, named < C_DEV + 2 * planes * PLANE)
    plan[:, 0:NB] = jnp.where(inside, moved, named)
    plan[:, SHIFT_AT : SHIFT_AT + NB] = shift_v[...]
    plan[:, GROUP_AT : GROUP_AT + 1] = groups

    drained = exports.at[pl.ds(1, planes - 1)]
    pltpu.make_async_copy(drained, drained, export_sems.at[1]).wait()
    pltpu.make_async_copy(drained, drained, export_sems.at[0]).wait()
    to_scalar = pltpu.make_async_copy(exports, exports_s, own_sem)
    to_scalar.start()
    to_scalar.wait()
    choose(0, exports_s, cells, outbox)
    sub = lax.broadcasted_iota(jnp.int32, (8, CAP), 0)

    def compact(k):
        fields = jnp.where(sub == 3, energy_v[k : k + 1], cells[k])
        picked = jnp.where(where_to[k : k + 1] == row.astype(F32), 1.0, 0.0)
        comp[k] = lax.dot_general(
            picked, fields, (((1,), (1,)), ((), ())),
            precision=lax.Precision.HIGHEST, preferred_element_type=F32,
        )

    for i in range(planes - 1):
        compact(i)
        blocks[i].wait_recv()
        choose(i + 1, exports_s, land[i], outbox)
        if (i + 2) % BATCH == 0:
            send_across(
                i + 2 - BATCH, planes, outbox, table, across_sems.at[0], across_sems.at[1]
            )
    compact(planes - 1)
    keep_own(planes, cells, outbox, table)
    for copy in regionals:
        copy.wait()
    for copy in blocks:
        copy.wait_send()
    drain(planes, outbox, table, across_sems.at[0], across_sems.at[1])


def moving_kernel(
    regions, planes, exports, energy, density, table,
    cells, land, outbox, region_sems, along_sems, across_sems,
):
    wait_for_all = greet(regions, planes)
    for k in range(C_DEV):
        cells[k, 0:1] = energy[k : k + 1]
        cells[k, 1:2] = density[k : k + 1]
    wait_for_all()
    regionals = region_copies(regions, cells, table, region_sems)
    blocks = [
        send_along(planes, ahead, cells, land.at[i], along_sems.at[0], along_sems.at[1])
        for i, ahead in enumerate(ORDER)
    ]
    for copy in blocks + list(regionals):
        copy.start()
    choose(0, exports, cells, outbox)
    pltpu.make_async_copy(land, land, along_sems.at[1]).wait()
    for i in range(planes - 1):
        choose(i + 1, exports, land.at[i], outbox)
        if (i + 2) % BATCH == 0:
            send_across(
                i + 2 - BATCH, planes, outbox, table, across_sems.at[0], across_sems.at[1]
            )
    keep_own(planes, cells, outbox, table)
    for copy in regionals:
        copy.wait()
    pltpu.make_async_copy(land, land, along_sems.at[0]).wait()
    drain(planes, outbox, table, across_sems.at[0], across_sems.at[1])


def fill_shifts(shifts):
    sub = lax.broadcasted_iota(jnp.int32, (8, CAP), 0)
    for s in range(NB):
        offset = (s // 9 - 1, s // 3 % 3 - 1, s % 3 - 1)
        shifts[s] = jnp.where(
            sub == 0, float(offset[0]),
            jnp.where(sub == 1, float(offset[1]), jnp.where(sub == 2, float(offset[2]), 0.0)),
        )


def wide(column):
    return jnp.broadcast_to(column, (GROUP, CAP))


def gather(plan, k, block_of, near):
    for n in range(NB):
        near[n] = block_of(plan[k, n], n)


def density_kernel(
    plan, table, comp, rank, density_old,
    density, density_too, comp_density,
    shifts, near, total,
):
    fill_shifts(shifts)
    sub = lax.broadcasted_iota(jnp.int32, (GROUP, CAP), 0)
    cube = 4.0 ** (-1.0 / 3.0)

    def cell(k, carry):
        gather(plan, k, lambda s, n: table[s] + shifts[plan[k, SHIFT_AT + n]], near)
        ranks = rank[pl.ds(k, 1), :]
        total[...] = jnp.zeros((GROUP, CAP), F32)
        groups = plan[k, GROUP_AT]

        def setup(g):
            at = pl.multiple_of(jnp.minimum(g, CAP // GROUP - 1) * GROUP, GROUP)
            tile = comp[k, pl.ds(at, GROUP), :]
            x, y, z, h = (wide(tile[:, f : f + 1]) for f in (0, 1, 2, 4))
            return x, y, z, 1.0 / h

        def finish(g, partial, norm):
            found = jnp.sum(partial, axis=1, keepdims=True) * norm
            at = pl.multiple_of(jnp.maximum(g, 0) * GROUP, GROUP)
            comp_density[k, pl.ds(at, GROUP), :] = found
            here = ranks == (sub + g * GROUP).astype(F32)
            total[...] += jnp.where(here, found, 0.0)

        def run(size):
            def group(g, carry):
                (x, y, z, inverse), partial, norm = carry
                finish(g - 1, partial, norm)
                following = setup(g + 1)
                scaled = cube * inverse
                partial = jnp.zeros((GROUP, CAP), F32)
                for n in range(size):
                    dx, dy, dz = x - near[n, 0:1], y - near[n, 1:2], z - near[n, 2:3]
                    square = jnp.maximum(dx * dx + dy * dy + dz * dz, TINY)
                    radius = square * lax.rsqrt(square)
                    outer = jnp.maximum(2.0 * cube - radius * scaled, 0.0)
                    inner = jnp.maximum(1.0 - radius * inverse, 0.0)
                    value = outer * outer * outer - inner * inner * inner
                    partial += near[n, 3:4] * value
                return following, partial, inverse * inverse * inverse * (1.0 / math.pi)

            none = jnp.zeros((GROUP, CAP), F32)
            _, partial, norm = lax.fori_loop(0, groups, group, (setup(0), none, none))
            finish(groups - 1, partial, norm)

        run(NB)
        summed = jnp.sum(total[...], axis=0, keepdims=True)
        mine = pl.ds(k, 1)
        found = jnp.where(ranks >= 0.0, summed, density_old[mine, :])
        density[mine, :] = found
        density_too[mine, :] = found
        return carry

    lax.fori_loop(0, C_DEV, cell, 0)


def force_kernel(
    plan, table, moving, comp, comp_density, rank, velocity, time_bin,
    acceleration, kicked, shifts, near, derived, more, total,
):
    sub = lax.broadcasted_iota(jnp.int32, (GROUP, CAP), 0)

    def derive(s, carry):
        h, m = table[s, 4:5], table[s, 3:4]
        e, rho = moving[s, 0:1], moving[s, 1:2]
        inverse = 1.0 / h
        second = inverse * inverse
        derived[s, 0:1] = second
        derived[s, 1:2] = second * inverse
        derived[s, 2:3] = 0.05 * h
        derived[s, 3:4] = m * (1.5 / math.pi)
        derived[s, 4:5] = (ADIABATIC - 1.0) * e / rho
        derived[s, 5:6] = 0.025 * jnp.sqrt(ADIABATIC * (ADIABATIC - 1.0) * e)
        derived[s, 6:7] = rho * (1.0 / 400.0)
        derived[s, 7:8] = rho
        return carry

    fill_shifts(shifts)
    lax.fori_loop(0, table.shape[0], derive, 0, unroll=6)

    def cell(k, carry):
        gather(plan, k, lambda s, n: table[s] + shifts[plan[k, SHIFT_AT + n]], near)
        gather(plan, k, lambda s, n: derived[s], more)
        ranks = rank[pl.ds(k, 1), :]
        total[...] = jnp.zeros((3, GROUP, CAP), F32)
        groups = plan[k, GROUP_AT]

        def setup(g):
            at = pl.multiple_of(jnp.minimum(g, CAP // GROUP - 1) * GROUP, GROUP)
            tile = comp[k, pl.ds(at, GROUP), :]
            x, y, z, e, h, vx, vy, vz = (wide(tile[:, f : f + 1]) for f in range(8))
            rho = comp_density[k, pl.ds(at, GROUP), :]
            inverse = 1.0 / h
            second = inverse * inverse
            press = (ADIABATIC - 1.0) * e / rho
            sound = 0.025 * jnp.sqrt(ADIABATIC * (ADIABATIC - 1.0) * e)
            return (
                x, y, z, vx, vy, vz, second, second * inverse, 0.05 * h, press, sound,
                rho * (1.0 / 400.0),
            )

        def finish(g, parts):
            here = ranks == (sub + g * GROUP).astype(F32)
            for i in range(3):
                total[i] += jnp.where(here, jnp.sum(parts[i], axis=1, keepdims=True), 0.0)

        def run(size):
            def group(g, carry):
                (x, y, z, vx, vy, vz, second, third, small, press, sound, thin), parts = carry
                finish(g - 1, parts)
                following = setup(g + 1)
                ax = ay = az = jnp.zeros((GROUP, CAP), F32)
                for n in range(size):
                    dx, dy, dz = x - near[n, 0:1], y - near[n, 1:2], z - near[n, 2:3]
                    square = jnp.maximum(dx * dx + dy * dy + dz * dz, TINY)
                    over = lax.rsqrt(square)
                    radius = square * over
                    reach = radius * third
                    outer = jnp.maximum(second - 0.5 * reach, 0.0)
                    inner = jnp.maximum(second - reach, 0.0)
                    slope = outer * outer - inner * inner
                    second_j = more[n, 0:1]
                    reach = radius * more[n, 1:2]
                    outer = jnp.maximum(second_j - 0.5 * reach, 0.0)
                    inner = jnp.maximum(second_j - reach, 0.0)
                    slope += outer * outer - inner * inner
                    approach = (
                        (vx - near[n, 5:6]) * dx
                        + (vy - near[n, 6:7]) * dy
                        + (vz - near[n, 7:8]) * dz
                    )
                    mean = small + more[n, 2:3]
                    mu = mean * jnp.minimum(approach, 0.0) * (1.0 / (square + mean * mean))
                    viscous = mu * (mu - (sound + more[n, 5:6])) * (1.0 / (thin + more[n, 6:7]))
                    weight = more[n, 3:4] * (press + more[n, 4:5] + viscous) * (slope * over)
                    ax += weight * dx
                    ay += weight * dy
                    az += weight * dz
                return following, (ax, ay, az)

            none = jnp.zeros((GROUP, CAP), F32)
            _, parts = lax.fori_loop(0, groups, group, (setup(0), (none, none, none)))
            finish(groups - 1, parts)

        run(NB)
        mine = pl.ds(k, 1)
        step = STEP_MAX * jnp.exp2(-time_bin[mine, :].astype(F32))
        for i in range(3):
            found = jnp.sum(total[i], axis=0, keepdims=True)
            acceleration[i, mine, :] = found
            kicked[i, mine, :] = velocity[i, mine, :] + found * step
        return carry

    lax.fori_loop(0, C_DEV, cell, 0)


def shards(
    regions, planes,
    position, velocity, smoothing, particle_mass, energy, density_old, cell_count, active,
    time_bin, pair_source, pair_shift, export,
):
    size = C_DEV + 2 * planes * PLANE + 2
    vmem = pl.BlockSpec(memory_space=pltpu.VMEM)
    smem = pl.BlockSpec(memory_space=pltpu.SMEM)
    hbm = pl.BlockSpec(memory_space=pltpu.HBM)
    dma = pltpu.SemaphoreType.DMA

    def shape(*dims, dtype=F32):
        return jax.ShapeDtypeStruct(dims, dtype)

    def ints(*dims):
        return pltpu.VMEM(dims, jnp.int32)

    def floats(*dims):
        return pltpu.VMEM(dims, F32)

    limit = 48 << 20
    table, comp, rank, plan, exports, energy, density_old = pl.pallas_call(
        functools.partial(static_kernel, regions, planes),
        out_shape=[
            shape(size, 8, CAP), shape(C_DEV, CAP, 8), shape(C_DEV, CAP),
            shape(C_DEV, CAP, dtype=jnp.int32),
            shape(planes, 2, planes * PLANE, dtype=jnp.int32), shape(C_DEV, CAP), shape(C_DEV, CAP),
        ],
        in_specs=[hbm] * 11,
        out_specs=[vmem] * 7,
        scratch_shapes=[
            floats(3, C_DEV, CAP), floats(3, C_DEV, CAP), floats(C_DEV, CAP), floats(C_DEV, CAP),
            ints(C_DEV, CAP), pltpu.SMEM((C_DEV,), jnp.int32),
            ints(C_DEV, NB), ints(C_DEV, NB),
            floats(C_DEV, 8, CAP), pltpu.SMEM((planes, 2, planes * PLANE), jnp.int32),
            floats(PLANE, 2 * planes, 8, CAP),
            *[floats(C_DEV, 8, CAP) for _ in range(planes - 1)],
            dma((11,)), dma((4,)), dma((2,)), dma((planes - 1,)), dma((planes - 1,)), dma((2,)),
            dma,
        ],
        compiler_params=pltpu.CompilerParams(
            collective_id=0, has_side_effects=True, vmem_limit_bytes=limit
        ),
    )(
        *(
            pltpu.with_memory_space_constraint(x, pltpu.HBM)
            for x in (
                position, velocity, smoothing, particle_mass, energy, active, cell_count, export.T,
                pair_source, pair_shift, density_old,
            )
        )
    )
    density, density_too, comp_density = pl.pallas_call(
        density_kernel,
        out_shape=[shape(C_DEV, CAP), shape(C_DEV, CAP), shape(C_DEV, CAP, CAP)],
        in_specs=[smem] + [vmem] * 4,
        out_specs=[vmem] * 3,
        scratch_shapes=[floats(NB, 8, CAP), floats(NB, 8, CAP), floats(GROUP, CAP)],
        compiler_params=pltpu.CompilerParams(vmem_limit_bytes=limit),
    )(plan, table, comp, rank, density_old)
    moving = pl.pallas_call(
        functools.partial(moving_kernel, regions, planes),
        out_shape=shape(size, 2, CAP),
        in_specs=[smem, vmem, vmem],
        out_specs=vmem,
        scratch_shapes=[
            floats(C_DEV, 2, CAP), floats(planes - 1, C_DEV, 2, CAP),
            floats(PLANE, 2 * planes, 2, CAP), dma((4,)), dma((2,)), dma((2,)),
        ],
        compiler_params=pltpu.CompilerParams(
            collective_id=1, has_side_effects=True, vmem_limit_bytes=limit
        ),
    )(exports, energy, density_too)
    acceleration, kicked = pl.pallas_call(
        force_kernel,
        out_shape=[shape(3, C_DEV, CAP), shape(3, C_DEV, CAP)],
        in_specs=[smem] + [vmem] * 7,
        out_specs=[vmem, vmem],
        scratch_shapes=[
            floats(NB, 8, CAP), floats(NB, 8, CAP), floats(size, 8, CAP), floats(NB, 8, CAP),
            floats(3, GROUP, CAP),
        ],
        compiler_params=pltpu.CompilerParams(vmem_limit_bytes=limit),
    )(plan, table, moving, comp, comp_density, rank, velocity, time_bin)
    return density, acceleration, kicked


def solution(mesh):
    both = ("region", "cell")
    flat, wide_rows = P(both, None), P(None, both, None)
    return jax.shard_map(
        functools.partial(shards, mesh.shape["region"], mesh.shape["cell"] // PLANE),
        mesh=mesh,
        in_specs=(
            wide_rows, wide_rows, flat, flat, flat, flat, P(both), flat, flat, flat, flat, flat,
        ),
        out_specs=(flat, wide_rows, wide_rows),
        check_vma=False,
    )
```

```python
import functools
import math

import jax
import jax.numpy as jnp
from jax import lax
from jax.experimental import pallas as pl
from jax.experimental.pallas import tpu as pltpu
from jax.sharding import PartitionSpec as P

MESH = pl.DeviceIdType.MESH
C_DEV = 8
CAP = 128
NB = 27
GROUP = 8
PLANE = 8
ORDER = (1, 7, 4, 2, 6, 3, 5)
BATCH = 2
ADIABATIC = 5.0 / 3.0
STEP_MAX = 0.2
TINY = 1e-30
F32 = jnp.float32
SHIFT_AT, GROUP_AT = 32, 64
SIZES = (8, 12, 15, 16, 17, 18, 19, 20, 22, 24, 27)
ROWS = NB + 8
X, Y, Z, INVERSE, VX, VY, VZ, SECOND, THIRD, SMALL, SOUND, HEAT = range(12)
TARGET = 12
SOUND_UNIT = 0.025
DENSITY_UNIT = 1.0 / 400.0


def place():
    r, c = lax.axis_index("region"), lax.axis_index("cell")
    return r, lax.div(c, PLANE), lax.rem(c, PLANE)


def along(z, u, planes, ahead):
    return lax.rem(z + ahead, planes) * PLANE + u


def across(z, u, ahead):
    return z * PLANE + lax.rem(u + ahead, PLANE)


def greet(regions, planes):
    r, z, u = place()
    barrier = pltpu.get_barrier_semaphore()
    for ahead in range(1, planes):
        pl.semaphore_signal(
            barrier, inc=1, device_id=(r, along(z, u, planes, ahead)), device_id_type=MESH
        )
    for ahead in range(1, PLANE):
        pl.semaphore_signal(
            barrier, inc=1, device_id=(r, across(z, u, ahead)), device_id_type=MESH
        )
    for ahead in (1, regions - 1):
        pl.semaphore_signal(
            barrier, inc=1, device_id=(lax.rem(r + ahead, regions), z * PLANE + u),
            device_id_type=MESH,
        )
    return lambda: pl.semaphore_wait(barrier, planes + PLANE)


def region_copies(regions, cells, table, sems):
    r, z, u = place()
    size = table.shape[0]
    up = pltpu.make_async_remote_copy(
        src_ref=cells.at[pl.ds(C_DEV - 1, 1)],
        dst_ref=table.at[pl.ds(size - 2, 1)],
        send_sem=sems.at[0],
        recv_sem=sems.at[1],
        device_id=(lax.rem(r + 1, regions), z * PLANE + u),
        device_id_type=MESH,
    )
    down = pltpu.make_async_remote_copy(
        src_ref=cells.at[pl.ds(0, 1)],
        dst_ref=table.at[pl.ds(size - 1, 1)],
        send_sem=sems.at[2],
        recv_sem=sems.at[3],
        device_id=(lax.rem(r + regions - 1, regions), z * PLANE + u),
        device_id_type=MESH,
    )
    return up, down


def send_along(planes, ahead, source, target, send_sem, recv_sem):
    r, z, u = place()
    return pltpu.make_async_remote_copy(
        src_ref=source, dst_ref=target, send_sem=send_sem, recv_sem=recv_sem,
        device_id=(r, along(z, u, planes, ahead)), device_id_type=MESH,
    )


def send_across(first, cells, outbox, table, send_sem, recv_sem):
    r, z, u = place()
    rows = 2 * BATCH

    def send(ahead, carry):
        to = lax.rem(u + ahead, PLANE)
        pltpu.make_async_remote_copy(
            src_ref=outbox.at[to, pl.ds(2 * first, rows)],
            dst_ref=table.at[pl.ds(C_DEV + 2 * cells * u + 2 * first, rows)],
            send_sem=send_sem, recv_sem=recv_sem,
            device_id=(r, z * PLANE + to), device_id_type=MESH,
        ).start()
        return carry

    lax.fori_loop(1, PLANE, send, 0)


def choose(slot, export, cells, outbox):
    r, z, u = place()

    def fill(to, carry):
        for q in range(2):
            outbox[to, 2 * slot + q] = cells[export[slot, q, z * PLANE + to]]
        return carry

    lax.fori_loop(0, PLANE, fill, 0, unroll=True)


def keep_own(planes, cells, outbox, table):
    r, z, u = place()
    for k in range(C_DEV):
        table[k] = cells[k]
    for i in range(2 * planes):
        table[C_DEV + 2 * planes * u + i] = outbox[u, i]


def drain(planes, outbox, table, send_sem, recv_sem):
    sent = outbox.at[pl.ds(0, PLANE - 1)]
    pltpu.make_async_copy(sent, sent, send_sem).wait()
    landed = table.at[pl.ds(0, 2 * planes * (PLANE - 1))]
    pltpu.make_async_copy(landed, landed, recv_sem).wait()


def static_kernel(
    regions, planes,
    position, velocity, smoothing, mass, energy, active, count, export, source, shift, old,
    table, targets, rank, plan, exports, energy_v, old_v,
    position_v, velocity_v, smoothing_v, mass_v, active_v, count_s, source_v, shift_v,
    cells, exports_s, outbox, *rest,
):
    land, (fetch_sems, region_sems, export_sems, along_send, along_recv, across_sems, own_sem) = (
        rest[: planes - 1], rest[planes - 1 :]
    )
    wait_for_all = greet(regions, planes)
    fetches = [
        pltpu.make_async_copy(a, b, fetch_sems.at[i])
        for i, (a, b) in enumerate((
            (position, position_v), (smoothing, smoothing_v), (mass, mass_v), (count, count_s),
            (velocity, velocity_v), (export, exports.at[0]), (energy, energy_v),
            (active, active_v), (source, source_v), (shift, shift_v), (old, old_v),
        ))
    ]
    for fetch in fetches:
        fetch.start()
    for fetch in fetches:
        fetch.wait()
    slot = lax.broadcasted_iota(jnp.int32, (1, CAP), 1)
    for k in range(C_DEV):
        for i in range(3):
            cells[k, i : i + 1] = position_v[i, k : k + 1]
            cells[k, 5 + i : 6 + i] = velocity_v[i, k : k + 1]
        cells[k, 3:4] = jnp.where(slot < count_s[k], mass_v[k : k + 1], 0.0)
        cells[k, 4:5] = smoothing_v[k : k + 1]
    wait_for_all()
    regionals = region_copies(regions, cells, table, region_sems)
    lists = [
        send_along(
            planes, ahead, exports.at[0], exports.at[i + 1], export_sems.at[0], export_sems.at[1]
        )
        for i, ahead in enumerate(ORDER)
    ]
    blocks = [
        send_along(planes, ahead, cells, land[i], along_send.at[i], along_recv.at[i])
        for i, ahead in enumerate(ORDER)
    ]
    for copy in lists + blocks[:2] + list(regionals) + blocks[2:]:
        copy.start()

    live = active_v[...] > 0
    row = lax.broadcasted_iota(jnp.int32, (CAP, CAP), 0)
    col = lax.broadcasted_iota(jnp.int32, (CAP, CAP), 1)
    upper = jnp.where(row <= col, 1.0, 0.0)
    ordinal = jnp.dot(jnp.where(live, 1.0, 0.0), upper, preferred_element_type=F32)
    where_to = jnp.where(live, ordinal - 1.0, -1000.0)
    rank[...] = where_to
    groups = (jnp.sum(active_v[...], axis=1, keepdims=True) + (GROUP - 1)) // GROUP
    r, z, u = place()
    named = source_v[...]
    other = named - C_DEV
    behind = jnp.bitwise_and(z + planes - jnp.right_shift(other, 4), planes - 1)
    slot_of = jnp.zeros_like(behind)
    for i, ahead in enumerate(ORDER):
        slot_of = jnp.where(behind == ahead, i + 1, slot_of)
    peer = jnp.bitwise_and(jnp.right_shift(other, 1), PLANE - 1)
    moved = C_DEV + 2 * planes * peer + 2 * slot_of + jnp.bitwise_and(other, 1)
    inside = jnp.logical_and(named >= C_DEV, named < C_DEV + 2 * planes * PLANE)
    plan[:, 0:NB] = jnp.where(inside, moved, named)
    plan[:, SHIFT_AT : SHIFT_AT + NB] = shift_v[...]
    plan[:, GROUP_AT : GROUP_AT + 1] = groups

    drained = exports.at[pl.ds(1, planes - 1)]
    pltpu.make_async_copy(drained, drained, export_sems.at[1]).wait()
    pltpu.make_async_copy(drained, drained, export_sems.at[0]).wait()
    to_scalar = pltpu.make_async_copy(exports, exports_s, own_sem)
    to_scalar.start()
    to_scalar.wait()
    choose(0, exports_s, cells, outbox)
    sub = lax.broadcasted_iota(jnp.int32, (8, CAP), 0)

    def compact(k):
        fields = jnp.where(sub == 3, energy_v[k : k + 1], cells[k])
        picked = jnp.where(where_to[k : k + 1] == row.astype(F32), 1.0, 0.0)
        found = lax.dot_general(
            picked, fields, (((1,), (1,)), ((), ())),
            precision=lax.Precision.HIGHEST, preferred_element_type=F32,
        )
        x, y, z, e, h, vx, vy, vz = (
            jnp.broadcast_to(found[:, f : f + 1], (CAP, CAP)) for f in range(8)
        )
        inverse = 1.0 / h
        second = inverse * inverse
        for at, value in (
            (X, x), (Y, y), (Z, z), (INVERSE, inverse), (VX, vx), (VY, vy), (VZ, vz),
            (SECOND, second), (THIRD, second * inverse), (SMALL, 0.05 * h),
            (SOUND, SOUND_UNIT * jnp.sqrt(ADIABATIC * (ADIABATIC - 1.0) * e)),
            (HEAT, (ADIABATIC - 1.0) * e),
        ):
            targets[at, k] = value

    for i in range(planes - 1):
        compact(i)
        blocks[i].wait_recv()
        choose(i + 1, exports_s, land[i], outbox)
        if (i + 2) % BATCH == 0:
            send_across(
                i + 2 - BATCH, planes, outbox, table, across_sems.at[0], across_sems.at[1]
            )
    compact(planes - 1)
    keep_own(planes, cells, outbox, table)
    for copy in regionals:
        copy.wait()
    for copy in blocks:
        copy.wait_send()
    drain(planes, outbox, table, across_sems.at[0], across_sems.at[1])


def offsets_of(table, plan):
    size = table.shape[0]
    ones = jnp.ones((8, CAP), F32)
    lane = lax.broadcasted_iota(jnp.int32, (8, CAP), 1)
    row = lax.broadcasted_iota(jnp.int32, (CAP, CAP), 0)
    col = lax.broadcasted_iota(jnp.int32, (CAP, CAP), 1)
    named = jnp.where(lane < NB, plan[...], -1)
    held = []
    for start in range(0, size, CAP):
        stop = min(start + CAP, size)
        live = jnp.where(table[start:stop, 3, :] > 0.0, 1.0, 0.0)
        if stop - start < CAP:
            live = jnp.concatenate([live, jnp.zeros((CAP - (stop - start), CAP), F32)], axis=0)
        held.append(
            lax.dot_general(ones, live, (((1,), (1,)), ((), ())), preferred_element_type=F32)
        )
    lines = []
    for k in range(C_DEV):
        line = jnp.zeros((8, CAP), F32)
        for i, counts in enumerate(held):
            same = jnp.where(named[k : k + 1] == row + i * CAP, 1.0, 0.0)
            line += jnp.dot(counts, same, preferred_element_type=F32)
        lines.append(line[0:1])
    before = jnp.where(row < col, 1.0, 0.0)
    return jnp.dot(jnp.concatenate(lines, axis=0), before, preferred_element_type=F32)


def moving_kernel(
    regions, planes, exports, energy, density, table_one, plan, derived, offsets,
    table, cells, land, outbox, region_sems, along_sems, across_sems,
):
    wait_for_all = greet(regions, planes)
    for k in range(C_DEV):
        heat = (ADIABATIC * (ADIABATIC - 1.0)) * energy[k : k + 1]
        cells[k, 0:1] = SOUND_UNIT * jnp.sqrt(heat)
        cells[k, 1:2] = DENSITY_UNIT * density[k : k + 1]
    wait_for_all()
    regionals = region_copies(regions, cells, table, region_sems)
    blocks = [
        send_along(planes, ahead, cells, land.at[i], along_sems.at[0], along_sems.at[1])
        for i, ahead in enumerate(ORDER)
    ]
    for copy in blocks + list(regionals):
        copy.start()
    choose(0, exports, cells, outbox)

    def prepare(s, carry):
        h, m = table_one[s, 4:5], table_one[s, 3:4]
        inverse = 1.0 / h
        second = inverse * inverse
        derived[s, 0:1] = second
        derived[s, 1:2] = second * inverse
        derived[s, 2:3] = 0.05 * h
        derived[s, 3:4] = m * (1.5 / math.pi)
        derived[s, 7:8] = m
        return carry

    lax.fori_loop(0, table.shape[0], prepare, 0, unroll=6)
    offsets[...] = offsets_of(table_one, plan).astype(jnp.int32)
    pltpu.make_async_copy(land, land, along_sems.at[1]).wait()
    for i in range(planes - 1):
        choose(i + 1, exports, land.at[i], outbox)
        if (i + 2) % BATCH == 0:
            send_across(
                i + 2 - BATCH, planes, outbox, table, across_sems.at[0], across_sems.at[1]
            )
    keep_own(planes, cells, outbox, table)
    for copy in regionals:
        copy.wait()
    pltpu.make_async_copy(land, land, along_sems.at[0]).wait()
    drain(planes, outbox, table, across_sems.at[0], across_sems.at[1])

    def complete(s, carry):
        sound, thin = table[s, 0:1], table[s, 1:2]
        derived[s, 4:5] = (4.0 / ADIABATIC) * (sound * sound) / thin
        derived[s, 5:7] = table[s]
        return carry

    lax.fori_loop(0, table.shape[0], complete, 0, unroll=6)


def fill_shifts(shifts):
    sub = lax.broadcasted_iota(jnp.int32, (8, CAP), 0)
    for s in range(NB):
        offset = (s // 9 - 1, s // 3 % 3 - 1, s % 3 - 1)
        shifts[s] = jnp.where(
            sub == 0, float(offset[0]),
            jnp.where(sub == 1, float(offset[1]), jnp.where(sub == 2, float(offset[2]), 0.0)),
        )


def pack(plan, offsets, k, blocks_of, deads, packed):
    lane = lax.broadcasted_iota(jnp.int32, (8, CAP), 1)
    current = deads
    for n in range(NB):
        at, end = offsets[k, n], offsets[k, n + 1]
        row, first = lax.shift_right_logical(at, 7), lax.bitwise_and(at, CAP - 1)
        kept = lane < first
        spilled = lax.shift_right_logical(end, 7) > row
        rolled = [pltpu.roll(block, first, 1) for block in blocks_of(plan[k, n], n)]
        current = [jnp.where(kept, old, new) for old, new in zip(current, rolled)]
        for ref, value in zip(packed, current):
            ref[row] = value
        current = [jnp.where(spilled, new, old) for old, new in zip(current, rolled)]
    at = offsets[k, NB]
    row, first = lax.shift_right_logical(at, 7), lax.bitwise_and(at, CAP - 1)
    for ref, value, dead in zip(packed, current, deads):
        ref[row] = jnp.where(lane < first, value, dead)
        for i in range(1, 8):
            ref[row + i] = dead
    return lax.shift_right_logical(at + CAP - 1, 7)


def by_size(rows, run):
    low = 0
    for size in SIZES:
        pl.when(jnp.logical_and(rows > low, rows <= size))(functools.partial(run, size))
        low = size


def density_kernel(
    plan, table, targets, rank, density_old,
    density, density_too, own,
    shifts, near, total,
):
    fill_shifts(shifts)
    sub = lax.broadcasted_iota(jnp.int32, (GROUP, CAP), 0)
    cube = 4.0 ** (-1.0 / 3.0)

    def cell(k, carry):
        for n in range(NB):
            near[n] = table[plan[k, n]] + shifts[plan[k, SHIFT_AT + n]]
        ranks = rank[pl.ds(k, 1), :]
        total[...] = jnp.zeros((GROUP, CAP), F32)
        groups = plan[k, GROUP_AT]

        def setup(g):
            at = pl.multiple_of(jnp.minimum(g, CAP // GROUP - 1) * GROUP, GROUP)
            return tuple(targets[f, k, pl.ds(at, GROUP), :] for f in (X, Y, Z, INVERSE))

        def finish(g, partial, norm):
            found = jnp.sum(partial, axis=1, keepdims=True) * norm
            at = pl.multiple_of(jnp.maximum(g, 0) * GROUP, GROUP)
            own[0, k, pl.ds(at, GROUP), :] = targets[HEAT, k, pl.ds(at, GROUP), :] / found
            own[1, k, pl.ds(at, GROUP), :] = jnp.broadcast_to(found, (GROUP, CAP)) * DENSITY_UNIT
            here = ranks == (sub + g * GROUP).astype(F32)
            total[...] += jnp.where(here, found, 0.0)

        def run(size):
            def group(g, carry):
                (x, y, z, inverse), partial, norm = carry
                finish(g - 1, partial, norm)
                following = setup(g + 1)
                scaled = cube * inverse
                partial = jnp.zeros((GROUP, CAP), F32)
                for n in range(size):
                    dx, dy, dz = x - near[n, 0:1], y - near[n, 1:2], z - near[n, 2:3]
                    square = jnp.maximum(dx * dx + dy * dy + dz * dz, TINY)
                    radius = square * lax.rsqrt(square)
                    outer = jnp.maximum(2.0 * cube - radius * scaled, 0.0)
                    inner = jnp.maximum(1.0 - radius * inverse, 0.0)
                    value = outer * outer * outer - inner * inner * inner
                    partial += near[n, 3:4] * value
                return following, partial, inverse * inverse * inverse * (1.0 / math.pi)

            none = jnp.zeros((GROUP, CAP), F32)
            _, partial, norm = lax.fori_loop(0, groups, group, (setup(0), none, none))
            finish(groups - 1, partial, norm)

        run(NB)
        summed = jnp.sum(total[...], axis=0, keepdims=True)
        mine = pl.ds(k, 1)
        found = jnp.where(ranks >= 0.0, summed, density_old[mine, :])
        density[mine, :] = found
        density_too[mine, :] = found
        return carry

    lax.fori_loop(0, C_DEV, cell, 0)


def force_kernel(
    plan, offsets, table, derived, targets, own, rank, velocity, time_bin,
    acceleration, kicked, shifts, near, more, total,
):
    sub = lax.broadcasted_iota(jnp.int32, (GROUP, CAP), 0)

    fill_shifts(shifts)
    deads = [table[0], jnp.where(sub == 3, 0.0, derived[0])]

    def cell(k, carry):
        rows = pack(
            plan, offsets, k,
            lambda s, n: (table[s] + shifts[plan[k, SHIFT_AT + n]], derived[s]),
            deads, (near, more),
        )
        ranks = rank[pl.ds(k, 1), :]
        total[...] = jnp.zeros((3, GROUP, CAP), F32)
        groups = plan[k, GROUP_AT]

        def setup(g):
            at = pl.multiple_of(jnp.minimum(g, CAP // GROUP - 1) * GROUP, GROUP)
            columns = (X, Y, Z, VX, VY, VZ, SECOND, THIRD, SMALL, SOUND)
            return tuple(targets[f, k, pl.ds(at, GROUP), :] for f in columns) + tuple(
                own[f, k, pl.ds(at, GROUP), :] for f in range(2)
            )

        def finish(g, parts):
            here = ranks == (sub + g * GROUP).astype(F32)
            for i in range(3):
                total[i] += jnp.where(here, jnp.sum(parts[i], axis=1, keepdims=True), 0.0)

        def run(size):
            def group(g, carry):
                (x, y, z, vx, vy, vz, second, third, small, sound, press, thin), parts = carry
                finish(g - 1, parts)
                following = setup(g + 1)
                ax = ay = az = jnp.zeros((GROUP, CAP), F32)
                for n in range(size):
                    dx, dy, dz = x - near[n, 0:1], y - near[n, 1:2], z - near[n, 2:3]
                    square = jnp.maximum(dx * dx + dy * dy + dz * dz, TINY)
                    over = lax.rsqrt(square)
                    radius = square * over
                    reach = radius * third
                    outer = jnp.maximum(second - 0.5 * reach, 0.0)
                    inner = jnp.maximum(second - reach, 0.0)
                    slope = outer * outer - inner * inner
                    second_j = more[n, 0:1]
                    reach = radius * more[n, 1:2]
                    outer = jnp.maximum(second_j - 0.5 * reach, 0.0)
                    inner = jnp.maximum(second_j - reach, 0.0)
                    slope += outer * outer - inner * inner
                    approach = (
                        (vx - near[n, 5:6]) * dx
                        + (vy - near[n, 6:7]) * dy
                        + (vz - near[n, 7:8]) * dz
                    )
                    mean = small + more[n, 2:3]
                    mu = mean * jnp.minimum(approach, 0.0) * (1.0 / (square + mean * mean))
                    viscous = mu * (mu - (sound + more[n, 5:6])) * (1.0 / (thin + more[n, 6:7]))
                    weight = more[n, 3:4] * (press + more[n, 4:5] + viscous) * (slope * over)
                    ax += weight * dx
                    ay += weight * dy
                    az += weight * dz
                return following, (ax, ay, az)

            none = jnp.zeros((GROUP, CAP), F32)
            _, parts = lax.fori_loop(0, groups, group, (setup(0), (none, none, none)))
            finish(groups - 1, parts)

        by_size(rows, run)
        mine = pl.ds(k, 1)
        step = STEP_MAX * jnp.exp2(-time_bin[mine, :].astype(F32))
        for i in range(3):
            found = jnp.sum(total[i], axis=0, keepdims=True)
            acceleration[i, mine, :] = found
            kicked[i, mine, :] = velocity[i, mine, :] + found * step
        return carry

    lax.fori_loop(0, C_DEV, cell, 0)


def shards(
    regions, planes,
    position, velocity, smoothing, particle_mass, energy, density_old, cell_count, active,
    time_bin, pair_source, pair_shift, export,
):
    size = C_DEV + 2 * planes * PLANE + 2
    vmem = pl.BlockSpec(memory_space=pltpu.VMEM)
    smem = pl.BlockSpec(memory_space=pltpu.SMEM)
    hbm = pl.BlockSpec(memory_space=pltpu.HBM)
    dma = pltpu.SemaphoreType.DMA

    def shape(*dims, dtype=F32):
        return jax.ShapeDtypeStruct(dims, dtype)

    def ints(*dims):
        return pltpu.VMEM(dims, jnp.int32)

    def floats(*dims):
        return pltpu.VMEM(dims, F32)

    limit = 32 << 20
    table, targets, rank, plan, exports, energy, density_old = pl.pallas_call(
        functools.partial(static_kernel, regions, planes),
        out_shape=[
            shape(size, 8, CAP), shape(TARGET, C_DEV, CAP, CAP), shape(C_DEV, CAP),
            shape(C_DEV, CAP, dtype=jnp.int32),
            shape(planes, 2, planes * PLANE, dtype=jnp.int32), shape(C_DEV, CAP), shape(C_DEV, CAP),
        ],
        in_specs=[hbm] * 11,
        out_specs=[vmem] * 7,
        scratch_shapes=[
            floats(3, C_DEV, CAP), floats(3, C_DEV, CAP), floats(C_DEV, CAP), floats(C_DEV, CAP),
            ints(C_DEV, CAP), pltpu.SMEM((C_DEV,), jnp.int32),
            ints(C_DEV, NB), ints(C_DEV, NB),
            floats(C_DEV, 8, CAP), pltpu.SMEM((planes, 2, planes * PLANE), jnp.int32),
            floats(PLANE, 2 * planes, 8, CAP),
            *[floats(C_DEV, 8, CAP) for _ in range(planes - 1)],
            dma((11,)), dma((4,)), dma((2,)), dma((planes - 1,)), dma((planes - 1,)), dma((2,)),
            dma,
        ],
        compiler_params=pltpu.CompilerParams(
            collective_id=0, has_side_effects=True, vmem_limit_bytes=limit
        ),
    )(
        *(
            pltpu.with_memory_space_constraint(x, pltpu.HBM)
            for x in (
                position, velocity, smoothing, particle_mass, energy, active, cell_count, export.T,
                pair_source, pair_shift, density_old,
            )
        )
    )
    density, density_too, own = pl.pallas_call(
        density_kernel,
        out_shape=[shape(C_DEV, CAP), shape(C_DEV, CAP), shape(2, C_DEV, CAP, CAP)],
        in_specs=[smem] + [vmem] * 4,
        out_specs=[vmem] * 3,
        scratch_shapes=[floats(NB, 8, CAP), floats(NB, 8, CAP), floats(GROUP, CAP)],
        compiler_params=pltpu.CompilerParams(vmem_limit_bytes=limit),
    )(plan, table, targets, rank, density_old)
    derived, offsets = pl.pallas_call(
        functools.partial(moving_kernel, regions, planes),
        out_shape=[shape(size, 8, CAP), shape(C_DEV, CAP, dtype=jnp.int32)],
        in_specs=[smem] + [vmem] * 4,
        out_specs=[vmem] * 2,
        scratch_shapes=[
            floats(size, 2, CAP), floats(C_DEV, 2, CAP), floats(planes - 1, C_DEV, 2, CAP),
            floats(PLANE, 2 * planes, 2, CAP), dma((4,)), dma((2,)), dma((2,)),
        ],
        compiler_params=pltpu.CompilerParams(
            collective_id=1, has_side_effects=True, vmem_limit_bytes=limit
        ),
    )(exports, energy, density_too, table, plan)
    acceleration, kicked = pl.pallas_call(
        force_kernel,
        out_shape=[shape(3, C_DEV, CAP), shape(3, C_DEV, CAP)],
        in_specs=[smem] * 2 + [vmem] * 7,
        out_specs=[vmem, vmem],
        scratch_shapes=[
            floats(NB, 8, CAP), floats(ROWS, 8, CAP), floats(ROWS, 8, CAP),
            floats(3, GROUP, CAP),
        ],
        compiler_params=pltpu.CompilerParams(vmem_limit_bytes=limit),
    )(plan, offsets, table, derived, targets, own, rank, velocity, time_bin)
    return density, acceleration, kicked


def solution(mesh):
    both = ("region", "cell")
    flat, wide_rows = P(both, None), P(None, both, None)
    return jax.shard_map(
        functools.partial(shards, mesh.shape["region"], mesh.shape["cell"] // PLANE),
        mesh=mesh,
        in_specs=(
            wide_rows, wide_rows, flat, flat, flat, flat, P(both), flat, flat, flat, flat, flat,
        ),
        out_specs=(flat, wide_rows, wide_rows),
        check_vma=False,
    )
```

```python
import functools
import math

import jax
import jax.numpy as jnp
from jax import lax
from jax.experimental import pallas as pl
from jax.experimental.pallas import tpu as pltpu
from jax.sharding import PartitionSpec as P

MESH = pl.DeviceIdType.MESH
C_DEV = 8
CAP = 128
NB = 27
GROUP = 8
PLANE = 8
ORDER = (1, 7, 4, 2, 6, 3, 5)
EARLY = 6
BATCH = 2
ADIABATIC = 5.0 / 3.0
STEP_MAX = 0.2
TINY = 1e-30
F32 = jnp.float32
SHIFT_AT, GROUP_AT = 32, 64
SIZES = (8, 12, 15, 16, 17, 18, 19, 20, 22, 24, 27)
ROWS = NB + 8
X, Y, Z, INVERSE, VX, VY, VZ, SECOND, THIRD, SMALL, SOUND, HEAT = range(12)
TARGET = 12
SOUND_UNIT = 0.025
DENSITY_UNIT = 1.0 / 400.0


def place():
    r, c = lax.axis_index("region"), lax.axis_index("cell")
    return r, lax.div(c, PLANE), lax.rem(c, PLANE)


def along(z, u, planes, ahead):
    return lax.rem(z + ahead, planes) * PLANE + u


def across(z, u, ahead):
    return z * PLANE + lax.rem(u + ahead, PLANE)


def greet(regions, planes):
    r, z, u = place()
    barrier = pltpu.get_barrier_semaphore()
    for ahead in range(1, planes):
        pl.semaphore_signal(
            barrier, inc=1, device_id=(r, along(z, u, planes, ahead)), device_id_type=MESH
        )
    for ahead in range(1, PLANE):
        pl.semaphore_signal(
            barrier, inc=1, device_id=(r, across(z, u, ahead)), device_id_type=MESH
        )
    for ahead in (1, regions - 1):
        pl.semaphore_signal(
            barrier, inc=1, device_id=(lax.rem(r + ahead, regions), z * PLANE + u),
            device_id_type=MESH,
        )
    return lambda: pl.semaphore_wait(barrier, planes + PLANE)


def region_copies(regions, cells, table, sems, first):
    r, z, u = place()
    size = table.shape[0]
    up = pltpu.make_async_remote_copy(
        src_ref=cells.at[pl.ds(C_DEV - 1, 1)],
        dst_ref=table.at[pl.ds(size - 2, 1)],
        send_sem=sems.at[first + 0],
        recv_sem=sems.at[first + 1],
        device_id=(lax.rem(r + 1, regions), z * PLANE + u),
        device_id_type=MESH,
    )
    down = pltpu.make_async_remote_copy(
        src_ref=cells.at[pl.ds(0, 1)],
        dst_ref=table.at[pl.ds(size - 1, 1)],
        send_sem=sems.at[first + 2],
        recv_sem=sems.at[first + 3],
        device_id=(lax.rem(r + regions - 1, regions), z * PLANE + u),
        device_id_type=MESH,
    )
    return up, down


def send_along(planes, ahead, source, target, send_sem, recv_sem):
    r, z, u = place()
    return pltpu.make_async_remote_copy(
        src_ref=source, dst_ref=target, send_sem=send_sem, recv_sem=recv_sem,
        device_id=(r, along(z, u, planes, ahead)), device_id_type=MESH,
    )


def send_across(first, slots, planes, outbox, table, send_sem, recv_sem):
    r, z, u = place()
    rows = 2 * slots

    def send(ahead, carry):
        to = lax.rem(u + ahead, PLANE)
        pltpu.make_async_remote_copy(
            src_ref=outbox.at[to, pl.ds(2 * first, rows)],
            dst_ref=table.at[pl.ds(C_DEV + 2 * planes * u + 2 * first, rows)],
            send_sem=send_sem, recv_sem=recv_sem,
            device_id=(r, z * PLANE + to), device_id_type=MESH,
        ).start()
        return carry

    lax.fori_loop(1, PLANE, send, 0)


def choose(slot, export, cells, outbox):
    r, z, u = place()

    def fill(to, carry):
        for q in range(2):
            outbox[to, 2 * slot + q] = cells[export[slot, q, z * PLANE + to]]
        return carry

    lax.fori_loop(0, PLANE, fill, 0, unroll=True)


def keep_own(planes, cells, outbox, table):
    r, z, u = place()
    for k in range(C_DEV):
        table[k] = cells[k]
    for i in range(2 * planes):
        table[C_DEV + 2 * planes * u + i] = outbox[u, i]


def drain(planes, outbox, table, send_sem, recv_sem):
    sent = outbox.at[pl.ds(0, PLANE - 1)]
    pltpu.make_async_copy(sent, sent, send_sem).wait()
    landed = table.at[pl.ds(0, 2 * planes * (PLANE - 1))]
    pltpu.make_async_copy(landed, landed, recv_sem).wait()


def static_kernel(
    regions, planes,
    position, velocity, smoothing, mass, energy, active, count, export, source, shift, old,
    table, sounds, targets, rank, plan, exports, old_v,
    energy_v, position_v, velocity_v, smoothing_v, mass_v, active_v, count_s, source_v, shift_v,
    cells, exports_s, outbox, *rest,
):
    land, (
        sound_land, sound_outbox,
        fetch_sems, region_sems, export_sems, along_send, along_recv, across_sems, own_sem,
        sound_sems,
    ) = rest[: planes - 1], rest[planes - 1 :]
    wait_for_all = greet(regions, planes)
    fetches = [
        pltpu.make_async_copy(a, b, fetch_sems.at[i])
        for i, (a, b) in enumerate((
            (position, position_v), (smoothing, smoothing_v), (mass, mass_v), (count, count_s),
            (velocity, velocity_v), (export, exports.at[0]), (energy, energy_v),
            (active, active_v), (source, source_v), (shift, shift_v), (old, old_v),
        ))
    ]
    for fetch in fetches:
        fetch.start()
    for fetch in fetches:
        fetch.wait()
    slot = lax.broadcasted_iota(jnp.int32, (1, CAP), 1)
    for k in range(C_DEV):
        for i in range(3):
            cells[k, i : i + 1] = position_v[i, k : k + 1]
            cells[k, 5 + i : 6 + i] = velocity_v[i, k : k + 1]
        cells[k, 3:4] = jnp.where(slot < count_s[k], mass_v[k : k + 1], 0.0)
        cells[k, 4:5] = smoothing_v[k : k + 1]
        heat = (ADIABATIC * (ADIABATIC - 1.0)) * energy_v[k : k + 1]
        sound_land[0, k] = SOUND_UNIT * jnp.sqrt(heat)
    wait_for_all()
    regionals = region_copies(regions, cells, table, region_sems, 0) + region_copies(
        regions, sound_land.at[0], sounds, region_sems, 4
    )
    calls = [
        send_along(
            planes, ahead, sound_land.at[0], sound_land.at[i + 1], sound_sems.at[0],
            sound_sems.at[1],
        )
        for i, ahead in enumerate(ORDER)
    ]
    lists = [
        send_along(
            planes, ahead, exports.at[0], exports.at[i + 1], export_sems.at[0], export_sems.at[1]
        )
        for i, ahead in enumerate(ORDER)
    ]
    blocks = [
        send_along(planes, ahead, cells, land[i], along_send.at[i], along_recv.at[i])
        for i, ahead in enumerate(ORDER)
    ]
    for copy in lists + calls + blocks[:2] + list(regionals) + blocks[2:]:
        copy.start()

    live = active_v[...] > 0
    row = lax.broadcasted_iota(jnp.int32, (CAP, CAP), 0)
    col = lax.broadcasted_iota(jnp.int32, (CAP, CAP), 1)
    upper = jnp.where(row <= col, 1.0, 0.0)
    ordinal = jnp.dot(jnp.where(live, 1.0, 0.0), upper, preferred_element_type=F32)
    where_to = jnp.where(live, ordinal - 1.0, -1000.0)
    rank[...] = where_to
    groups = (jnp.sum(active_v[...], axis=1, keepdims=True) + (GROUP - 1)) // GROUP
    r, z, u = place()
    named = source_v[...]
    other = named - C_DEV
    behind = jnp.bitwise_and(z + planes - jnp.right_shift(other, 4), planes - 1)
    slot_of = jnp.zeros_like(behind)
    for i, ahead in enumerate(ORDER):
        slot_of = jnp.where(behind == ahead, i + 1, slot_of)
    peer = jnp.bitwise_and(jnp.right_shift(other, 1), PLANE - 1)
    moved = C_DEV + 2 * planes * peer + 2 * slot_of + jnp.bitwise_and(other, 1)
    inside = jnp.logical_and(named >= C_DEV, named < C_DEV + 2 * planes * PLANE)
    plan[:, 0:NB] = jnp.where(inside, moved, named)
    plan[:, SHIFT_AT : SHIFT_AT + NB] = shift_v[...]
    plan[:, GROUP_AT : GROUP_AT + 1] = groups

    sub = lax.broadcasted_iota(jnp.int32, (8, CAP), 0)

    def compact(k):
        fields = jnp.where(sub == 3, energy_v[k : k + 1], cells[k])
        picked = jnp.where(where_to[k : k + 1] == row.astype(F32), 1.0, 0.0)
        found = lax.dot_general(
            picked, fields, (((1,), (1,)), ((), ())),
            precision=lax.Precision.HIGHEST, preferred_element_type=F32,
        )
        x, y, z, e, h, vx, vy, vz = (
            jnp.broadcast_to(found[:, f : f + 1], (CAP, CAP)) for f in range(8)
        )
        inverse = 1.0 / h
        second = inverse * inverse
        for at, value in (
            (X, x), (Y, y), (Z, z), (INVERSE, inverse), (VX, vx), (VY, vy), (VZ, vz),
            (SECOND, second), (THIRD, second * inverse), (SMALL, 0.05 * h),
            (SOUND, SOUND_UNIT * jnp.sqrt(ADIABATIC * (ADIABATIC - 1.0) * e)),
            (HEAT, (ADIABATIC - 1.0) * e),
        ):
            targets[at, k] = value

    for k in range(EARLY):
        compact(k)
    drained = exports.at[pl.ds(1, planes - 1)]
    pltpu.make_async_copy(drained, drained, export_sems.at[1]).wait()
    pltpu.make_async_copy(drained, drained, export_sems.at[0]).wait()
    to_scalar = pltpu.make_async_copy(exports, exports_s, own_sem)
    to_scalar.start()
    to_scalar.wait()
    heard = sound_land.at[pl.ds(1, planes - 1)]
    pltpu.make_async_copy(heard, heard, sound_sems.at[1]).wait()
    for slot in range(planes):
        choose(slot, exports_s, sound_land.at[slot], sound_outbox)
    send_across(0, planes, planes, sound_outbox, sounds, sound_sems.at[2], sound_sems.at[3])
    choose(0, exports_s, cells, outbox)
    for i in range(planes - 1):
        if i + EARLY < C_DEV:
            compact(i + EARLY)
        blocks[i].wait_recv()
        choose(i + 1, exports_s, land[i], outbox)
        if (i + 2) % BATCH == 0:
            send_across(
                i + 2 - BATCH, BATCH, planes, outbox, table, across_sems.at[0], across_sems.at[1]
            )
    keep_own(planes, cells, outbox, table)
    keep_own(planes, sound_land.at[0], sound_outbox, sounds)
    for copy in regionals:
        copy.wait()
    for copy in blocks:
        copy.wait_send()
    pltpu.make_async_copy(heard, heard, sound_sems.at[0]).wait()
    drain(planes, sound_outbox, sounds, sound_sems.at[2], sound_sems.at[3])
    drain(planes, outbox, table, across_sems.at[0], across_sems.at[1])


def offsets_of(table, plan):
    size = table.shape[0]
    ones = jnp.ones((8, CAP), F32)
    lane = lax.broadcasted_iota(jnp.int32, (8, CAP), 1)
    row = lax.broadcasted_iota(jnp.int32, (CAP, CAP), 0)
    col = lax.broadcasted_iota(jnp.int32, (CAP, CAP), 1)
    named = jnp.where(lane < NB, plan[...], -1)
    held = []
    for start in range(0, size, CAP):
        stop = min(start + CAP, size)
        live = jnp.where(table[start:stop, 3, :] > 0.0, 1.0, 0.0)
        if stop - start < CAP:
            live = jnp.concatenate([live, jnp.zeros((CAP - (stop - start), CAP), F32)], axis=0)
        held.append(
            lax.dot_general(ones, live, (((1,), (1,)), ((), ())), preferred_element_type=F32)
        )
    lines = []
    for k in range(C_DEV):
        line = jnp.zeros((8, CAP), F32)
        for i, counts in enumerate(held):
            same = jnp.where(named[k : k + 1] == row + i * CAP, 1.0, 0.0)
            line += jnp.dot(counts, same, preferred_element_type=F32)
        lines.append(line[0:1])
    before = jnp.where(row < col, 1.0, 0.0)
    return jnp.dot(jnp.concatenate(lines, axis=0), before, preferred_element_type=F32)


def by_distance(planes):
    others = [(i, j) for i in range(planes) for j in range(PLANE) if (i, j) != (0, 0)]

    def hops(other):
        return min(other[0], planes - other[0]) + min(other[1] // 2, (PLANE - other[1] + 1) // 2)

    return sorted(others, key=lambda other: -hops(other))


def moving_kernel(
    regions, planes, exports, density, sources, sounds, plan, derived, offsets,
    table, cells, outbox, region_sems, sems,
):
    r, z, u = place()
    others = by_distance(planes)
    barrier = pltpu.get_barrier_semaphore()

    def at(other):
        return lax.rem(z + other[0], planes) * PLANE + lax.rem(u + other[1], PLANE)

    for other in others:
        pl.semaphore_signal(barrier, inc=1, device_id=(r, at(other)), device_id_type=MESH)
    for ahead in (1, regions - 1):
        pl.semaphore_signal(
            barrier, inc=1, device_id=(lax.rem(r + ahead, regions), z * PLANE + u),
            device_id_type=MESH,
        )
    for k in range(C_DEV):
        cells[k] = DENSITY_UNIT * density[k : k + 1]
    for i, other in enumerate(others):
        for q in range(2):
            outbox[i, q] = cells[exports[0, q, at(other)]]
    pl.semaphore_wait(barrier, planes * PLANE + 1)
    for i, other in enumerate(others):
        slot = ((0,) + ORDER).index(other[0])
        pltpu.make_async_remote_copy(
            src_ref=outbox.at[i],
            dst_ref=table.at[pl.ds(C_DEV + 2 * planes * u + 2 * slot, 2)],
            send_sem=sems.at[0], recv_sem=sems.at[1],
            device_id=(r, at(other)), device_id_type=MESH,
        ).start()
    regionals = region_copies(regions, cells, table, region_sems, 0)
    for copy in regionals:
        copy.start()
    for k in range(C_DEV):
        table[k] = cells[k]
    for q in range(2):
        table[C_DEV + 2 * planes * u + q] = cells[exports[0, q, z * PLANE + u]]

    def prepare(s, carry):
        h, m = sources[s, 4:5], sources[s, 3:4]
        inverse = 1.0 / h
        second = inverse * inverse
        derived[s, 0:1] = second
        derived[s, 1:2] = second * inverse
        derived[s, 2:3] = 0.05 * h
        derived[s, 3:4] = m * (1.5 / math.pi)
        sound = sounds[s]
        derived[s, 5:6] = sound
        derived[s, 7:8] = (4.0 / ADIABATIC) * (sound * sound)
        return carry

    lax.fori_loop(0, table.shape[0], prepare, 0, unroll=6)
    offsets[...] = offsets_of(sources, plan).astype(jnp.int32)
    for copy in regionals:
        copy.wait()
    pltpu.make_async_copy(outbox, outbox, sems.at[0]).wait()
    landed = table.at[pl.ds(0, 2 * len(others))]
    pltpu.make_async_copy(landed, landed, sems.at[1]).wait()

    def complete(s, carry):
        thin = table[s]
        derived[s, 4:5] = derived[s, 7:8] / thin
        derived[s, 6:7] = thin
        return carry

    lax.fori_loop(0, table.shape[0], complete, 0, unroll=6)


def fill_shifts(shifts):
    sub = lax.broadcasted_iota(jnp.int32, (8, CAP), 0)
    for s in range(NB):
        offset = (s // 9 - 1, s // 3 % 3 - 1, s % 3 - 1)
        shifts[s] = jnp.where(
            sub == 0, float(offset[0]),
            jnp.where(sub == 1, float(offset[1]), jnp.where(sub == 2, float(offset[2]), 0.0)),
        )


def pack(plan, offsets, k, blocks_of, deads, packed):
    lane = lax.broadcasted_iota(jnp.int32, (8, CAP), 1)
    current = deads
    for n in range(NB):
        at, end = offsets[k, n], offsets[k, n + 1]
        row, first = lax.shift_right_logical(at, 7), lax.bitwise_and(at, CAP - 1)
        kept = lane < first
        spilled = lax.shift_right_logical(end, 7) > row
        rolled = [pltpu.roll(block, first, 1) for block in blocks_of(plan[k, n], n)]
        current = [jnp.where(kept, old, new) for old, new in zip(current, rolled)]
        for ref, value in zip(packed, current):
            ref[row] = value
        current = [jnp.where(spilled, new, old) for old, new in zip(current, rolled)]
    at = offsets[k, NB]
    row, first = lax.shift_right_logical(at, 7), lax.bitwise_and(at, CAP - 1)
    for ref, value, dead in zip(packed, current, deads):
        ref[row] = jnp.where(lane < first, value, dead)
        for i in range(1, 8):
            ref[row + i] = dead
    return lax.shift_right_logical(at + CAP - 1, 7)


def by_size(rows, run):
    low = 0
    for size in SIZES:
        pl.when(jnp.logical_and(rows > low, rows <= size))(functools.partial(run, size))
        low = size


def density_kernel(
    plan, table, targets, rank, density_old,
    density, density_too, own,
    shifts, near, total,
):
    fill_shifts(shifts)
    sub = lax.broadcasted_iota(jnp.int32, (GROUP, CAP), 0)
    cube = 4.0 ** (-1.0 / 3.0)

    def cell(k, carry):
        for n in range(NB):
            near[n] = table[plan[k, n]] + shifts[plan[k, SHIFT_AT + n]]
        ranks = rank[pl.ds(k, 1), :]
        total[...] = jnp.zeros((GROUP, CAP), F32)
        groups = plan[k, GROUP_AT]

        def setup(g):
            at = pl.multiple_of(jnp.minimum(g, CAP // GROUP - 1) * GROUP, GROUP)
            return tuple(targets[f, k, pl.ds(at, GROUP), :] for f in (X, Y, Z, INVERSE))

        def finish(g, partial, norm):
            found = jnp.sum(partial, axis=1, keepdims=True) * norm
            at = pl.multiple_of(jnp.maximum(g, 0) * GROUP, GROUP)
            own[0, k, pl.ds(at, GROUP), :] = targets[HEAT, k, pl.ds(at, GROUP), :] / found
            own[1, k, pl.ds(at, GROUP), :] = jnp.broadcast_to(found, (GROUP, CAP)) * DENSITY_UNIT
            here = ranks == (sub + g * GROUP).astype(F32)
            total[...] += jnp.where(here, found, 0.0)

        def run(size):
            def group(g, carry):
                (x, y, z, inverse), partial, norm = carry
                finish(g - 1, partial, norm)
                following = setup(g + 1)
                scaled = cube * inverse
                partial = jnp.zeros((GROUP, CAP), F32)
                for n in range(size):
                    dx, dy, dz = x - near[n, 0:1], y - near[n, 1:2], z - near[n, 2:3]
                    square = jnp.maximum(dx * dx + dy * dy + dz * dz, TINY)
                    radius = square * lax.rsqrt(square)
                    outer = jnp.maximum(2.0 * cube - radius * scaled, 0.0)
                    inner = jnp.maximum(1.0 - radius * inverse, 0.0)
                    value = outer * outer * outer - inner * inner * inner
                    partial += near[n, 3:4] * value
                return following, partial, inverse * inverse * inverse * (1.0 / math.pi)

            none = jnp.zeros((GROUP, CAP), F32)
            _, partial, norm = lax.fori_loop(0, groups, group, (setup(0), none, none))
            finish(groups - 1, partial, norm)

        run(NB)
        summed = jnp.sum(total[...], axis=0, keepdims=True)
        mine = pl.ds(k, 1)
        found = jnp.where(ranks >= 0.0, summed, density_old[mine, :])
        density[mine, :] = found
        density_too[mine, :] = found
        return carry

    lax.fori_loop(0, C_DEV, cell, 0)


def force_kernel(
    plan, offsets, table, derived, targets, own, rank, velocity, time_bin,
    acceleration, kicked, shifts, near, more, total,
):
    sub = lax.broadcasted_iota(jnp.int32, (GROUP, CAP), 0)

    fill_shifts(shifts)
    deads = [table[0], jnp.where(sub == 3, 0.0, derived[0])]

    def cell(k, carry):
        rows = pack(
            plan, offsets, k,
            lambda s, n: (table[s] + shifts[plan[k, SHIFT_AT + n]], derived[s]),
            deads, (near, more),
        )
        ranks = rank[pl.ds(k, 1), :]
        total[...] = jnp.zeros((3, GROUP, CAP), F32)
        groups = plan[k, GROUP_AT]

        def setup(g):
            at = pl.multiple_of(jnp.minimum(g, CAP // GROUP - 1) * GROUP, GROUP)
            columns = (X, Y, Z, VX, VY, VZ, SECOND, THIRD, SMALL, SOUND)
            return tuple(targets[f, k, pl.ds(at, GROUP), :] for f in columns) + tuple(
                own[f, k, pl.ds(at, GROUP), :] for f in range(2)
            )

        def finish(g, parts):
            here = ranks == (sub + g * GROUP).astype(F32)
            for i in range(3):
                total[i] += jnp.where(here, jnp.sum(parts[i], axis=1, keepdims=True), 0.0)

        def run(size):
            def group(g, carry):
                (x, y, z, vx, vy, vz, second, third, small, sound, press, thin), parts = carry
                finish(g - 1, parts)
                following = setup(g + 1)
                ax = ay = az = jnp.zeros((GROUP, CAP), F32)
                for n in range(size):
                    dx, dy, dz = x - near[n, 0:1], y - near[n, 1:2], z - near[n, 2:3]
                    square = jnp.maximum(dx * dx + dy * dy + dz * dz, TINY)
                    over = lax.rsqrt(square)
                    radius = square * over
                    reach = radius * third
                    outer = jnp.maximum(second - 0.5 * reach, 0.0)
                    inner = jnp.maximum(second - reach, 0.0)
                    slope = outer * outer - inner * inner
                    second_j = more[n, 0:1]
                    reach = radius * more[n, 1:2]
                    outer = jnp.maximum(second_j - 0.5 * reach, 0.0)
                    inner = jnp.maximum(second_j - reach, 0.0)
                    slope += outer * outer - inner * inner
                    approach = (
                        (vx - near[n, 5:6]) * dx
                        + (vy - near[n, 6:7]) * dy
                        + (vz - near[n, 7:8]) * dz
                    )
                    mean = small + more[n, 2:3]
                    mu = mean * jnp.minimum(approach, 0.0) * (1.0 / (square + mean * mean))
                    viscous = mu * (mu - (sound + more[n, 5:6])) * (1.0 / (thin + more[n, 6:7]))
                    weight = more[n, 3:4] * (press + more[n, 4:5] + viscous) * (slope * over)
                    ax += weight * dx
                    ay += weight * dy
                    az += weight * dz
                return following, (ax, ay, az)

            none = jnp.zeros((GROUP, CAP), F32)
            _, parts = lax.fori_loop(0, groups, group, (setup(0), (none, none, none)))
            finish(groups - 1, parts)

        by_size(rows, run)
        mine = pl.ds(k, 1)
        step = STEP_MAX * jnp.exp2(-time_bin[mine, :].astype(F32))
        for i in range(3):
            found = jnp.sum(total[i], axis=0, keepdims=True)
            acceleration[i, mine, :] = found
            kicked[i, mine, :] = velocity[i, mine, :] + found * step
        return carry

    lax.fori_loop(0, C_DEV, cell, 0)


def shards(
    regions, planes,
    position, velocity, smoothing, particle_mass, energy, density_old, cell_count, active,
    time_bin, pair_source, pair_shift, export,
):
    size = C_DEV + 2 * planes * PLANE + 2
    vmem = pl.BlockSpec(memory_space=pltpu.VMEM)
    smem = pl.BlockSpec(memory_space=pltpu.SMEM)
    hbm = pl.BlockSpec(memory_space=pltpu.HBM)
    dma = pltpu.SemaphoreType.DMA

    def shape(*dims, dtype=F32):
        return jax.ShapeDtypeStruct(dims, dtype)

    def ints(*dims):
        return pltpu.VMEM(dims, jnp.int32)

    def floats(*dims):
        return pltpu.VMEM(dims, F32)

    limit = 32 << 20
    table, sounds, targets, rank, plan, exports, density_old = pl.pallas_call(
        functools.partial(static_kernel, regions, planes),
        out_shape=[
            shape(size, 8, CAP), shape(size, 1, CAP), shape(TARGET, C_DEV, CAP, CAP),
            shape(C_DEV, CAP),
            shape(C_DEV, CAP, dtype=jnp.int32),
            shape(planes, 2, planes * PLANE, dtype=jnp.int32), shape(C_DEV, CAP),
        ],
        in_specs=[hbm] * 11,
        out_specs=[vmem] * 7,
        scratch_shapes=[
            floats(C_DEV, CAP), floats(3, C_DEV, CAP), floats(3, C_DEV, CAP), floats(C_DEV, CAP),
            floats(C_DEV, CAP), ints(C_DEV, CAP), pltpu.SMEM((C_DEV,), jnp.int32),
            ints(C_DEV, NB), ints(C_DEV, NB),
            floats(C_DEV, 8, CAP), pltpu.SMEM((planes, 2, planes * PLANE), jnp.int32),
            floats(PLANE, 2 * planes, 8, CAP),
            *[floats(C_DEV, 8, CAP) for _ in range(planes - 1)],
            floats(planes, C_DEV, 1, CAP), floats(PLANE, 2 * planes, 1, CAP),
            dma((11,)), dma((8,)), dma((2,)), dma((planes - 1,)), dma((planes - 1,)), dma((2,)),
            dma, dma((4,)),
        ],
        compiler_params=pltpu.CompilerParams(
            collective_id=0, has_side_effects=True, vmem_limit_bytes=limit
        ),
    )(
        *(
            pltpu.with_memory_space_constraint(x, pltpu.HBM)
            for x in (
                position, velocity, smoothing, particle_mass, energy, active, cell_count, export.T,
                pair_source, pair_shift, density_old,
            )
        )
    )
    density, density_too, own = pl.pallas_call(
        density_kernel,
        out_shape=[shape(C_DEV, CAP), shape(C_DEV, CAP), shape(2, C_DEV, CAP, CAP)],
        in_specs=[smem] + [vmem] * 4,
        out_specs=[vmem] * 3,
        scratch_shapes=[floats(NB, 8, CAP), floats(NB, 8, CAP), floats(GROUP, CAP)],
        compiler_params=pltpu.CompilerParams(vmem_limit_bytes=limit),
    )(plan, table, targets, rank, density_old)
    derived, offsets = pl.pallas_call(
        functools.partial(moving_kernel, regions, planes),
        out_shape=[shape(size, 8, CAP), shape(C_DEV, CAP, dtype=jnp.int32)],
        in_specs=[smem] + [vmem] * 4,
        out_specs=[vmem] * 2,
        scratch_shapes=[
            floats(size, 1, CAP), floats(C_DEV, 1, CAP),
            floats(planes * PLANE - 1, 2, 1, CAP), dma((4,)), dma((2,)),
        ],
        compiler_params=pltpu.CompilerParams(
            collective_id=1, has_side_effects=True, vmem_limit_bytes=limit
        ),
    )(exports, density_too, table, sounds, plan)
    acceleration, kicked = pl.pallas_call(
        force_kernel,
        out_shape=[shape(3, C_DEV, CAP), shape(3, C_DEV, CAP)],
        in_specs=[smem] * 2 + [vmem] * 7,
        out_specs=[vmem, vmem],
        scratch_shapes=[
            floats(NB, 8, CAP), floats(ROWS, 8, CAP), floats(ROWS, 8, CAP),
            floats(3, GROUP, CAP),
        ],
        compiler_params=pltpu.CompilerParams(vmem_limit_bytes=limit),
    )(plan, offsets, table, derived, targets, own, rank, velocity, time_bin)
    return density, acceleration, kicked


def solution(mesh):
    both = ("region", "cell")
    flat, wide_rows = P(both, None), P(None, both, None)
    return jax.shard_map(
        functools.partial(shards, mesh.shape["region"], mesh.shape["cell"] // PLANE),
        mesh=mesh,
        in_specs=(
            wide_rows, wide_rows, flat, flat, flat, flat, P(both), flat, flat, flat, flat, flat,
        ),
        out_specs=(flat, wide_rows, wide_rows),
        check_vma=False,
    )
```

```python
import functools
import math

import jax
import jax.numpy as jnp
from jax import lax
from jax.experimental import pallas as pl
from jax.experimental.pallas import tpu as pltpu
from jax.sharding import PartitionSpec as P

MESH = pl.DeviceIdType.MESH
C_DEV = 8
CAP = 128
NB = 27
GROUP = 8
PLANE = 8
ORDER = (1, 7, 4, 2, 6, 3, 5)
EARLY = 6
BATCH = 2
ADIABATIC = 5.0 / 3.0
STEP_MAX = 0.2
TINY = 1e-30
F32 = jnp.float32
SHIFT_AT, GROUP_AT = 32, 64
SIZES = (8, 12, 15, 16, 17, 18, 19, 20, 22, 24, 27)
ROWS = NB + 8
X, Y, Z, INVERSE, VX, VY, VZ, SECOND, THIRD, SMALL, SOUND, HEAT = range(12)
TARGET = 12
SOUND_UNIT = 0.025
DENSITY_UNIT = 1.0 / 400.0


def place():
    r, c = lax.axis_index("region"), lax.axis_index("cell")
    return r, lax.div(c, PLANE), lax.rem(c, PLANE)


def along(z, u, planes, ahead):
    return lax.rem(z + ahead, planes) * PLANE + u


def across(z, u, ahead):
    return z * PLANE + lax.rem(u + ahead, PLANE)


def greet(regions, planes):
    r, z, u = place()
    barrier = pltpu.get_barrier_semaphore()
    for ahead in range(1, planes):
        pl.semaphore_signal(
            barrier, inc=1, device_id=(r, along(z, u, planes, ahead)), device_id_type=MESH
        )
    for ahead in range(1, PLANE):
        pl.semaphore_signal(
            barrier, inc=1, device_id=(r, across(z, u, ahead)), device_id_type=MESH
        )
    for ahead in (1, regions - 1):
        pl.semaphore_signal(
            barrier, inc=1, device_id=(lax.rem(r + ahead, regions), z * PLANE + u),
            device_id_type=MESH,
        )
    return lambda: pl.semaphore_wait(barrier, planes + PLANE)


def region_copies(regions, cells, table, sems, first):
    r, z, u = place()
    size = table.shape[0]
    up = pltpu.make_async_remote_copy(
        src_ref=cells.at[pl.ds(C_DEV - 1, 1)],
        dst_ref=table.at[pl.ds(size - 2, 1)],
        send_sem=sems.at[first + 0],
        recv_sem=sems.at[first + 1],
        device_id=(lax.rem(r + 1, regions), z * PLANE + u),
        device_id_type=MESH,
    )
    down = pltpu.make_async_remote_copy(
        src_ref=cells.at[pl.ds(0, 1)],
        dst_ref=table.at[pl.ds(size - 1, 1)],
        send_sem=sems.at[first + 2],
        recv_sem=sems.at[first + 3],
        device_id=(lax.rem(r + regions - 1, regions), z * PLANE + u),
        device_id_type=MESH,
    )
    return up, down


def send_along(planes, ahead, source, target, send_sem, recv_sem):
    r, z, u = place()
    return pltpu.make_async_remote_copy(
        src_ref=source, dst_ref=target, send_sem=send_sem, recv_sem=recv_sem,
        device_id=(r, along(z, u, planes, ahead)), device_id_type=MESH,
    )


def send_across(first, slots, planes, outbox, table, send_sem, recv_sem):
    r, z, u = place()
    rows = 2 * slots

    def send(ahead, carry):
        to = lax.rem(u + ahead, PLANE)
        pltpu.make_async_remote_copy(
            src_ref=outbox.at[to, pl.ds(2 * first, rows)],
            dst_ref=table.at[pl.ds(C_DEV + 2 * planes * u + 2 * first, rows)],
            send_sem=send_sem, recv_sem=recv_sem,
            device_id=(r, z * PLANE + to), device_id_type=MESH,
        ).start()
        return carry

    lax.fori_loop(1, PLANE, send, 0)


def choose(slot, export, cells, outbox):
    r, z, u = place()

    def fill(to, carry):
        for q in range(2):
            outbox[to, 2 * slot + q] = cells[export[slot, q, z * PLANE + to]]
        return carry

    lax.fori_loop(0, PLANE, fill, 0, unroll=True)


def keep_own(planes, cells, outbox, table):
    r, z, u = place()
    for k in range(C_DEV):
        table[k] = cells[k]
    for i in range(2 * planes):
        table[C_DEV + 2 * planes * u + i] = outbox[u, i]


def drain(planes, outbox, table, send_sem, recv_sem):
    sent = outbox.at[pl.ds(0, PLANE - 1)]
    pltpu.make_async_copy(sent, sent, send_sem).wait()
    landed = table.at[pl.ds(0, 2 * planes * (PLANE - 1))]
    pltpu.make_async_copy(landed, landed, recv_sem).wait()


def static_kernel(
    regions, planes,
    position, velocity, smoothing, mass, energy, active, count, export, source, shift, old,
    table, sounds, targets, rank, plan, exports, old_v,
    energy_v, position_v, velocity_v, smoothing_v, mass_v, active_v, count_s, source_v, shift_v,
    cells, exports_s, outbox, *rest,
):
    land, (
        sound_land, sound_outbox,
        fetch_sems, region_sems, export_sems, along_send, along_recv, across_sems, own_sem,
        sound_sems,
    ) = rest[: planes - 1], rest[planes - 1 :]
    wait_for_all = greet(regions, planes)
    fetches = [
        pltpu.make_async_copy(a, b, fetch_sems.at[i])
        for i, (a, b) in enumerate((
            (position, position_v), (smoothing, smoothing_v), (mass, mass_v), (count, count_s),
            (velocity, velocity_v), (export, exports.at[0]), (energy, energy_v),
            (active, active_v), (source, source_v), (shift, shift_v), (old, old_v),
        ))
    ]
    for fetch in fetches:
        fetch.start()
    for fetch in fetches:
        fetch.wait()
    slot = lax.broadcasted_iota(jnp.int32, (1, CAP), 1)
    for k in range(C_DEV):
        for i in range(3):
            cells[k, i : i + 1] = position_v[i, k : k + 1]
            cells[k, 5 + i : 6 + i] = velocity_v[i, k : k + 1]
        cells[k, 3:4] = jnp.where(slot < count_s[k], mass_v[k : k + 1], 0.0)
        cells[k, 4:5] = smoothing_v[k : k + 1]
        heat = (ADIABATIC * (ADIABATIC - 1.0)) * energy_v[k : k + 1]
        sound_land[0, k] = SOUND_UNIT * jnp.sqrt(heat)
    wait_for_all()
    regionals = region_copies(regions, cells, table, region_sems, 0) + region_copies(
        regions, sound_land.at[0], sounds, region_sems, 4
    )
    calls = [
        send_along(
            planes, ahead, sound_land.at[0], sound_land.at[i + 1], sound_sems.at[0],
            sound_sems.at[1],
        )
        for i, ahead in enumerate(ORDER)
    ]
    lists = [
        send_along(
            planes, ahead, exports.at[0], exports.at[i + 1], export_sems.at[0], export_sems.at[1]
        )
        for i, ahead in enumerate(ORDER)
    ]
    blocks = [
        send_along(planes, ahead, cells, land[i], along_send.at[i], along_recv.at[i])
        for i, ahead in enumerate(ORDER)
    ]
    for copy in lists + calls + blocks[:2] + list(regionals) + blocks[2:]:
        copy.start()

    live = active_v[...] > 0
    row = lax.broadcasted_iota(jnp.int32, (CAP, CAP), 0)
    col = lax.broadcasted_iota(jnp.int32, (CAP, CAP), 1)
    upper = jnp.where(row <= col, 1.0, 0.0)
    ordinal = jnp.dot(jnp.where(live, 1.0, 0.0), upper, preferred_element_type=F32)
    where_to = jnp.where(live, ordinal - 1.0, -1000.0)
    rank[...] = where_to
    groups = (jnp.sum(active_v[...], axis=1, keepdims=True) + (GROUP - 1)) // GROUP
    r, z, u = place()
    named = source_v[...]
    other = named - C_DEV
    behind = jnp.bitwise_and(z + planes - jnp.right_shift(other, 4), planes - 1)
    slot_of = jnp.zeros_like(behind)
    for i, ahead in enumerate(ORDER):
        slot_of = jnp.where(behind == ahead, i + 1, slot_of)
    peer = jnp.bitwise_and(jnp.right_shift(other, 1), PLANE - 1)
    moved = C_DEV + 2 * planes * peer + 2 * slot_of + jnp.bitwise_and(other, 1)
    inside = jnp.logical_and(named >= C_DEV, named < C_DEV + 2 * planes * PLANE)
    plan[:, 0:NB] = jnp.where(inside, moved, named)
    plan[:, SHIFT_AT : SHIFT_AT + NB] = shift_v[...]
    plan[:, GROUP_AT : GROUP_AT + 1] = groups

    sub = lax.broadcasted_iota(jnp.int32, (8, CAP), 0)

    def compact(k):
        fields = jnp.where(sub == 3, energy_v[k : k + 1], cells[k])
        picked = jnp.where(where_to[k : k + 1] == row.astype(F32), 1.0, 0.0)
        found = lax.dot_general(
            picked, fields, (((1,), (1,)), ((), ())),
            precision=lax.Precision.HIGHEST, preferred_element_type=F32,
        )
        x, y, z, e, h, vx, vy, vz = (
            jnp.broadcast_to(found[:, f : f + 1], (CAP, CAP)) for f in range(8)
        )
        inverse = 1.0 / h
        second = inverse * inverse
        for at, value in (
            (X, x), (Y, y), (Z, z), (INVERSE, inverse), (VX, vx), (VY, vy), (VZ, vz),
            (SECOND, second), (THIRD, second * inverse), (SMALL, 0.05 * h),
            (SOUND, SOUND_UNIT * jnp.sqrt(ADIABATIC * (ADIABATIC - 1.0) * e)),
            (HEAT, (ADIABATIC - 1.0) * e),
        ):
            targets[at, k] = value

    for k in range(EARLY):
        compact(k)
    drained = exports.at[pl.ds(1, planes - 1)]
    pltpu.make_async_copy(drained, drained, export_sems.at[1]).wait()
    pltpu.make_async_copy(drained, drained, export_sems.at[0]).wait()
    to_scalar = pltpu.make_async_copy(exports, exports_s, own_sem)
    to_scalar.start()
    to_scalar.wait()
    heard = sound_land.at[pl.ds(1, planes - 1)]
    pltpu.make_async_copy(heard, heard, sound_sems.at[1]).wait()
    for slot in range(planes):
        choose(slot, exports_s, sound_land.at[slot], sound_outbox)
    send_across(0, planes, planes, sound_outbox, sounds, sound_sems.at[2], sound_sems.at[3])
    choose(0, exports_s, cells, outbox)
    for i in range(planes - 1):
        if i + EARLY < C_DEV:
            compact(i + EARLY)
        blocks[i].wait_recv()
        choose(i + 1, exports_s, land[i], outbox)
        if (i + 2) % BATCH == 0:
            send_across(
                i + 2 - BATCH, BATCH, planes, outbox, table, across_sems.at[0], across_sems.at[1]
            )
    keep_own(planes, cells, outbox, table)
    keep_own(planes, sound_land.at[0], sound_outbox, sounds)
    for copy in regionals:
        copy.wait()
    for copy in blocks:
        copy.wait_send()
    pltpu.make_async_copy(heard, heard, sound_sems.at[0]).wait()
    drain(planes, sound_outbox, sounds, sound_sems.at[2], sound_sems.at[3])
    drain(planes, outbox, table, across_sems.at[0], across_sems.at[1])


def offsets_of(table, plan):
    size = table.shape[0]
    ones = jnp.ones((8, CAP), F32)
    lane = lax.broadcasted_iota(jnp.int32, (8, CAP), 1)
    row = lax.broadcasted_iota(jnp.int32, (CAP, CAP), 0)
    col = lax.broadcasted_iota(jnp.int32, (CAP, CAP), 1)
    named = jnp.where(lane < NB, plan[...], -1)
    held = []
    for start in range(0, size, CAP):
        stop = min(start + CAP, size)
        live = jnp.where(table[start:stop, 3, :] > 0.0, 1.0, 0.0)
        if stop - start < CAP:
            live = jnp.concatenate([live, jnp.zeros((CAP - (stop - start), CAP), F32)], axis=0)
        held.append(
            lax.dot_general(ones, live, (((1,), (1,)), ((), ())), preferred_element_type=F32)
        )
    lines = []
    for k in range(C_DEV):
        line = jnp.zeros((8, CAP), F32)
        for i, counts in enumerate(held):
            same = jnp.where(named[k : k + 1] == row + i * CAP, 1.0, 0.0)
            line += jnp.dot(counts, same, preferred_element_type=F32)
        lines.append(line[0:1])
    before = jnp.where(row < col, 1.0, 0.0)
    return jnp.dot(jnp.concatenate(lines, axis=0), before, preferred_element_type=F32)


def by_distance(planes):
    others = [(i, j) for i in range(planes) for j in range(PLANE) if (i, j) != (0, 0)]

    def hops(other):
        return min(other[0], planes - other[0]) + min(other[1] // 2, (PLANE - other[1] + 1) // 2)

    return sorted(others, key=lambda other: -hops(other))


def moving_kernel(
    regions, planes, exports, density, sources, sounds, plan, derived, offsets,
    table, cells, outbox, region_sems, sems,
):
    r, z, u = place()
    others = by_distance(planes)
    barrier = pltpu.get_barrier_semaphore()

    def at(other):
        return lax.rem(z + other[0], planes) * PLANE + lax.rem(u + other[1], PLANE)

    for other in others:
        pl.semaphore_signal(barrier, inc=1, device_id=(r, at(other)), device_id_type=MESH)
    for ahead in (1, regions - 1):
        pl.semaphore_signal(
            barrier, inc=1, device_id=(lax.rem(r + ahead, regions), z * PLANE + u),
            device_id_type=MESH,
        )
    for k in range(C_DEV):
        cells[k] = DENSITY_UNIT * density[k : k + 1]
    for i, other in enumerate(others):
        for q in range(2):
            outbox[i, q] = cells[exports[0, q, at(other)]]
    pl.semaphore_wait(barrier, planes * PLANE + 1)
    for i, other in enumerate(others):
        slot = ((0,) + ORDER).index(other[0])
        pltpu.make_async_remote_copy(
            src_ref=outbox.at[i],
            dst_ref=table.at[pl.ds(C_DEV + 2 * planes * u + 2 * slot, 2)],
            send_sem=sems.at[0], recv_sem=sems.at[1],
            device_id=(r, at(other)), device_id_type=MESH,
        ).start()
    regionals = region_copies(regions, cells, table, region_sems, 0)
    for copy in regionals:
        copy.start()
    for k in range(C_DEV):
        table[k] = cells[k]
    for q in range(2):
        table[C_DEV + 2 * planes * u + q] = cells[exports[0, q, z * PLANE + u]]

    def prepare(s, carry):
        h, m = sources[s, 4:5], sources[s, 3:4]
        inverse = 1.0 / h
        second = inverse * inverse
        derived[s, 0:1] = second
        derived[s, 1:2] = second * inverse
        derived[s, 2:3] = 0.05 * h
        derived[s, 3:4] = m * (1.5 / math.pi)
        sound = sounds[s]
        derived[s, 5:6] = sound
        derived[s, 7:8] = (4.0 / ADIABATIC) * (sound * sound)
        return carry

    lax.fori_loop(0, table.shape[0], prepare, 0, unroll=6)
    offsets[...] = offsets_of(sources, plan).astype(jnp.int32)
    for copy in regionals:
        copy.wait()
    pltpu.make_async_copy(outbox, outbox, sems.at[0]).wait()
    landed = table.at[pl.ds(0, 2 * len(others))]
    pltpu.make_async_copy(landed, landed, sems.at[1]).wait()

    def complete(s, carry):
        thin = table[s]
        derived[s, 4:5] = derived[s, 7:8] / thin
        derived[s, 6:7] = thin
        return carry

    lax.fori_loop(0, table.shape[0], complete, 0, unroll=6)


def fill_shifts(shifts):
    sub = lax.broadcasted_iota(jnp.int32, (8, CAP), 0)
    for s in range(NB):
        offset = (s // 9 - 1, s // 3 % 3 - 1, s % 3 - 1)
        shifts[s] = jnp.where(
            sub == 0, float(offset[0]),
            jnp.where(sub == 1, float(offset[1]), jnp.where(sub == 2, float(offset[2]), 0.0)),
        )


def pack(plan, offsets, k, blocks_of, deads, packed):
    lane = lax.broadcasted_iota(jnp.int32, (8, CAP), 1)
    current = deads
    for n in range(NB):
        at, end = offsets[k, n], offsets[k, n + 1]
        row, first = lax.shift_right_logical(at, 7), lax.bitwise_and(at, CAP - 1)
        kept = lane < first
        spilled = lax.shift_right_logical(end, 7) > row
        rolled = [pltpu.roll(block, first, 1) for block in blocks_of(plan[k, n], n)]
        current = [jnp.where(kept, old, new) for old, new in zip(current, rolled)]
        for ref, value in zip(packed, current):
            ref[row] = value
        current = [jnp.where(spilled, new, old) for old, new in zip(current, rolled)]
    at = offsets[k, NB]
    row, first = lax.shift_right_logical(at, 7), lax.bitwise_and(at, CAP - 1)
    for ref, value, dead in zip(packed, current, deads):
        ref[row] = jnp.where(lane < first, value, dead)
        for i in range(1, 8):
            ref[row + i] = dead
    return lax.shift_right_logical(at + CAP - 1, 7)


def by_size(rows, run, sizes=SIZES):
    if len(sizes) == 1:
        run(sizes[0])
        return
    half = len(sizes) // 2
    fits = rows <= sizes[half - 1]
    pl.when(fits)(lambda: by_size(rows, run, sizes[:half]))
    pl.when(jnp.logical_not(fits))(lambda: by_size(rows, run, sizes[half:]))


def density_kernel(
    plan, table, targets, rank, density_old,
    density, own,
    shifts, near, total, left,
):
    fill_shifts(shifts)
    sub = lax.broadcasted_iota(jnp.int32, (GROUP, CAP), 0)
    cube = 4.0 ** (-1.0 / 3.0)
    none = jnp.zeros((GROUP, CAP), F32)
    total[...] = none
    left[0] = left[1] = none

    def finish(k, g, partial, norm):
        found = jnp.sum(partial, axis=1, keepdims=True) * norm
        at = pl.multiple_of(jnp.maximum(g, 0) * GROUP, GROUP)
        own[0, k, pl.ds(at, GROUP), :] = targets[HEAT, k, pl.ds(at, GROUP), :] / found
        own[1, k, pl.ds(at, GROUP), :] = jnp.broadcast_to(found, (GROUP, CAP)) * DENSITY_UNIT
        here = rank[pl.ds(k, 1), :] == (sub + g * GROUP).astype(F32)
        return jnp.where(here, found, 0.0)

    def settle(k):
        last = finish(k, plan[k, GROUP_AT] - 1, left[0], left[1])
        summed = jnp.sum(total[...] + last, axis=0, keepdims=True)
        mine = pl.ds(k, 1)
        density[mine, :] = jnp.where(rank[mine, :] >= 0.0, summed, density_old[mine, :])
        total[...] = none

    def cell(k, carry):
        settle(jnp.maximum(k - 1, 0))
        for n in range(NB):
            near[n] = table[plan[k, n]] + shifts[plan[k, SHIFT_AT + n]]

        def setup(g):
            at = pl.multiple_of(jnp.minimum(g, CAP // GROUP - 1) * GROUP, GROUP)
            return tuple(targets[f, k, pl.ds(at, GROUP), :] for f in (X, Y, Z, INVERSE))

        def group(g, carry):
            (x, y, z, inverse), partial, norm = carry
            total[...] += finish(k, g - 1, partial, norm)
            following = setup(g + 1)
            scaled = cube * inverse
            partial = none
            for n in range(NB):
                dx, dy, dz = x - near[n, 0:1], y - near[n, 1:2], z - near[n, 2:3]
                square = jnp.maximum(dx * dx + dy * dy + dz * dz, TINY)
                radius = square * lax.rsqrt(square)
                outer = jnp.maximum(2.0 * cube - radius * scaled, 0.0)
                inner = jnp.maximum(1.0 - radius * inverse, 0.0)
                value = outer * outer * outer - inner * inner * inner
                partial += near[n, 3:4] * value
            return following, partial, inverse * inverse * inverse * (1.0 / math.pi)

        _, left[0], left[1] = lax.fori_loop(
            0, plan[k, GROUP_AT], group, (setup(0), none, none)
        )
        return carry

    lax.fori_loop(0, C_DEV, cell, 0)
    settle(C_DEV - 1)


def force_kernel(
    plan, offsets, table, derived, targets, own, rank, velocity, time_bin, density_in,
    acceleration, kicked, density, shifts, near, more, total, left,
):
    density[...] = density_in[...]
    sub = lax.broadcasted_iota(jnp.int32, (GROUP, CAP), 0)
    none = jnp.zeros((GROUP, CAP), F32)
    for i in range(3):
        total[i] = left[i] = none

    fill_shifts(shifts)
    deads = [table[0], jnp.where(sub == 3, 0.0, derived[0])]

    def finish(k, g, parts):
        here = rank[pl.ds(k, 1), :] == (sub + g * GROUP).astype(F32)
        return [
            jnp.where(here, jnp.sum(part, axis=1, keepdims=True), 0.0) for part in parts
        ]

    def settle(k):
        last = finish(k, plan[k, GROUP_AT] - 1, [left[i] for i in range(3)])
        mine = pl.ds(k, 1)
        step = STEP_MAX * jnp.exp2(-time_bin[mine, :].astype(F32))
        for i in range(3):
            found = jnp.sum(total[i] + last[i], axis=0, keepdims=True)
            acceleration[i, mine, :] = found
            kicked[i, mine, :] = velocity[i, mine, :] + found * step
            total[i] = none

    def cell(k, carry):
        settle(jnp.maximum(k - 1, 0))
        rows = pack(
            plan, offsets, k,
            lambda s, n: (table[s] + shifts[plan[k, SHIFT_AT + n]], derived[s]),
            deads, (near, more),
        )

        def setup(g):
            at = pl.multiple_of(jnp.minimum(g, CAP // GROUP - 1) * GROUP, GROUP)
            columns = (X, Y, Z, VX, VY, VZ, SECOND, THIRD, SMALL, SOUND)
            return tuple(targets[f, k, pl.ds(at, GROUP), :] for f in columns) + tuple(
                own[f, k, pl.ds(at, GROUP), :] for f in range(2)
            )

        def run(size):
            def group(g, carry):
                (x, y, z, vx, vy, vz, second, third, small, sound, press, thin), parts = carry
                for i, found in enumerate(finish(k, g - 1, parts)):
                    total[i] += found
                following = setup(g + 1)
                ax = ay = az = jnp.zeros((GROUP, CAP), F32)
                for n in range(size):
                    dx, dy, dz = x - near[n, 0:1], y - near[n, 1:2], z - near[n, 2:3]
                    square = jnp.maximum(dx * dx + dy * dy + dz * dz, TINY)
                    over = lax.rsqrt(square)
                    radius = square * over
                    reach = radius * third
                    outer = jnp.maximum(second - 0.5 * reach, 0.0)
                    inner = jnp.maximum(second - reach, 0.0)
                    slope = outer * outer - inner * inner
                    second_j = more[n, 0:1]
                    reach = radius * more[n, 1:2]
                    outer = jnp.maximum(second_j - 0.5 * reach, 0.0)
                    inner = jnp.maximum(second_j - reach, 0.0)
                    slope += outer * outer - inner * inner
                    approach = (
                        (vx - near[n, 5:6]) * dx
                        + (vy - near[n, 6:7]) * dy
                        + (vz - near[n, 7:8]) * dz
                    )
                    mean = small + more[n, 2:3]
                    mu = mean * jnp.minimum(approach, 0.0) * (1.0 / (square + mean * mean))
                    viscous = mu * (mu - (sound + more[n, 5:6])) * (1.0 / (thin + more[n, 6:7]))
                    weight = more[n, 3:4] * (press + more[n, 4:5] + viscous) * (slope * over)
                    ax += weight * dx
                    ay += weight * dy
                    az += weight * dz
                return following, (ax, ay, az)

            _, parts = lax.fori_loop(
                0, plan[k, GROUP_AT], group, (setup(0), (none, none, none))
            )
            for i in range(3):
                left[i] = parts[i]

        by_size(rows, run)
        return carry

    lax.fori_loop(0, C_DEV, cell, 0)
    settle(C_DEV - 1)


def shards(
    regions, planes,
    position, velocity, smoothing, particle_mass, energy, density_old, cell_count, active,
    time_bin, pair_source, pair_shift, export,
):
    size = C_DEV + 2 * planes * PLANE + 2
    vmem = pl.BlockSpec(memory_space=pltpu.VMEM)
    smem = pl.BlockSpec(memory_space=pltpu.SMEM)
    hbm = pl.BlockSpec(memory_space=pltpu.HBM)
    dma = pltpu.SemaphoreType.DMA

    def shape(*dims, dtype=F32):
        return jax.ShapeDtypeStruct(dims, dtype)

    def ints(*dims):
        return pltpu.VMEM(dims, jnp.int32)

    def floats(*dims):
        return pltpu.VMEM(dims, F32)

    limit = 32 << 20
    table, sounds, targets, rank, plan, exports, density_old = pl.pallas_call(
        functools.partial(static_kernel, regions, planes),
        out_shape=[
            shape(size, 8, CAP), shape(size, 1, CAP), shape(TARGET, C_DEV, CAP, CAP),
            shape(C_DEV, CAP),
            shape(C_DEV, CAP, dtype=jnp.int32),
            shape(planes, 2, planes * PLANE, dtype=jnp.int32), shape(C_DEV, CAP),
        ],
        in_specs=[hbm] * 11,
        out_specs=[vmem] * 7,
        scratch_shapes=[
            floats(C_DEV, CAP), floats(3, C_DEV, CAP), floats(3, C_DEV, CAP), floats(C_DEV, CAP),
            floats(C_DEV, CAP), ints(C_DEV, CAP), pltpu.SMEM((C_DEV,), jnp.int32),
            ints(C_DEV, NB), ints(C_DEV, NB),
            floats(C_DEV, 8, CAP), pltpu.SMEM((planes, 2, planes * PLANE), jnp.int32),
            floats(PLANE, 2 * planes, 8, CAP),
            *[floats(C_DEV, 8, CAP) for _ in range(planes - 1)],
            floats(planes, C_DEV, 1, CAP), floats(PLANE, 2 * planes, 1, CAP),
            dma((11,)), dma((8,)), dma((2,)), dma((planes - 1,)), dma((planes - 1,)), dma((2,)),
            dma, dma((4,)),
        ],
        compiler_params=pltpu.CompilerParams(
            collective_id=0, has_side_effects=True, vmem_limit_bytes=limit
        ),
    )(
        *(
            pltpu.with_memory_space_constraint(x, pltpu.HBM)
            for x in (
                position, velocity, smoothing, particle_mass, energy, active, cell_count, export.T,
                pair_source, pair_shift, density_old,
            )
        )
    )
    density, own = pl.pallas_call(
        density_kernel,
        out_shape=[shape(C_DEV, CAP), shape(2, C_DEV, CAP, CAP)],
        in_specs=[smem] + [vmem] * 4,
        out_specs=[vmem] * 2,
        scratch_shapes=[
            floats(NB, 8, CAP), floats(NB, 8, CAP), floats(GROUP, CAP), floats(2, GROUP, CAP),
        ],
        compiler_params=pltpu.CompilerParams(vmem_limit_bytes=limit),
    )(plan, table, targets, rank, density_old)
    derived, offsets = pl.pallas_call(
        functools.partial(moving_kernel, regions, planes),
        out_shape=[shape(size, 8, CAP), shape(C_DEV, CAP, dtype=jnp.int32)],
        in_specs=[smem] + [vmem] * 4,
        out_specs=[vmem] * 2,
        scratch_shapes=[
            floats(size, 1, CAP), floats(C_DEV, 1, CAP),
            floats(planes * PLANE - 1, 2, 1, CAP), dma((4,)), dma((2,)),
        ],
        compiler_params=pltpu.CompilerParams(
            collective_id=1, has_side_effects=True, vmem_limit_bytes=limit
        ),
    )(exports, density, table, sounds, plan)
    acceleration, kicked, density = pl.pallas_call(
        force_kernel,
        out_shape=[shape(3, C_DEV, CAP), shape(3, C_DEV, CAP), shape(C_DEV, CAP)],
        in_specs=[smem] * 2 + [vmem] * 8,
        out_specs=[vmem] * 3,
        scratch_shapes=[
            floats(NB, 8, CAP), floats(ROWS, 8, CAP), floats(ROWS, 8, CAP),
            floats(3, GROUP, CAP), floats(3, GROUP, CAP),
        ],
        compiler_params=pltpu.CompilerParams(vmem_limit_bytes=limit),
    )(plan, offsets, table, derived, targets, own, rank, velocity, time_bin, density)
    return density, acceleration, kicked


def solution(mesh):
    both = ("region", "cell")
    flat, wide_rows = P(both, None), P(None, both, None)
    return jax.shard_map(
        functools.partial(shards, mesh.shape["region"], mesh.shape["cell"] // PLANE),
        mesh=mesh,
        in_specs=(
            wide_rows, wide_rows, flat, flat, flat, flat, P(both), flat, flat, flat, flat, flat,
        ),
        out_specs=(flat, wide_rows, wide_rows),
        check_vma=False,
    )
```

```python
import functools
import math

import jax
import jax.numpy as jnp
from jax import lax
from jax.experimental import pallas as pl
from jax.experimental.pallas import tpu as pltpu
from jax.sharding import PartitionSpec as P

MESH = pl.DeviceIdType.MESH
C_DEV = 8
CAP = 128
NB = 27
GROUP = 8
PLANE = 8
ORDER = (1, 7, 4, 2, 6, 3, 5)
EARLY = 6
BATCH = 2
ADIABATIC = 5.0 / 3.0
STEP_MAX = 0.2
TINY = 1e-30
F32 = jnp.float32
SHIFT_AT, GROUP_AT = 32, 64
SIZES = (8, 12, 15, 16, 17, 18, 19, 20, 22, 24, 27)
ROWS = NB + 8
X, Y, Z, INVERSE, VX, VY, VZ, SECOND, THIRD, SMALL, SOUND, HEAT = range(12)
TARGET = 12
SOUND_UNIT = 0.025
DENSITY_UNIT = 1.0 / 400.0


def place():
    r, c = lax.axis_index("region"), lax.axis_index("cell")
    return r, lax.div(c, PLANE), lax.rem(c, PLANE)


def along(z, u, planes, ahead):
    return lax.rem(z + ahead, planes) * PLANE + u


def across(z, u, ahead):
    return z * PLANE + lax.rem(u + ahead, PLANE)


def greet(regions, planes):
    r, z, u = place()
    barrier = pltpu.get_barrier_semaphore()
    for ahead in sorted(range(1, planes), key=lambda a: -min(a, planes - a)):
        pl.semaphore_signal(
            barrier, inc=1, device_id=(r, along(z, u, planes, ahead)), device_id_type=MESH
        )
    for ahead in range(1, PLANE):
        pl.semaphore_signal(
            barrier, inc=1, device_id=(r, across(z, u, ahead)), device_id_type=MESH
        )
    for ahead in (1, regions - 1):
        pl.semaphore_signal(
            barrier, inc=1, device_id=(lax.rem(r + ahead, regions), z * PLANE + u),
            device_id_type=MESH,
        )
    return lambda: pl.semaphore_wait(barrier, planes + PLANE)


def region_copies(regions, cells, table, sems, first):
    r, z, u = place()
    size = table.shape[0]
    up = pltpu.make_async_remote_copy(
        src_ref=cells.at[pl.ds(C_DEV - 1, 1)],
        dst_ref=table.at[pl.ds(size - 2, 1)],
        send_sem=sems.at[first + 0],
        recv_sem=sems.at[first + 1],
        device_id=(lax.rem(r + 1, regions), z * PLANE + u),
        device_id_type=MESH,
    )
    down = pltpu.make_async_remote_copy(
        src_ref=cells.at[pl.ds(0, 1)],
        dst_ref=table.at[pl.ds(size - 1, 1)],
        send_sem=sems.at[first + 2],
        recv_sem=sems.at[first + 3],
        device_id=(lax.rem(r + regions - 1, regions), z * PLANE + u),
        device_id_type=MESH,
    )
    return up, down


def send_along(planes, ahead, source, target, send_sem, recv_sem):
    r, z, u = place()
    return pltpu.make_async_remote_copy(
        src_ref=source, dst_ref=target, send_sem=send_sem, recv_sem=recv_sem,
        device_id=(r, along(z, u, planes, ahead)), device_id_type=MESH,
    )


def send_across(first, slots, planes, outbox, table, send_sem, recv_sem):
    r, z, u = place()
    rows = 2 * slots

    def send(ahead, carry):
        to = lax.rem(u + ahead, PLANE)
        pltpu.make_async_remote_copy(
            src_ref=outbox.at[to, pl.ds(2 * first, rows)],
            dst_ref=table.at[pl.ds(C_DEV + 2 * planes * u + 2 * first, rows)],
            send_sem=send_sem, recv_sem=recv_sem,
            device_id=(r, z * PLANE + to), device_id_type=MESH,
        ).start()
        return carry

    lax.fori_loop(1, PLANE, send, 0)


def choose(slot, export, cells, outbox):
    r, z, u = place()

    def fill(to, carry):
        for q in range(2):
            outbox[to, 2 * slot + q] = cells[export[slot, q, z * PLANE + to]]
        return carry

    lax.fori_loop(0, PLANE, fill, 0, unroll=True)


def keep_own(planes, cells, outbox, table):
    r, z, u = place()
    for k in range(C_DEV):
        table[k] = cells[k]
    for i in range(2 * planes):
        table[C_DEV + 2 * planes * u + i] = outbox[u, i]


def drain(planes, outbox, table, send_sem, recv_sem):
    sent = outbox.at[pl.ds(0, PLANE - 1)]
    pltpu.make_async_copy(sent, sent, send_sem).wait()
    landed = table.at[pl.ds(0, 2 * planes * (PLANE - 1))]
    pltpu.make_async_copy(landed, landed, recv_sem).wait()


def static_kernel(
    regions, planes,
    position, velocity, smoothing, mass, energy, active, count, export, source, shift, old,
    table, sounds, targets, rank, plan, exports, old_v,
    energy_v, position_v, velocity_v, smoothing_v, mass_v, active_v, count_s, source_v, shift_v,
    cells, exports_s, outbox, *rest,
):
    land, (
        sound_land, sound_outbox,
        fetch_sems, region_sems, export_sems, along_send, along_recv, across_sems, own_sem,
        sound_sems, own_s, list_sem,
    ) = rest[: planes - 1], rest[planes - 1 :]
    wait_for_all = greet(regions, planes)
    fetches = [
        pltpu.make_async_copy(a, b, fetch_sems.at[i])
        for i, (a, b) in enumerate((
            (position, position_v), (smoothing, smoothing_v), (mass, mass_v), (count, count_s),
            (velocity, velocity_v), (export, exports.at[0]), (energy, energy_v),
            (active, active_v), (source, source_v), (shift, shift_v), (old, old_v),
        ))
    ]
    for fetch in fetches:
        fetch.start()
    for fetch in fetches:
        fetch.wait()
    slot = lax.broadcasted_iota(jnp.int32, (1, CAP), 1)
    for k in range(C_DEV):
        for i in range(3):
            cells[k, i : i + 1] = position_v[i, k : k + 1]
            cells[k, 5 + i : 6 + i] = velocity_v[i, k : k + 1]
        cells[k, 3:4] = jnp.where(slot < count_s[k], mass_v[k : k + 1], 0.0)
        cells[k, 4:5] = smoothing_v[k : k + 1]
        heat = (ADIABATIC * (ADIABATIC - 1.0)) * energy_v[k : k + 1]
        sound_land[0, k] = SOUND_UNIT * jnp.sqrt(heat)
    wait_for_all()
    regionals = region_copies(regions, cells, table, region_sems, 0) + region_copies(
        regions, sound_land.at[0], sounds, region_sems, 4
    )
    calls = [
        send_along(
            planes, ahead, sound_land.at[0], sound_land.at[i + 1], sound_sems.at[0],
            sound_sems.at[1],
        )
        for i, ahead in enumerate(ORDER)
    ]
    lists = [
        send_along(
            planes, ahead, exports.at[0], exports.at[i + 1], export_sems.at[0], export_sems.at[1]
        )
        for i, ahead in enumerate(ORDER)
    ]
    blocks = [
        send_along(planes, ahead, cells, land[i], along_send.at[i], along_recv.at[i])
        for i, ahead in enumerate(ORDER)
    ]
    own_list = pltpu.make_async_copy(exports.at[pl.ds(0, 1)], own_s, list_sem)
    own_list.start()
    for copy in lists + calls + blocks[:2] + list(regionals) + blocks[2:]:
        copy.start()

    live = active_v[...] > 0
    row = lax.broadcasted_iota(jnp.int32, (CAP, CAP), 0)
    col = lax.broadcasted_iota(jnp.int32, (CAP, CAP), 1)
    upper = jnp.where(row <= col, 1.0, 0.0)
    ordinal = jnp.dot(jnp.where(live, 1.0, 0.0), upper, preferred_element_type=F32)
    where_to = jnp.where(live, ordinal - 1.0, -1000.0)
    rank[...] = where_to
    groups = (jnp.sum(active_v[...], axis=1, keepdims=True) + (GROUP - 1)) // GROUP
    r, z, u = place()
    named = source_v[...]
    other = named - C_DEV
    behind = jnp.bitwise_and(z + planes - jnp.right_shift(other, 4), planes - 1)
    slot_of = jnp.zeros_like(behind)
    for i, ahead in enumerate(ORDER):
        slot_of = jnp.where(behind == ahead, i + 1, slot_of)
    peer = jnp.bitwise_and(jnp.right_shift(other, 1), PLANE - 1)
    moved = C_DEV + 2 * planes * peer + 2 * slot_of + jnp.bitwise_and(other, 1)
    inside = jnp.logical_and(named >= C_DEV, named < C_DEV + 2 * planes * PLANE)
    plan[:, 0:NB] = jnp.where(inside, moved, named)
    plan[:, SHIFT_AT : SHIFT_AT + NB] = shift_v[...]
    plan[:, GROUP_AT : GROUP_AT + 1] = groups

    sub = lax.broadcasted_iota(jnp.int32, (8, CAP), 0)

    def compact(k):
        fields = jnp.where(sub == 3, energy_v[k : k + 1], cells[k])
        picked = jnp.where(where_to[k : k + 1] == row.astype(F32), 1.0, 0.0)
        found = lax.dot_general(
            picked, fields, (((1,), (1,)), ((), ())),
            precision=lax.Precision.HIGHEST, preferred_element_type=F32,
        )
        x, y, z, e, h, vx, vy, vz = (
            jnp.broadcast_to(found[:, f : f + 1], (CAP, CAP)) for f in range(8)
        )
        inverse = 1.0 / h
        second = inverse * inverse
        for at, value in (
            (X, x), (Y, y), (Z, z), (INVERSE, inverse), (VX, vx), (VY, vy), (VZ, vz),
            (SECOND, second), (THIRD, 0.5 * second * inverse), (SMALL, 0.05 * h),
            (SOUND, SOUND_UNIT * jnp.sqrt(ADIABATIC * (ADIABATIC - 1.0) * e)),
            (HEAT, (ADIABATIC - 1.0) * e),
        ):
            targets[at, k] = value

    for k in range(EARLY):
        compact(k)
    own_list.wait()
    choose(0, own_s, cells, outbox)
    drained = exports.at[pl.ds(1, planes - 1)]
    pltpu.make_async_copy(drained, drained, export_sems.at[1]).wait()
    pltpu.make_async_copy(drained, drained, export_sems.at[0]).wait()
    to_scalar = pltpu.make_async_copy(exports, exports_s, own_sem)
    to_scalar.start()
    to_scalar.wait()
    heard = sound_land.at[pl.ds(1, planes - 1)]
    pltpu.make_async_copy(heard, heard, sound_sems.at[1]).wait()
    for slot in range(planes):
        choose(slot, exports_s, sound_land.at[slot], sound_outbox)
    send_across(0, planes, planes, sound_outbox, sounds, sound_sems.at[2], sound_sems.at[3])
    for i in range(planes - 1):
        if i + EARLY < C_DEV:
            compact(i + EARLY)
        blocks[i].wait_recv()
        choose(i + 1, exports_s, land[i], outbox)
        if (i + 2) % BATCH == 0:
            send_across(
                i + 2 - BATCH, BATCH, planes, outbox, table, across_sems.at[0], across_sems.at[1]
            )
    keep_own(planes, cells, outbox, table)
    keep_own(planes, sound_land.at[0], sound_outbox, sounds)
    for copy in regionals:
        copy.wait()
    for copy in blocks:
        copy.wait_send()
    pltpu.make_async_copy(heard, heard, sound_sems.at[0]).wait()
    drain(planes, sound_outbox, sounds, sound_sems.at[2], sound_sems.at[3])
    drain(planes, outbox, table, across_sems.at[0], across_sems.at[1])


def offsets_of(table, plan):
    size = table.shape[0]
    ones = jnp.ones((8, CAP), F32)
    lane = lax.broadcasted_iota(jnp.int32, (8, CAP), 1)
    row = lax.broadcasted_iota(jnp.int32, (CAP, CAP), 0)
    col = lax.broadcasted_iota(jnp.int32, (CAP, CAP), 1)
    named = jnp.where(lane < NB, plan[...], -1)
    held = []
    for start in range(0, size, CAP):
        stop = min(start + CAP, size)
        live = jnp.where(table[start:stop, 3, :] > 0.0, 1.0, 0.0)
        if stop - start < CAP:
            live = jnp.concatenate([live, jnp.zeros((CAP - (stop - start), CAP), F32)], axis=0)
        held.append(
            lax.dot_general(ones, live, (((1,), (1,)), ((), ())), preferred_element_type=F32)
        )
    lines = []
    for k in range(C_DEV):
        line = jnp.zeros((8, CAP), F32)
        for i, counts in enumerate(held):
            same = jnp.where(named[k : k + 1] == row + i * CAP, 1.0, 0.0)
            line += jnp.dot(counts, same, preferred_element_type=F32)
        lines.append(line[0:1])
    before = jnp.where(row < col, 1.0, 0.0)
    return jnp.dot(jnp.concatenate(lines, axis=0), before, preferred_element_type=F32)


def by_distance(planes):
    others = [(i, j) for i in range(planes) for j in range(PLANE) if (i, j) != (0, 0)]

    def hops(other):
        return min(other[0], planes - other[0]) + min(other[1] // 2, (PLANE - other[1] + 1) // 2)

    return sorted(others, key=lambda other: -hops(other))


def moving_kernel(
    regions, planes, exports, density, sources, sounds, plan, derived, offsets,
    table, cells, outbox, region_sems, sems,
):
    r, z, u = place()
    others = by_distance(planes)
    barrier = pltpu.get_barrier_semaphore()

    def at(other):
        return lax.rem(z + other[0], planes) * PLANE + lax.rem(u + other[1], PLANE)

    for other in others:
        pl.semaphore_signal(barrier, inc=1, device_id=(r, at(other)), device_id_type=MESH)
    for ahead in (1, regions - 1):
        pl.semaphore_signal(
            barrier, inc=1, device_id=(lax.rem(r + ahead, regions), z * PLANE + u),
            device_id_type=MESH,
        )
    for k in range(C_DEV):
        cells[k] = DENSITY_UNIT * density[k : k + 1]
    for i, other in enumerate(others):
        for q in range(2):
            outbox[i, q] = cells[exports[0, q, at(other)]]
    pl.semaphore_wait(barrier, planes * PLANE + 1)
    for i, other in enumerate(others):
        slot = ((0,) + ORDER).index(other[0])
        pltpu.make_async_remote_copy(
            src_ref=outbox.at[i],
            dst_ref=table.at[pl.ds(C_DEV + 2 * planes * u + 2 * slot, 2)],
            send_sem=sems.at[0], recv_sem=sems.at[1],
            device_id=(r, at(other)), device_id_type=MESH,
        ).start()
    regionals = region_copies(regions, cells, table, region_sems, 0)
    for copy in regionals:
        copy.start()
    for k in range(C_DEV):
        table[k] = cells[k]
    for q in range(2):
        table[C_DEV + 2 * planes * u + q] = cells[exports[0, q, z * PLANE + u]]

    def prepare(s, carry):
        h, m = sources[s, 4:5], sources[s, 3:4]
        inverse = 1.0 / h
        second = inverse * inverse
        derived[s, 0:1] = second
        derived[s, 1:2] = 0.5 * second * inverse
        derived[s, 2:3] = 0.05 * h
        derived[s, 3:4] = m * (1.5 / math.pi)
        sound = sounds[s]
        derived[s, 5:6] = sound
        derived[s, 7:8] = (4.0 / ADIABATIC) * (sound * sound)
        return carry

    lax.fori_loop(0, table.shape[0], prepare, 0, unroll=6)
    offsets[...] = offsets_of(sources, plan).astype(jnp.int32)
    for copy in regionals:
        copy.wait()
    pltpu.make_async_copy(outbox, outbox, sems.at[0]).wait()
    landed = table.at[pl.ds(0, 2 * len(others))]
    pltpu.make_async_copy(landed, landed, sems.at[1]).wait()

    def complete(s, carry):
        thin = table[s]
        derived[s, 4:5] = derived[s, 7:8] / thin
        derived[s, 6:7] = thin
        return carry

    lax.fori_loop(0, table.shape[0], complete, 0, unroll=6)


def fill_shifts(shifts):
    sub = lax.broadcasted_iota(jnp.int32, (8, CAP), 0)
    for s in range(NB):
        offset = (s // 9 - 1, s // 3 % 3 - 1, s % 3 - 1)
        shifts[s] = jnp.where(
            sub == 0, float(offset[0]),
            jnp.where(sub == 1, float(offset[1]), jnp.where(sub == 2, float(offset[2]), 0.0)),
        )


def pack(plan, offsets, k, blocks_of, deads, packed):
    lane = lax.broadcasted_iota(jnp.int32, (8, CAP), 1)
    current = deads
    for n in range(NB):
        at, end = offsets[k, n], offsets[k, n + 1]
        row, first = lax.shift_right_logical(at, 7), lax.bitwise_and(at, CAP - 1)
        kept = lane < first
        spilled = lax.shift_right_logical(end, 7) > row
        rolled = [pltpu.roll(block, first, 1) for block in blocks_of(plan[k, n], n)]
        current = [jnp.where(kept, old, new) for old, new in zip(current, rolled)]
        for ref, value in zip(packed, current):
            ref[row] = value
        current = [jnp.where(spilled, new, old) for old, new in zip(current, rolled)]
    at = offsets[k, NB]
    row, first = lax.shift_right_logical(at, 7), lax.bitwise_and(at, CAP - 1)
    for ref, value, dead in zip(packed, current, deads):
        ref[row] = jnp.where(lane < first, value, dead)
        for i in range(1, 8):
            ref[row + i] = dead
    return lax.shift_right_logical(at + CAP - 1, 7)


def by_size(rows, run, sizes=SIZES):
    if len(sizes) == 1:
        run(sizes[0])
        return
    half = len(sizes) // 2
    fits = rows <= sizes[half - 1]
    pl.when(fits)(lambda: by_size(rows, run, sizes[:half]))
    pl.when(jnp.logical_not(fits))(lambda: by_size(rows, run, sizes[half:]))


def density_kernel(
    plan, table, targets, rank, density_old,
    density, own,
    shifts, near, total, left,
):
    fill_shifts(shifts)
    sub = lax.broadcasted_iota(jnp.int32, (GROUP, CAP), 0)
    cube = 4.0 ** (-1.0 / 3.0)
    none = jnp.zeros((GROUP, CAP), F32)
    total[...] = none
    left[0] = left[1] = none

    def finish(k, g, partial, norm):
        found = jnp.sum(partial, axis=1, keepdims=True) * norm
        at = pl.multiple_of(jnp.maximum(g, 0) * GROUP, GROUP)
        own[0, k, pl.ds(at, GROUP), :] = targets[HEAT, k, pl.ds(at, GROUP), :] / found
        own[1, k, pl.ds(at, GROUP), :] = jnp.broadcast_to(found, (GROUP, CAP)) * DENSITY_UNIT
        here = rank[pl.ds(k, 1), :] == (sub + g * GROUP).astype(F32)
        return jnp.where(here, found, 0.0)

    def settle(k):
        last = finish(k, plan[k, GROUP_AT] - 1, left[0], left[1])
        summed = jnp.sum(total[...] + last, axis=0, keepdims=True)
        mine = pl.ds(k, 1)
        density[mine, :] = jnp.where(rank[mine, :] >= 0.0, summed, density_old[mine, :])
        total[...] = none

    def cell(k, carry):
        settle(jnp.maximum(k - 1, 0))
        for n in range(NB):
            near[n] = table[plan[k, n]] + shifts[plan[k, SHIFT_AT + n]]

        def setup(g):
            at = pl.multiple_of(jnp.minimum(g, CAP // GROUP - 1) * GROUP, GROUP)
            return tuple(targets[f, k, pl.ds(at, GROUP), :] for f in (X, Y, Z, INVERSE))

        def group(g, carry):
            (x, y, z, inverse), partial, norm = carry
            total[...] += finish(k, g - 1, partial, norm)
            following = setup(g + 1)
            scaled = cube * inverse
            partial = none
            for n in range(NB):
                dx, dy, dz = x - near[n, 0:1], y - near[n, 1:2], z - near[n, 2:3]
                square = jnp.maximum(dx * dx + dy * dy + dz * dz, TINY)
                radius = square * lax.rsqrt(square)
                outer = jnp.maximum(2.0 * cube - radius * scaled, 0.0)
                inner = jnp.maximum(1.0 - radius * inverse, 0.0)
                value = outer * outer * outer - inner * inner * inner
                partial += near[n, 3:4] * value
            return following, partial, inverse * inverse * inverse * (1.0 / math.pi)

        _, left[0], left[1] = lax.fori_loop(
            0, plan[k, GROUP_AT], group, (setup(0), none, none)
        )
        return carry

    lax.fori_loop(0, C_DEV, cell, 0)
    settle(C_DEV - 1)


def force_kernel(
    plan, offsets, table, derived, targets, own, rank, velocity, time_bin, density_in,
    acceleration, kicked, density, shifts, near, more, total, left,
):
    density[...] = density_in[...]
    sub = lax.broadcasted_iota(jnp.int32, (GROUP, CAP), 0)
    none = jnp.zeros((GROUP, CAP), F32)
    for i in range(3):
        total[i] = left[i] = none

    fill_shifts(shifts)
    deads = [table[0], jnp.where(sub == 3, 0.0, derived[0])]

    def finish(k, g, parts):
        here = rank[pl.ds(k, 1), :] == (sub + g * GROUP).astype(F32)
        return [
            jnp.where(here, jnp.sum(part, axis=1, keepdims=True), 0.0) for part in parts
        ]

    def settle(k):
        last = finish(k, plan[k, GROUP_AT] - 1, [left[i] for i in range(3)])
        mine = pl.ds(k, 1)
        step = STEP_MAX * jnp.exp2(-time_bin[mine, :].astype(F32))
        for i in range(3):
            found = jnp.sum(total[i] + last[i], axis=0, keepdims=True)
            acceleration[i, mine, :] = found
            kicked[i, mine, :] = velocity[i, mine, :] + found * step
            total[i] = none

    def cell(k, carry):
        settle(jnp.maximum(k - 1, 0))
        rows = pack(
            plan, offsets, k,
            lambda s, n: (table[s] + shifts[plan[k, SHIFT_AT + n]], derived[s]),
            deads, (near, more),
        )

        def setup(g):
            at = pl.multiple_of(jnp.minimum(g, CAP // GROUP - 1) * GROUP, GROUP)
            columns = (X, Y, Z, VX, VY, VZ, SECOND, THIRD, SMALL, SOUND)
            return tuple(targets[f, k, pl.ds(at, GROUP), :] for f in columns) + tuple(
                own[f, k, pl.ds(at, GROUP), :] for f in range(2)
            )

        def run(size):
            def group(g, carry):
                (x, y, z, vx, vy, vz, second, third, small, sound, press, thin), parts = carry
                for i, found in enumerate(finish(k, g - 1, parts)):
                    total[i] += found
                following = setup(g + 1)
                ax = ay = az = jnp.zeros((GROUP, CAP), F32)
                for n in range(size):
                    dx, dy, dz = x - near[n, 0:1], y - near[n, 1:2], z - near[n, 2:3]
                    square = jnp.maximum(dx * dx + dy * dy + dz * dz, TINY)
                    over = lax.rsqrt(square)
                    radius = square * over
                    half = radius * third
                    outer = second - half
                    inner = jnp.maximum(outer - half, 0.0)
                    outer = jnp.maximum(outer, 0.0)
                    slope = outer * outer - inner * inner
                    half = radius * more[n, 1:2]
                    outer = more[n, 0:1] - half
                    inner = jnp.maximum(outer - half, 0.0)
                    outer = jnp.maximum(outer, 0.0)
                    slope += outer * outer - inner * inner
                    approach = (
                        (vx - near[n, 5:6]) * dx
                        + (vy - near[n, 6:7]) * dy
                        + (vz - near[n, 7:8]) * dz
                    )
                    mean = small + more[n, 2:3]
                    mu = mean * jnp.minimum(approach, 0.0) * (1.0 / (square + mean * mean))
                    viscous = mu * (mu - (sound + more[n, 5:6])) * (1.0 / (thin + more[n, 6:7]))
                    weight = more[n, 3:4] * (press + more[n, 4:5] + viscous) * (slope * over)
                    ax += weight * dx
                    ay += weight * dy
                    az += weight * dz
                return following, (ax, ay, az)

            _, parts = lax.fori_loop(
                0, plan[k, GROUP_AT], group, (setup(0), (none, none, none))
            )
            for i in range(3):
                left[i] = parts[i]

        by_size(rows, run)
        return carry

    lax.fori_loop(0, C_DEV, cell, 0)
    settle(C_DEV - 1)


def shards(
    regions, planes,
    position, velocity, smoothing, particle_mass, energy, density_old, cell_count, active,
    time_bin, pair_source, pair_shift, export,
):
    size = C_DEV + 2 * planes * PLANE + 2
    vmem = pl.BlockSpec(memory_space=pltpu.VMEM)
    smem = pl.BlockSpec(memory_space=pltpu.SMEM)
    hbm = pl.BlockSpec(memory_space=pltpu.HBM)
    dma = pltpu.SemaphoreType.DMA

    def shape(*dims, dtype=F32):
        return jax.ShapeDtypeStruct(dims, dtype)

    def ints(*dims):
        return pltpu.VMEM(dims, jnp.int32)

    def floats(*dims):
        return pltpu.VMEM(dims, F32)

    limit = 32 << 20
    table, sounds, targets, rank, plan, exports, density_old = pl.pallas_call(
        functools.partial(static_kernel, regions, planes),
        out_shape=[
            shape(size, 8, CAP), shape(size, 1, CAP), shape(TARGET, C_DEV, CAP, CAP),
            shape(C_DEV, CAP),
            shape(C_DEV, CAP, dtype=jnp.int32),
            shape(planes, 2, planes * PLANE, dtype=jnp.int32), shape(C_DEV, CAP),
        ],
        in_specs=[hbm] * 11,
        out_specs=[vmem] * 7,
        scratch_shapes=[
            floats(C_DEV, CAP), floats(3, C_DEV, CAP), floats(3, C_DEV, CAP), floats(C_DEV, CAP),
            floats(C_DEV, CAP), ints(C_DEV, CAP), pltpu.SMEM((C_DEV,), jnp.int32),
            ints(C_DEV, NB), ints(C_DEV, NB),
            floats(C_DEV, 8, CAP), pltpu.SMEM((planes, 2, planes * PLANE), jnp.int32),
            floats(PLANE, 2 * planes, 8, CAP),
            *[floats(C_DEV, 8, CAP) for _ in range(planes - 1)],
            floats(planes, C_DEV, 1, CAP), floats(PLANE, 2 * planes, 1, CAP),
            dma((11,)), dma((8,)), dma((2,)), dma((planes - 1,)), dma((planes - 1,)), dma((2,)),
            dma, dma((4,)), pltpu.SMEM((1, 2, planes * PLANE), jnp.int32), dma,
        ],
        compiler_params=pltpu.CompilerParams(
            collective_id=0, has_side_effects=True, vmem_limit_bytes=limit
        ),
    )(
        *(
            pltpu.with_memory_space_constraint(x, pltpu.HBM)
            for x in (
                position, velocity, smoothing, particle_mass, energy, active, cell_count, export.T,
                pair_source, pair_shift, density_old,
            )
        )
    )
    density, own = pl.pallas_call(
        density_kernel,
        out_shape=[shape(C_DEV, CAP), shape(2, C_DEV, CAP, CAP)],
        in_specs=[smem] + [vmem] * 4,
        out_specs=[vmem] * 2,
        scratch_shapes=[
            floats(NB, 8, CAP), floats(NB, 8, CAP), floats(GROUP, CAP), floats(2, GROUP, CAP),
        ],
        compiler_params=pltpu.CompilerParams(vmem_limit_bytes=limit),
    )(plan, table, targets, rank, density_old)
    derived, offsets = pl.pallas_call(
        functools.partial(moving_kernel, regions, planes),
        out_shape=[shape(size, 8, CAP), shape(C_DEV, CAP, dtype=jnp.int32)],
        in_specs=[smem] + [vmem] * 4,
        out_specs=[vmem] * 2,
        scratch_shapes=[
            floats(size, 1, CAP), floats(C_DEV, 1, CAP),
            floats(planes * PLANE - 1, 2, 1, CAP), dma((4,)), dma((2,)),
        ],
        compiler_params=pltpu.CompilerParams(
            collective_id=1, has_side_effects=True, vmem_limit_bytes=limit
        ),
    )(exports, density, table, sounds, plan)
    acceleration, kicked, density = pl.pallas_call(
        force_kernel,
        out_shape=[shape(3, C_DEV, CAP), shape(3, C_DEV, CAP), shape(C_DEV, CAP)],
        in_specs=[smem] * 2 + [vmem] * 8,
        out_specs=[vmem] * 3,
        scratch_shapes=[
            floats(NB, 8, CAP), floats(ROWS, 8, CAP), floats(ROWS, 8, CAP),
            floats(3, GROUP, CAP), floats(3, GROUP, CAP),
        ],
        compiler_params=pltpu.CompilerParams(vmem_limit_bytes=limit),
    )(plan, offsets, table, derived, targets, own, rank, velocity, time_bin, density)
    return density, acceleration, kicked


def solution(mesh):
    both = ("region", "cell")
    flat, wide_rows = P(both, None), P(None, both, None)
    return jax.shard_map(
        functools.partial(shards, mesh.shape["region"], mesh.shape["cell"] // PLANE),
        mesh=mesh,
        in_specs=(
            wide_rows, wide_rows, flat, flat, flat, flat, P(both), flat, flat, flat, flat, flat,
        ),
        out_specs=(flat, wide_rows, wide_rows),
        check_vma=False,
    )
```

```python
import functools
import math

import jax
import jax.numpy as jnp
from jax import lax
from jax.experimental import pallas as pl
from jax.experimental.pallas import tpu as pltpu
from jax.sharding import PartitionSpec as P

MESH = pl.DeviceIdType.MESH
C_DEV = 8
CAP = 128
NB = 27
GROUP = 8
PLANE = 8
ORDER = (1, 7, 4, 2, 6, 3, 5)
EARLY = 6
BATCH = 2
ADIABATIC = 5.0 / 3.0
STEP_MAX = 0.2
TINY = 1e-30
F32 = jnp.float32
SHIFT_AT, GROUP_AT = 32, 64
SIZES = (8, 12, 15, 16, 17, 18, 19, 20, 22, 24, 27)
ROWS = NB + 8
X, Y, Z, INVERSE, VX, VY, VZ, SECOND, THIRD, SMALL, SOUND, HEAT = range(12)
TARGET = 12
SOUND_UNIT = 0.025
DENSITY_UNIT = 1.0 / 400.0


def place():
    r, c = lax.axis_index("region"), lax.axis_index("cell")
    return r, lax.div(c, PLANE), lax.rem(c, PLANE)


def along(z, u, planes, ahead):
    return lax.rem(z + ahead, planes) * PLANE + u


def across(z, u, ahead):
    return z * PLANE + lax.rem(u + ahead, PLANE)


def greet(regions, planes):
    r, z, u = place()
    barrier = pltpu.get_barrier_semaphore()
    for ahead in sorted(range(1, planes), key=lambda a: -min(a, planes - a)):
        pl.semaphore_signal(
            barrier, inc=1, device_id=(r, along(z, u, planes, ahead)), device_id_type=MESH
        )
    for ahead in range(1, PLANE):
        pl.semaphore_signal(
            barrier, inc=1, device_id=(r, across(z, u, ahead)), device_id_type=MESH
        )
    for ahead in (1, regions - 1):
        pl.semaphore_signal(
            barrier, inc=1, device_id=(lax.rem(r + ahead, regions), z * PLANE + u),
            device_id_type=MESH,
        )
    return lambda: pl.semaphore_wait(barrier, planes + PLANE)


def region_copies(regions, cells, table, sems, first):
    r, z, u = place()
    size = table.shape[0]
    up = pltpu.make_async_remote_copy(
        src_ref=cells.at[pl.ds(C_DEV - 1, 1)],
        dst_ref=table.at[pl.ds(size - 2, 1)],
        send_sem=sems.at[first + 0],
        recv_sem=sems.at[first + 1],
        device_id=(lax.rem(r + 1, regions), z * PLANE + u),
        device_id_type=MESH,
    )
    down = pltpu.make_async_remote_copy(
        src_ref=cells.at[pl.ds(0, 1)],
        dst_ref=table.at[pl.ds(size - 1, 1)],
        send_sem=sems.at[first + 2],
        recv_sem=sems.at[first + 3],
        device_id=(lax.rem(r + regions - 1, regions), z * PLANE + u),
        device_id_type=MESH,
    )
    return up, down


def send_along(planes, ahead, source, target, send_sem, recv_sem):
    r, z, u = place()
    return pltpu.make_async_remote_copy(
        src_ref=source, dst_ref=target, send_sem=send_sem, recv_sem=recv_sem,
        device_id=(r, along(z, u, planes, ahead)), device_id_type=MESH,
    )


def send_across(first, slots, planes, outbox, table, send_sem, recv_sem):
    r, z, u = place()
    rows = 2 * slots

    for ahead in (4, 3, 5, 2, 6, 1, 7):
        to = lax.rem(u + ahead, PLANE)
        pltpu.make_async_remote_copy(
            src_ref=outbox.at[to, pl.ds(2 * first, rows)],
            dst_ref=table.at[pl.ds(C_DEV + 2 * planes * u + 2 * first, rows)],
            send_sem=send_sem, recv_sem=recv_sem,
            device_id=(r, z * PLANE + to), device_id_type=MESH,
        ).start()


def choose(slot, export, cells, outbox):
    r, z, u = place()

    def fill(to, carry):
        for q in range(2):
            outbox[to, 2 * slot + q] = cells[export[slot, q, z * PLANE + to]]
        return carry

    lax.fori_loop(0, PLANE, fill, 0, unroll=True)


def keep_own(planes, cells, outbox, table):
    r, z, u = place()
    for k in range(C_DEV):
        table[k] = cells[k]
    for i in range(2 * planes):
        table[C_DEV + 2 * planes * u + i] = outbox[u, i]


def drain(planes, outbox, table, send_sem, recv_sem):
    sent = outbox.at[pl.ds(0, PLANE - 1)]
    pltpu.make_async_copy(sent, sent, send_sem).wait()
    landed = table.at[pl.ds(0, 2 * planes * (PLANE - 1))]
    pltpu.make_async_copy(landed, landed, recv_sem).wait()


def static_kernel(
    regions, planes,
    position, velocity, smoothing, mass, energy, active, count, export, source, shift, old,
    table, sounds, targets, rank, plan, exports, old_v,
    energy_v, position_v, velocity_v, smoothing_v, mass_v, active_v, count_s, source_v, shift_v,
    cells, exports_s, outbox, *rest,
):
    land, (
        sound_land, sound_outbox,
        fetch_sems, region_sems, export_sems, along_send, along_recv, across_sems, own_sem,
        sound_sems, own_s, list_sem,
    ) = rest[: planes - 1], rest[planes - 1 :]
    wait_for_all = greet(regions, planes)
    fetches = [
        pltpu.make_async_copy(a, b, fetch_sems.at[i])
        for i, (a, b) in enumerate((
            (position, position_v), (smoothing, smoothing_v), (mass, mass_v), (count, count_s),
            (velocity, velocity_v), (export, exports.at[0]), (energy, energy_v),
            (active, active_v), (source, source_v), (shift, shift_v), (old, old_v),
        ))
    ]
    for fetch in fetches:
        fetch.start()
    for fetch in fetches:
        fetch.wait()
    slot = lax.broadcasted_iota(jnp.int32, (1, CAP), 1)
    for k in range(C_DEV):
        for i in range(3):
            cells[k, i : i + 1] = position_v[i, k : k + 1]
            cells[k, 5 + i : 6 + i] = velocity_v[i, k : k + 1]
        cells[k, 3:4] = jnp.where(slot < count_s[k], mass_v[k : k + 1], 0.0)
        cells[k, 4:5] = smoothing_v[k : k + 1]
        heat = (ADIABATIC * (ADIABATIC - 1.0)) * energy_v[k : k + 1]
        sound_land[0, k] = SOUND_UNIT * jnp.sqrt(heat)
    wait_for_all()
    regionals = region_copies(regions, cells, table, region_sems, 0) + region_copies(
        regions, sound_land.at[0], sounds, region_sems, 4
    )
    calls = [
        send_along(
            planes, ahead, sound_land.at[0], sound_land.at[i + 1], sound_sems.at[0],
            sound_sems.at[1],
        )
        for i, ahead in enumerate(ORDER)
    ]
    lists = [
        send_along(
            planes, ahead, exports.at[0], exports.at[i + 1], export_sems.at[0], export_sems.at[1]
        )
        for i, ahead in enumerate(ORDER)
    ]
    blocks = [
        send_along(planes, ahead, cells, land[i], along_send.at[i], along_recv.at[i])
        for i, ahead in enumerate(ORDER)
    ]
    own_list = pltpu.make_async_copy(exports.at[pl.ds(0, 1)], own_s, list_sem)
    own_list.start()
    for copy in lists + calls + blocks[:2] + list(regionals) + blocks[2:]:
        copy.start()

    live = active_v[...] > 0
    row = lax.broadcasted_iota(jnp.int32, (CAP, CAP), 0)
    col = lax.broadcasted_iota(jnp.int32, (CAP, CAP), 1)
    upper = jnp.where(row <= col, 1.0, 0.0)
    ordinal = jnp.dot(jnp.where(live, 1.0, 0.0), upper, preferred_element_type=F32)
    where_to = jnp.where(live, ordinal - 1.0, -1000.0)
    rank[...] = where_to
    groups = (jnp.sum(active_v[...], axis=1, keepdims=True) + (GROUP - 1)) // GROUP
    r, z, u = place()
    named = source_v[...]
    other = named - C_DEV
    behind = jnp.bitwise_and(z + planes - jnp.right_shift(other, 4), planes - 1)
    slot_of = jnp.zeros_like(behind)
    for i, ahead in enumerate(ORDER):
        slot_of = jnp.where(behind == ahead, i + 1, slot_of)
    peer = jnp.bitwise_and(jnp.right_shift(other, 1), PLANE - 1)
    moved = C_DEV + 2 * planes * peer + 2 * slot_of + jnp.bitwise_and(other, 1)
    inside = jnp.logical_and(named >= C_DEV, named < C_DEV + 2 * planes * PLANE)
    plan[:, 0:NB] = jnp.where(inside, moved, named)
    plan[:, SHIFT_AT : SHIFT_AT + NB] = shift_v[...]
    plan[:, GROUP_AT : GROUP_AT + 1] = groups

    sub = lax.broadcasted_iota(jnp.int32, (8, CAP), 0)

    def compact(k):
        fields = jnp.where(sub == 3, energy_v[k : k + 1], cells[k])
        picked = jnp.where(where_to[k : k + 1] == row.astype(F32), 1.0, 0.0)
        found = lax.dot_general(
            picked, fields, (((1,), (1,)), ((), ())),
            precision=lax.Precision.HIGHEST, preferred_element_type=F32,
        )
        x, y, z, e, h, vx, vy, vz = (
            jnp.broadcast_to(found[:, f : f + 1], (CAP, CAP)) for f in range(8)
        )
        inverse = 1.0 / h
        second = inverse * inverse
        for at, value in (
            (X, x), (Y, y), (Z, z), (INVERSE, inverse), (VX, vx), (VY, vy), (VZ, vz),
            (SECOND, second), (THIRD, 0.5 * second * inverse), (SMALL, 0.05 * h),
            (SOUND, SOUND_UNIT * jnp.sqrt(ADIABATIC * (ADIABATIC - 1.0) * e)),
            (HEAT, (ADIABATIC - 1.0) * e),
        ):
            targets[at, k] = value

    for k in range(EARLY):
        compact(k)
    own_list.wait()
    choose(0, own_s, cells, outbox)
    drained = exports.at[pl.ds(1, planes - 1)]
    pltpu.make_async_copy(drained, drained, export_sems.at[1]).wait()
    pltpu.make_async_copy(drained, drained, export_sems.at[0]).wait()
    to_scalar = pltpu.make_async_copy(exports, exports_s, own_sem)
    to_scalar.start()
    to_scalar.wait()
    heard = sound_land.at[pl.ds(1, planes - 1)]
    pltpu.make_async_copy(heard, heard, sound_sems.at[1]).wait()
    for slot in range(planes):
        choose(slot, exports_s, sound_land.at[slot], sound_outbox)
    send_across(0, planes, planes, sound_outbox, sounds, sound_sems.at[2], sound_sems.at[3])
    for i in range(planes - 1):
        if i + EARLY < C_DEV:
            compact(i + EARLY)
        blocks[i].wait_recv()
        choose(i + 1, exports_s, land[i], outbox)
        if (i + 2) % BATCH == 0:
            send_across(
                i + 2 - BATCH, BATCH, planes, outbox, table, across_sems.at[0], across_sems.at[1]
            )
    keep_own(planes, cells, outbox, table)
    keep_own(planes, sound_land.at[0], sound_outbox, sounds)
    for copy in regionals:
        copy.wait()
    for copy in blocks:
        copy.wait_send()
    pltpu.make_async_copy(heard, heard, sound_sems.at[0]).wait()
    drain(planes, sound_outbox, sounds, sound_sems.at[2], sound_sems.at[3])
    drain(planes, outbox, table, across_sems.at[0], across_sems.at[1])


def offsets_of(table, plan):
    size = table.shape[0]
    ones = jnp.ones((8, CAP), F32)
    lane = lax.broadcasted_iota(jnp.int32, (8, CAP), 1)
    row = lax.broadcasted_iota(jnp.int32, (CAP, CAP), 0)
    col = lax.broadcasted_iota(jnp.int32, (CAP, CAP), 1)
    named = jnp.where(lane < NB, plan[...], -1)
    held = []
    for start in range(0, size, CAP):
        stop = min(start + CAP, size)
        live = jnp.where(table[start:stop, 3, :] > 0.0, 1.0, 0.0)
        if stop - start < CAP:
            live = jnp.concatenate([live, jnp.zeros((CAP - (stop - start), CAP), F32)], axis=0)
        held.append(
            lax.dot_general(ones, live, (((1,), (1,)), ((), ())), preferred_element_type=F32)
        )
    lines = []
    for k in range(C_DEV):
        line = jnp.zeros((8, CAP), F32)
        for i, counts in enumerate(held):
            same = jnp.where(named[k : k + 1] == row + i * CAP, 1.0, 0.0)
            line += jnp.dot(counts, same, preferred_element_type=F32)
        lines.append(line[0:1])
    before = jnp.where(row < col, 1.0, 0.0)
    return jnp.dot(jnp.concatenate(lines, axis=0), before, preferred_element_type=F32)


def by_distance(planes):
    others = [(i, j) for i in range(planes) for j in range(PLANE) if (i, j) != (0, 0)]

    def hops(other):
        return min(other[0], planes - other[0]) + min(other[1] // 2, (PLANE - other[1] + 1) // 2)

    return sorted(others, key=lambda other: -hops(other))


def moving_kernel(
    regions, planes, exports, density, sources, sounds, plan, derived, offsets,
    table, cells, outbox, region_sems, sems,
):
    r, z, u = place()
    others = by_distance(planes)
    barrier = pltpu.get_barrier_semaphore()

    def at(other):
        return lax.rem(z + other[0], planes) * PLANE + lax.rem(u + other[1], PLANE)

    for other in others:
        pl.semaphore_signal(barrier, inc=1, device_id=(r, at(other)), device_id_type=MESH)
    for ahead in (1, regions - 1):
        pl.semaphore_signal(
            barrier, inc=1, device_id=(lax.rem(r + ahead, regions), z * PLANE + u),
            device_id_type=MESH,
        )
    for k in range(C_DEV):
        cells[k] = DENSITY_UNIT * density[k : k + 1]
    for i, other in enumerate(others):
        for q in range(2):
            outbox[i, q] = cells[exports[0, q, at(other)]]
    pl.semaphore_wait(barrier, planes * PLANE + 1)
    for i, other in enumerate(others):
        slot = ((0,) + ORDER).index(other[0])
        pltpu.make_async_remote_copy(
            src_ref=outbox.at[i],
            dst_ref=table.at[pl.ds(C_DEV + 2 * planes * u + 2 * slot, 2)],
            send_sem=sems.at[0], recv_sem=sems.at[1],
            device_id=(r, at(other)), device_id_type=MESH,
        ).start()
    regionals = region_copies(regions, cells, table, region_sems, 0)
    for copy in regionals:
        copy.start()
    for k in range(C_DEV):
        table[k] = cells[k]
    for q in range(2):
        table[C_DEV + 2 * planes * u + q] = cells[exports[0, q, z * PLANE + u]]

    def prepare(s, carry):
        h, m = sources[s, 4:5], sources[s, 3:4]
        inverse = 1.0 / h
        second = inverse * inverse
        derived[s, 0:1] = second
        derived[s, 1:2] = 0.5 * second * inverse
        derived[s, 2:3] = 0.05 * h
        derived[s, 3:4] = m * (1.5 / math.pi)
        sound = sounds[s]
        derived[s, 5:6] = sound
        derived[s, 7:8] = (4.0 / ADIABATIC) * (sound * sound)
        return carry

    lax.fori_loop(0, table.shape[0], prepare, 0, unroll=6)
    offsets[...] = offsets_of(sources, plan).astype(jnp.int32)
    for copy in regionals:
        copy.wait()
    pltpu.make_async_copy(outbox, outbox, sems.at[0]).wait()
    landed = table.at[pl.ds(0, 2 * len(others))]
    pltpu.make_async_copy(landed, landed, sems.at[1]).wait()

    def complete(s, carry):
        thin = table[s]
        derived[s, 4:5] = derived[s, 7:8] / thin
        derived[s, 6:7] = thin
        return carry

    lax.fori_loop(0, table.shape[0], complete, 0, unroll=6)


def fill_shifts(shifts):
    sub = lax.broadcasted_iota(jnp.int32, (8, CAP), 0)
    for s in range(NB):
        offset = (s // 9 - 1, s // 3 % 3 - 1, s % 3 - 1)
        shifts[s] = jnp.where(
            sub == 0, float(offset[0]),
            jnp.where(sub == 1, float(offset[1]), jnp.where(sub == 2, float(offset[2]), 0.0)),
        )


def pack(plan, offsets, k, blocks_of, deads, packed):
    lane = lax.broadcasted_iota(jnp.int32, (8, CAP), 1)
    current = deads
    for n in range(NB):
        at, end = offsets[k, n], offsets[k, n + 1]
        row, first = lax.shift_right_logical(at, 7), lax.bitwise_and(at, CAP - 1)
        kept = lane < first
        spilled = lax.shift_right_logical(end, 7) > row
        rolled = [pltpu.roll(block, first, 1) for block in blocks_of(plan[k, n], n)]
        current = [jnp.where(kept, old, new) for old, new in zip(current, rolled)]
        for ref, value in zip(packed, current):
            ref[row] = value
        current = [jnp.where(spilled, new, old) for old, new in zip(current, rolled)]
    at = offsets[k, NB]
    row, first = lax.shift_right_logical(at, 7), lax.bitwise_and(at, CAP - 1)
    for ref, value, dead in zip(packed, current, deads):
        ref[row] = jnp.where(lane < first, value, dead)
        for i in range(1, 8):
            ref[row + i] = dead
    return lax.shift_right_logical(at + CAP - 1, 7)


def by_size(rows, run, sizes=SIZES):
    if len(sizes) == 1:
        run(sizes[0])
        return
    half = len(sizes) // 2
    fits = rows <= sizes[half - 1]
    pl.when(fits)(lambda: by_size(rows, run, sizes[:half]))
    pl.when(jnp.logical_not(fits))(lambda: by_size(rows, run, sizes[half:]))


def density_kernel(
    plan, table, targets, rank, density_old,
    density, own,
    shifts, near, total, left,
):
    fill_shifts(shifts)
    sub = lax.broadcasted_iota(jnp.int32, (GROUP, CAP), 0)
    cube = 4.0 ** (-1.0 / 3.0)
    none = jnp.zeros((GROUP, CAP), F32)
    total[...] = none
    left[0] = left[1] = none

    def finish(k, g, partial, norm):
        found = jnp.sum(partial, axis=1, keepdims=True) * norm
        at = pl.multiple_of(jnp.maximum(g, 0) * GROUP, GROUP)
        own[0, k, pl.ds(at, GROUP), :] = targets[HEAT, k, pl.ds(at, GROUP), :] / found
        own[1, k, pl.ds(at, GROUP), :] = jnp.broadcast_to(found, (GROUP, CAP)) * DENSITY_UNIT
        here = rank[pl.ds(k, 1), :] == (sub + g * GROUP).astype(F32)
        return jnp.where(here, found, 0.0)

    def settle(k):
        last = finish(k, plan[k, GROUP_AT] - 1, left[0], left[1])
        summed = jnp.sum(total[...] + last, axis=0, keepdims=True)
        mine = pl.ds(k, 1)
        density[mine, :] = jnp.where(rank[mine, :] >= 0.0, summed, density_old[mine, :])
        total[...] = none

    def cell(k, carry):
        settle(jnp.maximum(k - 1, 0))
        for n in range(NB):
            near[n] = table[plan[k, n]] + shifts[plan[k, SHIFT_AT + n]]

        def setup(g):
            at = pl.multiple_of(jnp.minimum(g, CAP // GROUP - 1) * GROUP, GROUP)
            return tuple(targets[f, k, pl.ds(at, GROUP), :] for f in (X, Y, Z, INVERSE))

        def group(g, carry):
            (x, y, z, inverse), partial, norm = carry
            total[...] += finish(k, g - 1, partial, norm)
            following = setup(g + 1)
            scaled = cube * inverse
            partial = none
            for n in range(NB):
                dx, dy, dz = x - near[n, 0:1], y - near[n, 1:2], z - near[n, 2:3]
                square = jnp.maximum(dx * dx + dy * dy + dz * dz, TINY)
                radius = square * lax.rsqrt(square)
                outer = jnp.maximum(2.0 * cube - radius * scaled, 0.0)
                inner = jnp.maximum(1.0 - radius * inverse, 0.0)
                value = outer * outer * outer - inner * inner * inner
                partial += near[n, 3:4] * value
            return following, partial, inverse * inverse * inverse * (1.0 / math.pi)

        _, left[0], left[1] = lax.fori_loop(
            0, plan[k, GROUP_AT], group, (setup(0), none, none)
        )
        return carry

    lax.fori_loop(0, C_DEV, cell, 0)
    settle(C_DEV - 1)


def force_kernel(
    plan, offsets, table, derived, targets, own, rank, velocity, time_bin, density_in,
    acceleration, kicked, density, shifts, near, more, total, left,
):
    density[...] = density_in[...]
    sub = lax.broadcasted_iota(jnp.int32, (GROUP, CAP), 0)
    none = jnp.zeros((GROUP, CAP), F32)
    for i in range(3):
        total[i] = left[i] = none

    fill_shifts(shifts)
    deads = [table[0], jnp.where(sub == 3, 0.0, derived[0])]

    def finish(k, g, parts):
        here = rank[pl.ds(k, 1), :] == (sub + g * GROUP).astype(F32)
        return [
            jnp.where(here, jnp.sum(part, axis=1, keepdims=True), 0.0) for part in parts
        ]

    def settle(k):
        last = finish(k, plan[k, GROUP_AT] - 1, [left[i] for i in range(3)])
        mine = pl.ds(k, 1)
        step = STEP_MAX * jnp.exp2(-time_bin[mine, :].astype(F32))
        for i in range(3):
            found = jnp.sum(total[i] + last[i], axis=0, keepdims=True)
            acceleration[i, mine, :] = found
            kicked[i, mine, :] = velocity[i, mine, :] + found * step
            total[i] = none

    def cell(k, carry):
        settle(jnp.maximum(k - 1, 0))
        rows = pack(
            plan, offsets, k,
            lambda s, n: (table[s] + shifts[plan[k, SHIFT_AT + n]], derived[s]),
            deads, (near, more),
        )

        def setup(g):
            at = pl.multiple_of(jnp.minimum(g, CAP // GROUP - 1) * GROUP, GROUP)
            columns = (X, Y, Z, VX, VY, VZ, SECOND, THIRD, SMALL, SOUND)
            return tuple(targets[f, k, pl.ds(at, GROUP), :] for f in columns) + tuple(
                own[f, k, pl.ds(at, GROUP), :] for f in range(2)
            )

        def run(size):
            def group(g, carry):
                (x, y, z, vx, vy, vz, second, third, small, sound, press, thin), parts = carry
                for i, found in enumerate(finish(k, g - 1, parts)):
                    total[i] += found
                following = setup(g + 1)
                ax = ay = az = jnp.zeros((GROUP, CAP), F32)
                for n in range(size):
                    dx, dy, dz = x - near[n, 0:1], y - near[n, 1:2], z - near[n, 2:3]
                    square = jnp.maximum(dx * dx + dy * dy + dz * dz, TINY)
                    over = lax.rsqrt(square)
                    radius = square * over
                    half = radius * third
                    outer = second - half
                    inner = jnp.maximum(outer - half, 0.0)
                    outer = jnp.maximum(outer, 0.0)
                    slope = outer * outer - inner * inner
                    half = radius * more[n, 1:2]
                    outer = more[n, 0:1] - half
                    inner = jnp.maximum(outer - half, 0.0)
                    outer = jnp.maximum(outer, 0.0)
                    slope += outer * outer - inner * inner
                    approach = (
                        (vx - near[n, 5:6]) * dx
                        + (vy - near[n, 6:7]) * dy
                        + (vz - near[n, 7:8]) * dz
                    )
                    mean = small + more[n, 2:3]
                    mu = mean * jnp.minimum(approach, 0.0) * (1.0 / (square + mean * mean))
                    viscous = mu * (mu - (sound + more[n, 5:6])) * (1.0 / (thin + more[n, 6:7]))
                    weight = more[n, 3:4] * (press + more[n, 4:5] + viscous) * (slope * over)
                    ax += weight * dx
                    ay += weight * dy
                    az += weight * dz
                return following, (ax, ay, az)

            _, parts = lax.fori_loop(
                0, plan[k, GROUP_AT], group, (setup(0), (none, none, none))
            )
            for i in range(3):
                left[i] = parts[i]

        by_size(rows, run)
        return carry

    lax.fori_loop(0, C_DEV, cell, 0)
    settle(C_DEV - 1)


def shards(
    regions, planes,
    position, velocity, smoothing, particle_mass, energy, density_old, cell_count, active,
    time_bin, pair_source, pair_shift, export,
):
    size = C_DEV + 2 * planes * PLANE + 2
    vmem = pl.BlockSpec(memory_space=pltpu.VMEM)
    smem = pl.BlockSpec(memory_space=pltpu.SMEM)
    hbm = pl.BlockSpec(memory_space=pltpu.HBM)
    dma = pltpu.SemaphoreType.DMA

    def shape(*dims, dtype=F32):
        return jax.ShapeDtypeStruct(dims, dtype)

    def ints(*dims):
        return pltpu.VMEM(dims, jnp.int32)

    def floats(*dims):
        return pltpu.VMEM(dims, F32)

    limit = 32 << 20
    table, sounds, targets, rank, plan, exports, density_old = pl.pallas_call(
        functools.partial(static_kernel, regions, planes),
        out_shape=[
            shape(size, 8, CAP), shape(size, 1, CAP), shape(TARGET, C_DEV, CAP, CAP),
            shape(C_DEV, CAP),
            shape(C_DEV, CAP, dtype=jnp.int32),
            shape(planes, 2, planes * PLANE, dtype=jnp.int32), shape(C_DEV, CAP),
        ],
        in_specs=[hbm] * 11,
        out_specs=[vmem] * 7,
        scratch_shapes=[
            floats(C_DEV, CAP), floats(3, C_DEV, CAP), floats(3, C_DEV, CAP), floats(C_DEV, CAP),
            floats(C_DEV, CAP), ints(C_DEV, CAP), pltpu.SMEM((C_DEV,), jnp.int32),
            ints(C_DEV, NB), ints(C_DEV, NB),
            floats(C_DEV, 8, CAP), pltpu.SMEM((planes, 2, planes * PLANE), jnp.int32),
            floats(PLANE, 2 * planes, 8, CAP),
            *[floats(C_DEV, 8, CAP) for _ in range(planes - 1)],
            floats(planes, C_DEV, 1, CAP), floats(PLANE, 2 * planes, 1, CAP),
            dma((11,)), dma((8,)), dma((2,)), dma((planes - 1,)), dma((planes - 1,)), dma((2,)),
            dma, dma((4,)), pltpu.SMEM((1, 2, planes * PLANE), jnp.int32), dma,
        ],
        compiler_params=pltpu.CompilerParams(
            collective_id=0, has_side_effects=True, vmem_limit_bytes=limit
        ),
    )(
        *(
            pltpu.with_memory_space_constraint(x, pltpu.HBM)
            for x in (
                position, velocity, smoothing, particle_mass, energy, active, cell_count, export.T,
                pair_source, pair_shift, density_old,
            )
        )
    )
    density, own = pl.pallas_call(
        density_kernel,
        out_shape=[shape(C_DEV, CAP), shape(2, C_DEV, CAP, CAP)],
        in_specs=[smem] + [vmem] * 4,
        out_specs=[vmem] * 2,
        scratch_shapes=[
            floats(NB, 8, CAP), floats(NB, 8, CAP), floats(GROUP, CAP), floats(2, GROUP, CAP),
        ],
        compiler_params=pltpu.CompilerParams(vmem_limit_bytes=limit),
    )(plan, table, targets, rank, density_old)
    derived, offsets = pl.pallas_call(
        functools.partial(moving_kernel, regions, planes),
        out_shape=[shape(size, 8, CAP), shape(C_DEV, CAP, dtype=jnp.int32)],
        in_specs=[smem] + [vmem] * 4,
        out_specs=[vmem] * 2,
        scratch_shapes=[
            floats(size, 1, CAP), floats(C_DEV, 1, CAP),
            floats(planes * PLANE - 1, 2, 1, CAP), dma((4,)), dma((2,)),
        ],
        compiler_params=pltpu.CompilerParams(
            collective_id=1, has_side_effects=True, vmem_limit_bytes=limit
        ),
    )(exports, density, table, sounds, plan)
    acceleration, kicked, density = pl.pallas_call(
        force_kernel,
        out_shape=[shape(3, C_DEV, CAP), shape(3, C_DEV, CAP), shape(C_DEV, CAP)],
        in_specs=[smem] * 2 + [vmem] * 8,
        out_specs=[vmem] * 3,
        scratch_shapes=[
            floats(NB, 8, CAP), floats(ROWS, 8, CAP), floats(ROWS, 8, CAP),
            floats(3, GROUP, CAP), floats(3, GROUP, CAP),
        ],
        compiler_params=pltpu.CompilerParams(vmem_limit_bytes=limit),
    )(plan, offsets, table, derived, targets, own, rank, velocity, time_bin, density)
    return density, acceleration, kicked


def solution(mesh):
    both = ("region", "cell")
    flat, wide_rows = P(both, None), P(None, both, None)
    return jax.shard_map(
        functools.partial(shards, mesh.shape["region"], mesh.shape["cell"] // PLANE),
        mesh=mesh,
        in_specs=(
            wide_rows, wide_rows, flat, flat, flat, flat, P(both), flat, flat, flat, flat, flat,
        ),
        out_specs=(flat, wide_rows, wide_rows),
        check_vma=False,
    )
```

```python
import functools
import math

import jax
import jax.numpy as jnp
from jax import lax
from jax.experimental import pallas as pl
from jax.experimental.pallas import tpu as pltpu
from jax.sharding import PartitionSpec as P

MESH = pl.DeviceIdType.MESH
C_DEV = 8
CAP = 128
NB = 27
GROUP = 8
PLANE = 8
ORDER = (1, 7, 4, 2, 6, 3, 5)
EARLY = 6
BATCH = 2
ADIABATIC = 5.0 / 3.0
STEP_MAX = 0.2
TINY = 1e-30
F32 = jnp.float32
SHIFT_AT, GROUP_AT = 32, 64
SIZES = (8, 12, 15, 16, 17, 18, 19, 20, 22, 24, 27)
ROWS = NB + 8
X, Y, Z, INVERSE, VX, VY, VZ, SECOND, THIRD, SMALL, SOUND, HEAT = range(12)
TARGET = 12
SOUND_UNIT = 0.025
DENSITY_UNIT = 1.0 / 400.0


def place():
    r, c = lax.axis_index("region"), lax.axis_index("cell")
    return r, lax.div(c, PLANE), lax.rem(c, PLANE)


def along(z, u, planes, ahead):
    return lax.rem(z + ahead, planes) * PLANE + u


def across(z, u, ahead):
    return z * PLANE + lax.rem(u + ahead, PLANE)


def greet(regions, planes):
    r, z, u = place()
    barrier = pltpu.get_barrier_semaphore()
    for ahead in sorted(range(1, planes), key=lambda a: -min(a, planes - a)):
        pl.semaphore_signal(
            barrier, inc=1, device_id=(r, along(z, u, planes, ahead)), device_id_type=MESH
        )
    for ahead in range(1, PLANE):
        pl.semaphore_signal(
            barrier, inc=1, device_id=(r, across(z, u, ahead)), device_id_type=MESH
        )
    for ahead in (1, regions - 1):
        pl.semaphore_signal(
            barrier, inc=1, device_id=(lax.rem(r + ahead, regions), z * PLANE + u),
            device_id_type=MESH,
        )
    return lambda: pl.semaphore_wait(barrier, planes + PLANE)


def region_copies(regions, cells, table, sems, first):
    r, z, u = place()
    size = table.shape[0]
    up = pltpu.make_async_remote_copy(
        src_ref=cells.at[pl.ds(C_DEV - 1, 1)],
        dst_ref=table.at[pl.ds(size - 2, 1)],
        send_sem=sems.at[first + 0],
        recv_sem=sems.at[first + 1],
        device_id=(lax.rem(r + 1, regions), z * PLANE + u),
        device_id_type=MESH,
    )
    down = pltpu.make_async_remote_copy(
        src_ref=cells.at[pl.ds(0, 1)],
        dst_ref=table.at[pl.ds(size - 1, 1)],
        send_sem=sems.at[first + 2],
        recv_sem=sems.at[first + 3],
        device_id=(lax.rem(r + regions - 1, regions), z * PLANE + u),
        device_id_type=MESH,
    )
    return up, down


def send_along(planes, ahead, source, target, send_sem, recv_sem):
    r, z, u = place()
    return pltpu.make_async_remote_copy(
        src_ref=source, dst_ref=target, send_sem=send_sem, recv_sem=recv_sem,
        device_id=(r, along(z, u, planes, ahead)), device_id_type=MESH,
    )


def send_across(first, slots, planes, outbox, table, send_sem, recv_sem):
    r, z, u = place()
    rows = 2 * slots

    for ahead in (4, 3, 5, 2, 6, 1, 7):
        to = lax.rem(u + ahead, PLANE)
        pltpu.make_async_remote_copy(
            src_ref=outbox.at[to, pl.ds(2 * first, rows)],
            dst_ref=table.at[pl.ds(C_DEV + 2 * planes * u + 2 * first, rows)],
            send_sem=send_sem, recv_sem=recv_sem,
            device_id=(r, z * PLANE + to), device_id_type=MESH,
        ).start()


def choose(slot, export, cells, outbox):
    r, z, u = place()

    def fill(to, carry):
        for q in range(2):
            outbox[to, 2 * slot + q] = cells[export[slot, q, z * PLANE + to]]
        return carry

    lax.fori_loop(0, PLANE, fill, 0, unroll=True)


def keep_own(planes, cells, outbox, table):
    r, z, u = place()
    for k in range(C_DEV):
        table[k] = cells[k]
    for i in range(2 * planes):
        table[C_DEV + 2 * planes * u + i] = outbox[u, i]


def drain(planes, outbox, table, send_sem, recv_sem):
    sent = outbox.at[pl.ds(0, PLANE - 1)]
    pltpu.make_async_copy(sent, sent, send_sem).wait()
    landed = table.at[pl.ds(0, 2 * planes * (PLANE - 1))]
    pltpu.make_async_copy(landed, landed, recv_sem).wait()


def static_kernel(
    regions, planes,
    position, velocity, smoothing, mass, energy, active, count, export, source, shift, old,
    table, sounds, targets, rank, plan, exports, old_v,
    energy_v, position_v, velocity_v, smoothing_v, mass_v, active_v, count_s, source_v, shift_v,
    cells, exports_s, outbox, *rest,
):
    land, (
        sound_land, sound_outbox,
        fetch_sems, region_sems, export_sems, along_send, along_recv, across_sems, own_sem,
        sound_sems, own_s, list_sem,
    ) = rest[: planes - 1], rest[planes - 1 :]
    wait_for_all = greet(regions, planes)
    fetches = [
        pltpu.make_async_copy(a, b, fetch_sems.at[i])
        for i, (a, b) in enumerate((
            (position, position_v), (smoothing, smoothing_v), (mass, mass_v), (count, count_s),
            (velocity, velocity_v), (export, exports.at[0]), (energy, energy_v),
            (active, active_v), (source, source_v), (shift, shift_v), (old, old_v),
        ))
    ]
    for fetch in fetches:
        fetch.start()
    for fetch in fetches:
        fetch.wait()
    slot = lax.broadcasted_iota(jnp.int32, (1, CAP), 1)
    for k in range(C_DEV):
        for i in range(3):
            cells[k, i : i + 1] = position_v[i, k : k + 1]
            cells[k, 5 + i : 6 + i] = velocity_v[i, k : k + 1]
        cells[k, 3:4] = jnp.where(slot < count_s[k], mass_v[k : k + 1], 0.0)
        cells[k, 4:5] = smoothing_v[k : k + 1]
        heat = (ADIABATIC * (ADIABATIC - 1.0)) * energy_v[k : k + 1]
        sound_land[0, k] = SOUND_UNIT * jnp.sqrt(heat)
    wait_for_all()
    regionals = region_copies(regions, cells, table, region_sems, 0) + region_copies(
        regions, sound_land.at[0], sounds, region_sems, 4
    )
    calls = [
        send_along(
            planes, ahead, sound_land.at[0], sound_land.at[i + 1], sound_sems.at[0],
            sound_sems.at[1],
        )
        for i, ahead in enumerate(ORDER)
    ]
    lists = [
        send_along(
            planes, ahead, exports.at[0], exports.at[i + 1], export_sems.at[0], export_sems.at[1]
        )
        for i, ahead in enumerate(ORDER)
    ]
    blocks = [
        send_along(planes, ahead, cells, land[i], along_send.at[i], along_recv.at[i])
        for i, ahead in enumerate(ORDER)
    ]
    own_list = pltpu.make_async_copy(exports.at[pl.ds(0, 1)], own_s, list_sem)
    own_list.start()
    for copy in lists + calls:
        copy.start()
    first_core = lax.rem(lax.axis_index("cell"), 2) == 0

    def start_blocks(order):
        for ahead in order:
            blocks[ORDER.index(ahead)].start()

    pl.when(first_core)(lambda: start_blocks(ORDER))
    pl.when(jnp.logical_not(first_core))(lambda: start_blocks([planes - a for a in ORDER]))
    for copy in regionals:
        copy.start()

    live = active_v[...] > 0
    row = lax.broadcasted_iota(jnp.int32, (CAP, CAP), 0)
    col = lax.broadcasted_iota(jnp.int32, (CAP, CAP), 1)
    upper = jnp.where(row <= col, 1.0, 0.0)
    ordinal = jnp.dot(jnp.where(live, 1.0, 0.0), upper, preferred_element_type=F32)
    where_to = jnp.where(live, ordinal - 1.0, -1000.0)
    rank[...] = where_to
    groups = (jnp.sum(active_v[...], axis=1, keepdims=True) + (GROUP - 1)) // GROUP
    r, z, u = place()
    named = source_v[...]
    other = named - C_DEV
    behind = jnp.bitwise_and(z + planes - jnp.right_shift(other, 4), planes - 1)
    slot_of = jnp.zeros_like(behind)
    for i, ahead in enumerate(ORDER):
        slot_of = jnp.where(behind == ahead, i + 1, slot_of)
    peer = jnp.bitwise_and(jnp.right_shift(other, 1), PLANE - 1)
    moved = C_DEV + 2 * planes * peer + 2 * slot_of + jnp.bitwise_and(other, 1)
    inside = jnp.logical_and(named >= C_DEV, named < C_DEV + 2 * planes * PLANE)
    plan[:, 0:NB] = jnp.where(inside, moved, named)
    plan[:, SHIFT_AT : SHIFT_AT + NB] = shift_v[...]
    plan[:, GROUP_AT : GROUP_AT + 1] = groups

    sub = lax.broadcasted_iota(jnp.int32, (8, CAP), 0)

    def compact(k):
        fields = jnp.where(sub == 3, energy_v[k : k + 1], cells[k])
        picked = jnp.where(where_to[k : k + 1] == row.astype(F32), 1.0, 0.0)
        found = lax.dot_general(
            picked, fields, (((1,), (1,)), ((), ())),
            precision=lax.Precision.HIGHEST, preferred_element_type=F32,
        )
        x, y, z, e, h, vx, vy, vz = (
            jnp.broadcast_to(found[:, f : f + 1], (CAP, CAP)) for f in range(8)
        )
        inverse = 1.0 / h
        second = inverse * inverse
        for at, value in (
            (X, x), (Y, y), (Z, z), (INVERSE, inverse), (VX, vx), (VY, vy), (VZ, vz),
            (SECOND, second), (THIRD, 0.5 * second * inverse), (SMALL, 0.05 * h),
            (SOUND, SOUND_UNIT * jnp.sqrt(ADIABATIC * (ADIABATIC - 1.0) * e)),
            (HEAT, (ADIABATIC - 1.0) * e),
        ):
            targets[at, k] = value

    for k in range(EARLY):
        compact(k)
    own_list.wait()
    choose(0, own_s, cells, outbox)
    drained = exports.at[pl.ds(1, planes - 1)]
    pltpu.make_async_copy(drained, drained, export_sems.at[1]).wait()
    pltpu.make_async_copy(drained, drained, export_sems.at[0]).wait()
    to_scalar = pltpu.make_async_copy(exports, exports_s, own_sem)
    to_scalar.start()
    to_scalar.wait()
    heard = sound_land.at[pl.ds(1, planes - 1)]
    pltpu.make_async_copy(heard, heard, sound_sems.at[1]).wait()
    for slot in range(planes):
        choose(slot, exports_s, sound_land.at[slot], sound_outbox)
    send_across(0, planes, planes, sound_outbox, sounds, sound_sems.at[2], sound_sems.at[3])
    for i in range(planes - 1):
        if i + EARLY < C_DEV:
            compact(i + EARLY)
        blocks[i].wait_recv()
        choose(i + 1, exports_s, land[i], outbox)
        if (i + 2) % BATCH == 0:
            send_across(
                i + 2 - BATCH, BATCH, planes, outbox, table, across_sems.at[0], across_sems.at[1]
            )
    keep_own(planes, cells, outbox, table)
    keep_own(planes, sound_land.at[0], sound_outbox, sounds)
    for copy in regionals:
        copy.wait()
    for copy in blocks:
        copy.wait_send()
    pltpu.make_async_copy(heard, heard, sound_sems.at[0]).wait()
    drain(planes, sound_outbox, sounds, sound_sems.at[2], sound_sems.at[3])
    drain(planes, outbox, table, across_sems.at[0], across_sems.at[1])


def offsets_of(table, plan):
    size = table.shape[0]
    ones = jnp.ones((8, CAP), F32)
    lane = lax.broadcasted_iota(jnp.int32, (8, CAP), 1)
    row = lax.broadcasted_iota(jnp.int32, (CAP, CAP), 0)
    col = lax.broadcasted_iota(jnp.int32, (CAP, CAP), 1)
    named = jnp.where(lane < NB, plan[...], -1)
    held = []
    for start in range(0, size, CAP):
        stop = min(start + CAP, size)
        live = jnp.where(table[start:stop, 3, :] > 0.0, 1.0, 0.0)
        if stop - start < CAP:
            live = jnp.concatenate([live, jnp.zeros((CAP - (stop - start), CAP), F32)], axis=0)
        held.append(
            lax.dot_general(ones, live, (((1,), (1,)), ((), ())), preferred_element_type=F32)
        )
    lines = []
    for k in range(C_DEV):
        line = jnp.zeros((8, CAP), F32)
        for i, counts in enumerate(held):
            same = jnp.where(named[k : k + 1] == row + i * CAP, 1.0, 0.0)
            line += jnp.dot(counts, same, preferred_element_type=F32)
        lines.append(line[0:1])
    before = jnp.where(row < col, 1.0, 0.0)
    return jnp.dot(jnp.concatenate(lines, axis=0), before, preferred_element_type=F32)


def by_distance(planes):
    others = [(i, j) for i in range(planes) for j in range(PLANE) if (i, j) != (0, 0)]

    def hops(other):
        return min(other[0], planes - other[0]) + min(other[1] // 2, (PLANE - other[1] + 1) // 2)

    return sorted(others, key=lambda other: -hops(other))


def moving_kernel(
    regions, planes, exports, density, sources, sounds, plan, derived, offsets,
    table, cells, outbox, region_sems, sems,
):
    r, z, u = place()
    others = by_distance(planes)
    barrier = pltpu.get_barrier_semaphore()

    def at(other):
        return lax.rem(z + other[0], planes) * PLANE + lax.rem(u + other[1], PLANE)

    for other in others:
        pl.semaphore_signal(barrier, inc=1, device_id=(r, at(other)), device_id_type=MESH)
    for ahead in (1, regions - 1):
        pl.semaphore_signal(
            barrier, inc=1, device_id=(lax.rem(r + ahead, regions), z * PLANE + u),
            device_id_type=MESH,
        )
    for k in range(C_DEV):
        cells[k] = DENSITY_UNIT * density[k : k + 1]
    for i, other in enumerate(others):
        for q in range(2):
            outbox[i, q] = cells[exports[0, q, at(other)]]
    pl.semaphore_wait(barrier, planes * PLANE + 1)
    for i, other in enumerate(others):
        slot = ((0,) + ORDER).index(other[0])
        pltpu.make_async_remote_copy(
            src_ref=outbox.at[i],
            dst_ref=table.at[pl.ds(C_DEV + 2 * planes * u + 2 * slot, 2)],
            send_sem=sems.at[0], recv_sem=sems.at[1],
            device_id=(r, at(other)), device_id_type=MESH,
        ).start()
    regionals = region_copies(regions, cells, table, region_sems, 0)
    for copy in regionals:
        copy.start()
    for k in range(C_DEV):
        table[k] = cells[k]
    for q in range(2):
        table[C_DEV + 2 * planes * u + q] = cells[exports[0, q, z * PLANE + u]]

    def prepare(s, carry):
        h, m = sources[s, 4:5], sources[s, 3:4]
        inverse = 1.0 / h
        second = inverse * inverse
        derived[s, 0:1] = second
        derived[s, 1:2] = 0.5 * second * inverse
        derived[s, 2:3] = 0.05 * h
        derived[s, 3:4] = m * (1.5 / math.pi)
        sound = sounds[s]
        derived[s, 5:6] = sound
        derived[s, 7:8] = (4.0 / ADIABATIC) * (sound * sound)
        return carry

    lax.fori_loop(0, table.shape[0], prepare, 0, unroll=6)
    offsets[...] = offsets_of(sources, plan).astype(jnp.int32)
    for copy in regionals:
        copy.wait()
    pltpu.make_async_copy(outbox, outbox, sems.at[0]).wait()
    landed = table.at[pl.ds(0, 2 * len(others))]
    pltpu.make_async_copy(landed, landed, sems.at[1]).wait()

    def complete(s, carry):
        thin = table[s]
        derived[s, 4:5] = derived[s, 7:8] / thin
        derived[s, 6:7] = thin
        return carry

    lax.fori_loop(0, table.shape[0], complete, 0, unroll=6)


def fill_shifts(shifts):
    sub = lax.broadcasted_iota(jnp.int32, (8, CAP), 0)
    for s in range(NB):
        offset = (s // 9 - 1, s // 3 % 3 - 1, s % 3 - 1)
        shifts[s] = jnp.where(
            sub == 0, float(offset[0]),
            jnp.where(sub == 1, float(offset[1]), jnp.where(sub == 2, float(offset[2]), 0.0)),
        )


def pack(plan, offsets, k, blocks_of, deads, packed):
    lane = lax.broadcasted_iota(jnp.int32, (8, CAP), 1)
    current = deads
    for n in range(NB):
        at, end = offsets[k, n], offsets[k, n + 1]
        row, first = lax.shift_right_logical(at, 7), lax.bitwise_and(at, CAP - 1)
        kept = lane < first
        spilled = lax.shift_right_logical(end, 7) > row
        rolled = [pltpu.roll(block, first, 1) for block in blocks_of(plan[k, n], n)]
        current = [jnp.where(kept, old, new) for old, new in zip(current, rolled)]
        for ref, value in zip(packed, current):
            ref[row] = value
        current = [jnp.where(spilled, new, old) for old, new in zip(current, rolled)]
    at = offsets[k, NB]
    row, first = lax.shift_right_logical(at, 7), lax.bitwise_and(at, CAP - 1)
    for ref, value, dead in zip(packed, current, deads):
        ref[row] = jnp.where(lane < first, value, dead)
        for i in range(1, 8):
            ref[row + i] = dead
    return lax.shift_right_logical(at + CAP - 1, 7)


def by_size(rows, run, sizes=SIZES):
    if len(sizes) == 1:
        run(sizes[0])
        return
    half = len(sizes) // 2
    fits = rows <= sizes[half - 1]
    pl.when(fits)(lambda: by_size(rows, run, sizes[:half]))
    pl.when(jnp.logical_not(fits))(lambda: by_size(rows, run, sizes[half:]))


def density_kernel(
    plan, table, targets, rank, density_old,
    density, own,
    shifts, near, total, left,
):
    fill_shifts(shifts)
    sub = lax.broadcasted_iota(jnp.int32, (GROUP, CAP), 0)
    cube = 4.0 ** (-1.0 / 3.0)
    none = jnp.zeros((GROUP, CAP), F32)
    total[...] = none
    left[0] = left[1] = none

    def finish(k, g, partial, norm):
        found = jnp.sum(partial, axis=1, keepdims=True) * norm
        at = pl.multiple_of(jnp.maximum(g, 0) * GROUP, GROUP)
        own[0, k, pl.ds(at, GROUP), :] = targets[HEAT, k, pl.ds(at, GROUP), :] / found
        own[1, k, pl.ds(at, GROUP), :] = jnp.broadcast_to(found, (GROUP, CAP)) * DENSITY_UNIT
        here = rank[pl.ds(k, 1), :] == (sub + g * GROUP).astype(F32)
        return jnp.where(here, found, 0.0)

    def settle(k):
        last = finish(k, plan[k, GROUP_AT] - 1, left[0], left[1])
        summed = jnp.sum(total[...] + last, axis=0, keepdims=True)
        mine = pl.ds(k, 1)
        density[mine, :] = jnp.where(rank[mine, :] >= 0.0, summed, density_old[mine, :])
        total[...] = none

    def cell(k, carry):
        settle(jnp.maximum(k - 1, 0))
        for n in range(NB):
            near[n] = table[plan[k, n]] + shifts[plan[k, SHIFT_AT + n]]

        def setup(g):
            at = pl.multiple_of(jnp.minimum(g, CAP // GROUP - 1) * GROUP, GROUP)
            return tuple(targets[f, k, pl.ds(at, GROUP), :] for f in (X, Y, Z, INVERSE))

        def group(g, carry):
            (x, y, z, inverse), partial, norm = carry
            total[...] += finish(k, g - 1, partial, norm)
            following = setup(g + 1)
            scaled = cube * inverse
            partial = none
            for n in range(NB):
                dx, dy, dz = x - near[n, 0:1], y - near[n, 1:2], z - near[n, 2:3]
                square = jnp.maximum(dx * dx + dy * dy + dz * dz, TINY)
                radius = square * lax.rsqrt(square)
                outer = jnp.maximum(2.0 * cube - radius * scaled, 0.0)
                inner = jnp.maximum(1.0 - radius * inverse, 0.0)
                value = outer * outer * outer - inner * inner * inner
                partial += near[n, 3:4] * value
            return following, partial, inverse * inverse * inverse * (1.0 / math.pi)

        _, left[0], left[1] = lax.fori_loop(
            0, plan[k, GROUP_AT], group, (setup(0), none, none)
        )
        return carry

    lax.fori_loop(0, C_DEV, cell, 0)
    settle(C_DEV - 1)


def force_kernel(
    plan, offsets, table, derived, targets, own, rank, velocity, time_bin, density_in,
    acceleration, kicked, density, shifts, near, more, total, left,
):
    density[...] = density_in[...]
    sub = lax.broadcasted_iota(jnp.int32, (GROUP, CAP), 0)
    none = jnp.zeros((GROUP, CAP), F32)
    for i in range(3):
        total[i] = left[i] = none

    fill_shifts(shifts)
    deads = [table[0], jnp.where(sub == 3, 0.0, derived[0])]

    def finish(k, g, parts):
        here = rank[pl.ds(k, 1), :] == (sub + g * GROUP).astype(F32)
        return [
            jnp.where(here, jnp.sum(part, axis=1, keepdims=True), 0.0) for part in parts
        ]

    def settle(k):
        last = finish(k, plan[k, GROUP_AT] - 1, [left[i] for i in range(3)])
        mine = pl.ds(k, 1)
        step = STEP_MAX * jnp.exp2(-time_bin[mine, :].astype(F32))
        for i in range(3):
            found = jnp.sum(total[i] + last[i], axis=0, keepdims=True)
            acceleration[i, mine, :] = found
            kicked[i, mine, :] = velocity[i, mine, :] + found * step
            total[i] = none

    def cell(k, carry):
        settle(jnp.maximum(k - 1, 0))
        rows = pack(
            plan, offsets, k,
            lambda s, n: (table[s] + shifts[plan[k, SHIFT_AT + n]], derived[s]),
            deads, (near, more),
        )

        def setup(g):
            at = pl.multiple_of(jnp.minimum(g, CAP // GROUP - 1) * GROUP, GROUP)
            columns = (X, Y, Z, VX, VY, VZ, SECOND, THIRD, SMALL, SOUND)
            return tuple(targets[f, k, pl.ds(at, GROUP), :] for f in columns) + tuple(
                own[f, k, pl.ds(at, GROUP), :] for f in range(2)
            )

        def run(size):
            def group(g, carry):
                (x, y, z, vx, vy, vz, second, third, small, sound, press, thin), parts = carry
                for i, found in enumerate(finish(k, g - 1, parts)):
                    total[i] += found
                following = setup(g + 1)
                ax = ay = az = jnp.zeros((GROUP, CAP), F32)
                for n in range(size):
                    dx, dy, dz = x - near[n, 0:1], y - near[n, 1:2], z - near[n, 2:3]
                    square = jnp.maximum(dx * dx + dy * dy + dz * dz, TINY)
                    over = lax.rsqrt(square)
                    radius = square * over
                    half = radius * third
                    outer = second - half
                    inner = jnp.maximum(outer - half, 0.0)
                    outer = jnp.maximum(outer, 0.0)
                    slope = outer * outer - inner * inner
                    half = radius * more[n, 1:2]
                    outer = more[n, 0:1] - half
                    inner = jnp.maximum(outer - half, 0.0)
                    outer = jnp.maximum(outer, 0.0)
                    slope += outer * outer - inner * inner
                    approach = (
                        (vx - near[n, 5:6]) * dx
                        + (vy - near[n, 6:7]) * dy
                        + (vz - near[n, 7:8]) * dz
                    )
                    mean = small + more[n, 2:3]
                    mu = mean * jnp.minimum(approach, 0.0) * (1.0 / (square + mean * mean))
                    viscous = mu * (mu - (sound + more[n, 5:6])) * (1.0 / (thin + more[n, 6:7]))
                    weight = more[n, 3:4] * (press + more[n, 4:5] + viscous) * (slope * over)
                    ax += weight * dx
                    ay += weight * dy
                    az += weight * dz
                return following, (ax, ay, az)

            _, parts = lax.fori_loop(
                0, plan[k, GROUP_AT], group, (setup(0), (none, none, none))
            )
            for i in range(3):
                left[i] = parts[i]

        by_size(rows, run)
        return carry

    lax.fori_loop(0, C_DEV, cell, 0)
    settle(C_DEV - 1)


def shards(
    regions, planes,
    position, velocity, smoothing, particle_mass, energy, density_old, cell_count, active,
    time_bin, pair_source, pair_shift, export,
):
    size = C_DEV + 2 * planes * PLANE + 2
    vmem = pl.BlockSpec(memory_space=pltpu.VMEM)
    smem = pl.BlockSpec(memory_space=pltpu.SMEM)
    hbm = pl.BlockSpec(memory_space=pltpu.HBM)
    dma = pltpu.SemaphoreType.DMA

    def shape(*dims, dtype=F32):
        return jax.ShapeDtypeStruct(dims, dtype)

    def ints(*dims):
        return pltpu.VMEM(dims, jnp.int32)

    def floats(*dims):
        return pltpu.VMEM(dims, F32)

    limit = 32 << 20
    table, sounds, targets, rank, plan, exports, density_old = pl.pallas_call(
        functools.partial(static_kernel, regions, planes),
        out_shape=[
            shape(size, 8, CAP), shape(size, 1, CAP), shape(TARGET, C_DEV, CAP, CAP),
            shape(C_DEV, CAP),
            shape(C_DEV, CAP, dtype=jnp.int32),
            shape(planes, 2, planes * PLANE, dtype=jnp.int32), shape(C_DEV, CAP),
        ],
        in_specs=[hbm] * 11,
        out_specs=[vmem] * 7,
        scratch_shapes=[
            floats(C_DEV, CAP), floats(3, C_DEV, CAP), floats(3, C_DEV, CAP), floats(C_DEV, CAP),
            floats(C_DEV, CAP), ints(C_DEV, CAP), pltpu.SMEM((C_DEV,), jnp.int32),
            ints(C_DEV, NB), ints(C_DEV, NB),
            floats(C_DEV, 8, CAP), pltpu.SMEM((planes, 2, planes * PLANE), jnp.int32),
            floats(PLANE, 2 * planes, 8, CAP),
            *[floats(C_DEV, 8, CAP) for _ in range(planes - 1)],
            floats(planes, C_DEV, 1, CAP), floats(PLANE, 2 * planes, 1, CAP),
            dma((11,)), dma((8,)), dma((2,)), dma((planes - 1,)), dma((planes - 1,)), dma((2,)),
            dma, dma((4,)), pltpu.SMEM((1, 2, planes * PLANE), jnp.int32), dma,
        ],
        compiler_params=pltpu.CompilerParams(
            collective_id=0, has_side_effects=True, vmem_limit_bytes=limit
        ),
    )(
        *(
            pltpu.with_memory_space_constraint(x, pltpu.HBM)
            for x in (
                position, velocity, smoothing, particle_mass, energy, active, cell_count, export.T,
                pair_source, pair_shift, density_old,
            )
        )
    )
    density, own = pl.pallas_call(
        density_kernel,
        out_shape=[shape(C_DEV, CAP), shape(2, C_DEV, CAP, CAP)],
        in_specs=[smem] + [vmem] * 4,
        out_specs=[vmem] * 2,
        scratch_shapes=[
            floats(NB, 8, CAP), floats(NB, 8, CAP), floats(GROUP, CAP), floats(2, GROUP, CAP),
        ],
        compiler_params=pltpu.CompilerParams(vmem_limit_bytes=limit),
    )(plan, table, targets, rank, density_old)
    derived, offsets = pl.pallas_call(
        functools.partial(moving_kernel, regions, planes),
        out_shape=[shape(size, 8, CAP), shape(C_DEV, CAP, dtype=jnp.int32)],
        in_specs=[smem] + [vmem] * 4,
        out_specs=[vmem] * 2,
        scratch_shapes=[
            floats(size, 1, CAP), floats(C_DEV, 1, CAP),
            floats(planes * PLANE - 1, 2, 1, CAP), dma((4,)), dma((2,)),
        ],
        compiler_params=pltpu.CompilerParams(
            collective_id=1, has_side_effects=True, vmem_limit_bytes=limit
        ),
    )(exports, density, table, sounds, plan)
    acceleration, kicked, density = pl.pallas_call(
        force_kernel,
        out_shape=[shape(3, C_DEV, CAP), shape(3, C_DEV, CAP), shape(C_DEV, CAP)],
        in_specs=[smem] * 2 + [vmem] * 8,
        out_specs=[vmem] * 3,
        scratch_shapes=[
            floats(NB, 8, CAP), floats(ROWS, 8, CAP), floats(ROWS, 8, CAP),
            floats(3, GROUP, CAP), floats(3, GROUP, CAP),
        ],
        compiler_params=pltpu.CompilerParams(vmem_limit_bytes=limit),
    )(plan, offsets, table, derived, targets, own, rank, velocity, time_bin, density)
    return density, acceleration, kicked


def solution(mesh):
    both = ("region", "cell")
    flat, wide_rows = P(both, None), P(None, both, None)
    return jax.shard_map(
        functools.partial(shards, mesh.shape["region"], mesh.shape["cell"] // PLANE),
        mesh=mesh,
        in_specs=(
            wide_rows, wide_rows, flat, flat, flat, flat, P(both), flat, flat, flat, flat, flat,
        ),
        out_specs=(flat, wide_rows, wide_rows),
        check_vma=False,
    )
```
